128 devices in a mesh: clip: 4 (over y_hi, core), tm: 32 (over x, z, y_lo).
Axes of the slice: x: 4, y: 4 (y_hi: 2, y_lo: 2; y = y_hi * 2 + y_lo), z: 4, core: 2. Of those that a mesh axis runs over, the one named last changes fastest.
Arguments:
- half_one: bfloat16 [4, 32, 14, 14, 768], P('clip', 'tm'), may hold values from -6 to 6
- half_two: bfloat16 [4, 32, 14, 14, 768], P('clip', 'tm'), may hold values from -6 to 6
- grad_one: bfloat16 [4, 32, 14, 14, 768], P('clip', 'tm'), may hold values from -6 to 6
- grad_two: bfloat16 [4, 32, 14, 14, 768], P('clip', 'tm'), may hold values from -12 to 12
- norm_gain: float32 [2, 768], replicated, may hold values from 0.1 to 1.9
- attn_weight: bfloat16 [4, 768, 768], replicated, may hold values from -0.21875 to 0.21875
- mlp_weight: bfloat16 [2, 3072, 768], replicated, may hold values from -0.15625 to 0.15625
- pool_kernel: float32 [3, 4, 4, 1536], replicated, may hold values from -0.875 to 0.875
Outputs:
- input_one: bfloat16 [4, 32, 14, 14, 768], P('clip', 'tm')
- input_two: bfloat16 [4, 32, 14, 14, 768], P('clip', 'tm')
- input_grad_one: bfloat16 [4, 32, 14, 14, 768], P('clip', 'tm')
- input_grad_two: bfloat16 [4, 32, 14, 14, 768], P('clip', 'tm')
- attn_grad: float32 [4, 768, 768], P(None, None, ('clip', 'tm'))
- mlp_grad: float32 [2, 3072, 768], P(None, None, ('clip', 'tm'))
- kernel_grad: float32 [3, 4, 4, 1536], P(None, None, None, ('clip', 'tm'))
- gain_grad: float32 [2, 768], P(None, ('clip', 'tm'))
The draws below stay inside these ranges and needn't reach their ends.
All inputs are finite; a program needn't handle non-finite values.
Results may differ from the reference program's by a relative error of at most 0.025.
Values may be sent and summed in bfloat16 or wider, within the bound.
A program may use at most 192 MiB of HBM per device.

```python
from functools import partial
import jax
import jax.numpy as jnp
from jax import lax

D = 768
FF = 3072
HEAD_DIM = 64
GRID = 14
FRAMES = 32
CLIPS = 4


def strengthened(values, stream_key, source, target, parts, factor):
    owner, partner = [(jnp.arange(values.shape[dim]) // (values.shape[dim] // parts)).reshape([-1 if axis == dim else 1 for axis in range(values.ndim)]) for dim in (source, target)]
    chosen = jax.random.permutation(stream_key, parts)[partner]
    strong = (owner == chosen) | (owner == (partner + parts // 2) % parts)
    return jnp.where(strong, factor * values, values)


def block_scale(own_key, extent, shards, low, high):
    loudness = 1.0
    for dim, blocks in shards:
        steps = jax.random.uniform(jax.random.fold_in(jax.random.fold_in(own_key, 6), dim), (blocks,), jnp.float32, low / len(shards), high / len(shards))
        loudness = loudness * jnp.repeat(jnp.exp(steps), extent[dim] // blocks).reshape((-1,) + (1,) * (len(extent) - 1 - dim))
    return loudness


def bell_draw(own_key, shape, scale, bound, cuts=(), held_as=jnp.bfloat16):
    entries = scale * jax.random.normal(own_key, shape, jnp.float32)
    if cuts:
        entries = entries * block_scale(own_key, shape, cuts, -0.22, 0.18)
    return jnp.clip(entries, -bound, bound).astype(held_as)


def gaussian_with(own_key, dims, scale, limit, cuts, heavy, held_as=jnp.bfloat16):
    values = scale * jax.random.normal(own_key, dims, jnp.float32)
    if cuts:
        values = values * block_scale(own_key, dims, cuts, -0.22, 0.18)
    return jnp.clip(strengthened(values, jax.random.fold_in(own_key, 3), *heavy), -limit, limit).astype(held_as)


def setup_inputs(seed: int = 0) -> dict:
    splits = jax.random.split(jax.random.key(seed), 9)
    return {
        "half_one": bell_draw(splits[0], (CLIPS, FRAMES, GRID, GRID, D), 1.0, 6.0, ((0, 4), (1, 32))),
        "half_two": bell_draw(splits[1], (CLIPS, FRAMES, GRID, GRID, D), 1.0, 6.0, ((0, 4), (1, 32))),
        "grad_one": bell_draw(splits[2], (CLIPS, FRAMES, GRID, GRID, D), 1.0, 6.0, ((0, 4), (1, 32))),
        "grad_two": gaussian_with(splits[3], (CLIPS, FRAMES, GRID, GRID, D), 1.0, 12.0, ((0, 4), (1, 32)), (1, 4, 32, 2.75)),
        "norm_gain": jnp.clip(1.0 + 0.18 * jax.random.normal(splits[4], (2, D), jnp.float32), 0.1, 1.9),
        "attn_weight": bell_draw(splits[5], (4, D, D), D ** -0.5, 0.21875),
        "mlp_weight": bell_draw(splits[6], (2, FF, D), (2 * D) ** -0.5, 0.15625),
        "pool_kernel": bell_draw(splits[7], (3, 4, 4, 2 * D), 48 ** -0.5, 0.875, (), jnp.float32),
    }


def normalize(values, gain):
    centre = lax.optimization_barrier(jnp.mean(values, axis=-1, keepdims=True))
    centred = values - centre
    spread = lax.optimization_barrier(jnp.mean(centred * centred, axis=-1, keepdims=True))
    return centred * lax.rsqrt(spread + 1e-05) * gain

def pool_frames(frames_in, kernel):
    length = frames_in.shape[1] - 2
    padded = jnp.pad(frames_in, ((0, 0), (0, 0), (1, 1), (1, 1), (0, 0)))
    blocks = padded.reshape(frames_in.shape[0], length + 2, 4, 4, 4, 4, frames_in.shape[-1])
    result = jnp.zeros((frames_in.shape[0], length, 4, 4, frames_in.shape[-1]), jnp.float32)
    for offset in range(3):
        result = result + jnp.einsum('ctaibje,ije->ctabe', blocks[:, offset:offset + length], kernel[offset])
    return result.reshape(frames_in.shape[0], length * 16, frames_in.shape[-1])

def pool_padded(frames_in, kernel):
    widened = jnp.pad(frames_in, ((0, 0), (1, 1), (0, 0), (0, 0), (0, 0)))
    return pool_frames(widened, kernel)

def soft_probs(query_h, key_h):
    score_scale = HEAD_DIM ** (-0.5)
    scores = jnp.dot(query_h, key_h.T, preferred_element_type=jnp.float32) * score_scale
    weights = jnp.exp(scores)
    return weights / lax.optimization_barrier(jnp.sum(weights, axis=-1, keepdims=True))

def head_forward(pieces):
    query_h, key_h, value_h = pieces
    probs = soft_probs(query_h, key_h)
    return jnp.dot(probs.astype(jnp.bfloat16), value_h, preferred_element_type=jnp.float32).astype(jnp.bfloat16)

def head_backward(pieces):
    query_h, key_h, value_h, grad_h = pieces
    score_scale = HEAD_DIM ** (-0.5)
    probs = soft_probs(query_h, key_h)
    probs_b = probs.astype(jnp.bfloat16)
    d_value = jnp.dot(probs_b.T, grad_h, preferred_element_type=jnp.float32)
    d_probs = jnp.dot(grad_h, value_h.T, preferred_element_type=jnp.float32)
    d_scores = (probs * (d_probs - lax.optimization_barrier(jnp.sum(probs * d_probs, axis=-1, keepdims=True)))).astype(jnp.bfloat16)
    d_query = (jnp.dot(d_scores, key_h, preferred_element_type=jnp.float32) * score_scale).astype(jnp.bfloat16)
    d_key = jnp.dot(d_scores.T, query_h, preferred_element_type=jnp.float32) * score_scale
    return (d_query, d_key, d_value)

def clip_pass(one, two, cot_one, cot_two, norm_gain, attn_weight, mlp_weight, pool_kernel):
    frame_count = one.shape[0]
    width = one.shape[-1]
    heads = width // HEAD_DIM
    rows = frame_count * 196
    one_flat = one.reshape(rows, width)
    two_flat = two.reshape(rows, width)
    cot_one_flat = cot_one.reshape(rows, width)
    cot_two_flat = cot_two.reshape(rows, width)
    normed_one = normalize(one_flat.astype(jnp.float32), norm_gain[0]).astype(jnp.bfloat16)
    hidden = jnp.dot(normed_one, mlp_weight[0].T, preferred_element_type=jnp.float32)
    active, gelu_back = jax.vjp(jax.nn.gelu, hidden)
    active_b = active.astype(jnp.bfloat16)
    branch_g = jnp.dot(active_b, mlp_weight[1], preferred_element_type=jnp.float32)
    input_two = (two_flat.astype(jnp.float32) - branch_g).astype(jnp.bfloat16)
    d_active = jnp.dot(cot_two_flat, mlp_weight[1].T, preferred_element_type=jnp.float32)
    d_down = jnp.dot(active_b.T, cot_two_flat, preferred_element_type=jnp.float32)
    d_hidden = gelu_back(d_active)[0].astype(jnp.bfloat16)
    d_up = jnp.dot(d_hidden.T, normed_one, preferred_element_type=jnp.float32)
    d_normed = jnp.dot(d_hidden, mlp_weight[0], preferred_element_type=jnp.float32)
    _, norm_back = jax.vjp(normalize, one_flat.astype(jnp.float32), norm_gain[0])
    d_first, d_gain_one = norm_back(d_normed)
    total_one = cot_one_flat.astype(jnp.float32) + d_first
    total_b = total_one.astype(jnp.bfloat16)
    normed_two = normalize(input_two.astype(jnp.float32), norm_gain[1]).astype(jnp.bfloat16)
    qkv_weight = jnp.concatenate([attn_weight[0], attn_weight[1], attn_weight[2]], axis=1)
    query = jnp.dot(normed_two, attn_weight[0], preferred_element_type=jnp.float32).astype(jnp.bfloat16)
    keyval = jnp.dot(normed_two, qkv_weight[:, width:], preferred_element_type=jnp.float32).astype(jnp.bfloat16)
    kv_frames = keyval.reshape(1, frame_count, 14, 14, 2 * width).astype(jnp.float32)
    pooled, pool_back = jax.vjp(partial(pool_padded, kv_frames), pool_kernel)
    pooled_b = pooled.astype(jnp.bfloat16)[0]
    key_count = pooled_b.shape[0]
    key_heads = pooled_b[:, :width].reshape(key_count, heads, HEAD_DIM).transpose(1, 0, 2)
    value_heads = pooled_b[:, width:].reshape(key_count, heads, HEAD_DIM).transpose(1, 0, 2)
    query_heads = query.reshape(rows, heads, HEAD_DIM).transpose(1, 0, 2)
    attended = lax.map(head_forward, (query_heads, key_heads, value_heads))
    attended = attended.transpose(1, 0, 2).reshape(rows, width)
    branch_f = jnp.dot(attended, attn_weight[3], preferred_element_type=jnp.float32)
    input_one = (one_flat.astype(jnp.float32) - branch_f).astype(jnp.bfloat16)
    d_out = jnp.dot(attended.T, total_b, preferred_element_type=jnp.float32)
    d_attended = jnp.dot(total_b, attn_weight[3].T, preferred_element_type=jnp.float32).astype(jnp.bfloat16)
    grad_heads = d_attended.reshape(rows, heads, HEAD_DIM).transpose(1, 0, 2)
    d_query, d_key, d_value = lax.map(head_backward, (query_heads, key_heads, value_heads, grad_heads))
    d_query = d_query.transpose(1, 0, 2).reshape(rows, width)
    d_key = d_key.transpose(1, 0, 2).reshape(key_count, width)
    d_value = d_value.transpose(1, 0, 2).reshape(key_count, width)
    d_pooled = jnp.concatenate([d_key, d_value], axis=-1)[None]
    d_kernel = pool_back(d_pooled)[0]
    _, frame_back = jax.vjp(partial(pool_padded, kernel=pool_kernel), kv_frames)
    d_keyval = frame_back(d_pooled)[0].reshape(rows, 2 * width).astype(jnp.bfloat16)
    d_proj = jnp.concatenate([d_query, d_keyval], axis=1)
    d_normed_two = jnp.dot(d_proj, qkv_weight.T, preferred_element_type=jnp.float32)
    d_qkv = jnp.dot(normed_two.T, d_proj, preferred_element_type=jnp.float32)
    _, norm_back_two = jax.vjp(normalize, input_two.astype(jnp.float32), norm_gain[1])
    d_second, d_gain_two = norm_back_two(d_normed_two)
    input_grad_two = (cot_two_flat.astype(jnp.float32) + d_second).astype(jnp.bfloat16)
    shape_out = one.shape
    attn_part = jnp.stack([d_qkv[:, :width], d_qkv[:, width:2 * width], d_qkv[:, 2 * width:], d_out])
    mlp_part = jnp.stack([d_up, d_down])
    gain_part = jnp.stack([d_gain_one, d_gain_two])
    return (input_one.reshape(shape_out), input_two.reshape(shape_out), total_b.reshape(shape_out), input_grad_two.reshape(shape_out), attn_part, mlp_part, d_kernel, gain_part)

def reference(half_one, half_two, grad_one, grad_two, norm_gain, attn_weight, mlp_weight, pool_kernel):
    firsts, seconds, grad_firsts, grad_seconds = ([], [], [], [])
    attn_sum = jnp.zeros(attn_weight.shape, jnp.float32)
    mlp_sum = jnp.zeros(mlp_weight.shape, jnp.float32)
    kernel_sum = jnp.zeros(pool_kernel.shape, jnp.float32)
    gain_sum = jnp.zeros(norm_gain.shape, jnp.float32)
    for index in range(CLIPS):
        result = clip_pass(half_one[index], half_two[index], grad_one[index], grad_two[index], norm_gain, attn_weight, mlp_weight, pool_kernel)
        firsts.append(result[0])
        seconds.append(result[1])
        grad_firsts.append(result[2])
        grad_seconds.append(result[3])
        attn_sum = attn_sum + result[4]
        mlp_sum = mlp_sum + result[5]
        kernel_sum = kernel_sum + result[6]
        gain_sum = gain_sum + result[7]
    return (jnp.stack(firsts), jnp.stack(seconds), jnp.stack(grad_firsts), jnp.stack(grad_seconds), attn_sum, mlp_sum, kernel_sum, gain_sum)
```

```python
from functools import partial

import jax
import jax.numpy as jnp
from jax import lax
from jax.experimental import pallas as pl
from jax.experimental.pallas import tpu as pltpu
from jax.sharding import PartitionSpec as P

D = 768
FF = 3072
KV = 2 * D
ROWS = 224
CHUNK = 512
STEPS = FF // CHUNK
HALF = 384
MIB = 1024 * 1024
F32 = jnp.float32
BF16 = jnp.bfloat16
MESH = pl.DeviceIdType.MESH


def dot(a, b):
    return lax.dot_general(a, b, (((1,), (0,)), ((), ())), preferred_element_type=F32)


def dot_nt(a, b):
    return lax.dot_general(a, b, (((1,), (1,)), ((), ())), preferred_element_type=F32)


def dot_tn(a, b):
    return lax.dot_general(a, b, (((0,), (0,)), ((), ())), preferred_element_type=F32)


def iota(shape, dim):
    return lax.broadcasted_iota(jnp.int32, shape, dim)


def source_column(rows, part):
    owner_at = (rows * 43691) >> 18
    inner = rows - owner_at * 6
    core = owner_at >> 6
    digits = ((owner_at >> 4) & 3, (owner_at >> 2) & 3, owner_at & 3)
    x, y, z = (digits[(axis - part) % 3] for axis in range(3))
    owner = (y >> 1) * 64 + core * 32 + x * 8 + z * 2 + (y & 1)
    return owner * 6 + inner


def permutation(part):
    source = source_column(iota((D, 128), 0), part)
    lanes = iota((D, 128), 1)
    pieces = [
        jnp.where(source == lanes + 128 * k, 1.0, 0.0).astype(BF16) for k in range(D // 128)
    ]
    return jnp.concatenate(pieces, axis=1)


def norm_stats(values):
    centre = jnp.mean(values, axis=-1, keepdims=True)
    centred = values - centre
    spread = jnp.mean(centred * centred, axis=-1, keepdims=True)
    scale = lax.rsqrt(spread + 1e-05)
    return centred * scale, scale


def norm_back(unit, scale, gain, cotangent):
    d_unit = cotangent * gain
    first = jnp.mean(d_unit, axis=-1, keepdims=True)
    second = jnp.mean(d_unit * unit, axis=-1, keepdims=True)
    return scale * (d_unit - first - unit * second)


def load_padded(ref, pad):
    pad[...] = jnp.zeros(pad.shape, pad.dtype)
    pad[:, 0:14, :] = ref[0, 0]
    return pad[...].reshape(ROWS, D)


def store_grid(ref, values):
    ref[0, 0] = values.reshape(14, 16, D)[:, 0:14, :]


def cell_maps():
    row = iota((ROWS, 48), 0)
    across, down = (row & 15) + 1, (row >> 4) + 1
    valid = across < 15
    cell = (down & 3) * 4 + (across & 3)
    lane = iota((ROWS, 48), 1)
    cells = jnp.where(valid & ((lane & 15) == cell), 1.0, 0.0).astype(BF16)
    row = iota((ROWS, 16), 0)
    across, down = (row & 15) + 1, (row >> 4) + 1
    block = (down >> 2) * 4 + (across >> 2)
    blocks = jnp.where((across < 15) & (iota((ROWS, 16), 1) == block), 1.0, 0.0).astype(BF16)
    return cells, blocks


def spread_kernel(cells, flat):
    high = flat.astype(BF16)
    rest = flat - high.astype(F32)
    middle = rest.astype(BF16)
    low = (rest - middle.astype(F32)).astype(BF16)
    return dot(cells, jnp.concatenate([high, middle, low], axis=0))


def gather_rows(one_hot, values):
    high = values.astype(BF16)
    low = (values - high.astype(F32)).astype(BF16)
    return dot_tn(one_hot, high) + dot_tn(one_hot, low)


def mlp_kernel(
    one_ref, two_ref, cot_one_ref, cot_two_ref, gain_ref, up_ref, down_ref, attn_hbm, pool_ref,
    two_out, total_out, grad_out, normed_out, query_out, keyval_out, datt_out, total_pad_out,
    part_out, gain_out,
    pad, normed, cot, left, branch, d_normed, attn, pool, sem,
):
    step = pl.program_id(0)
    attn_copy = pltpu.make_async_copy(attn_hbm, attn, sem)

    @pl.when(step == 0)
    def _():
        attn_copy.start()
        unit, _ = norm_stats(load_padded(one_ref, pad).astype(F32))
        normed[...] = (unit * gain_ref[0:1, :]).astype(BF16)
        cot[...] = load_padded(cot_two_ref, pad)
        branch[...] = jnp.zeros(branch.shape, F32)
        d_normed[...] = jnp.zeros(d_normed.shape, F32)

    @pl.when(step % 2 == 0)
    def _():
        for part in range(3):

            @pl.when(step == 2 * part)
            def _():
                order = permutation(part)
                left[0] = dot_nt(order, normed[...]).astype(BF16)
                left[1] = dot_nt(order, cot[...]).astype(BF16)

    hidden = dot_nt(normed[...], up_ref[0])
    inner = 0.7978845608028654 * (hidden + 0.044715 * hidden * hidden * hidden)
    tanh = jnp.tanh(inner)
    half_sum = 0.5 * (1.0 + tanh)
    active = (hidden * half_sum).astype(BF16)
    slope = half_sum + 0.5 * hidden * (1.0 - tanh * tanh) * (
        0.7978845608028654 * (1.0 + 3.0 * 0.044715 * hidden * hidden)
    )
    d_hidden = (slope * dot_nt(cot[...], down_ref[0])).astype(BF16)
    branch[...] += dot(active, down_ref[0])
    d_normed[...] += dot(d_hidden, up_ref[0])
    grad_out[:, 0:CHUNK] = dot(left[0], d_hidden).astype(BF16)
    grad_out[:, CHUNK:] = dot(left[1], active).astype(BF16)

    @pl.when(step == STEPS - 1)
    def _():
        attn_copy.wait()
        unit, scale = norm_stats(load_padded(one_ref, pad).astype(F32))
        back = d_normed[...]
        gain_out[...] = jnp.sum(back * unit, axis=0, keepdims=True)
        d_first = norm_back(unit, scale, gain_ref[0:1, :], back)
        total = (load_padded(cot_one_ref, pad).astype(F32) + d_first).astype(BF16)
        store_grid(total_out, total)
        total_pad_out[...] = total
        datt_out[...] = dot_nt(total, attn[3]).astype(BF16)
        restored = (load_padded(two_ref, pad).astype(F32) - branch[...]).astype(BF16)
        store_grid(two_out, restored)
        unit_two, _ = norm_stats(restored.astype(F32))
        normed_two = (unit_two * gain_ref[1:2, :]).astype(BF16)
        normed_out[...] = normed_two
        query_out[...] = dot(normed_two, attn[0]).astype(BF16)
        keyval_out[:, 0:D] = dot(normed_two, attn[1]).astype(BF16)
        keyval_out[:, D:] = dot(normed_two, attn[2]).astype(BF16)
        cells, blocks = cell_maps()
        for offset in range(3):
            for i in range(4):
                pool[4 * i : 4 * i + 4, :] = pool_ref[offset, i]
            weighted = spread_kernel(cells, pool[...]) * keyval_out[...].astype(F32)
            part_out[offset] = gather_rows(blocks, weighted)


def run_mlp(half_one, half_two, grad_one, grad_two, norm_gain, attn_weight, mlp_weight, pool_kernel):
    grid_block = pl.BlockSpec((1, 1, 14, 14, D), lambda f: (0, 0, 0, 0, 0))

    def whole(*shape):
        return pl.BlockSpec(shape, lambda f: (0,) * len(shape))

    shape = jax.ShapeDtypeStruct
    return pl.pallas_call(
        mlp_kernel,
        grid=(STEPS,),
        in_specs=[
            grid_block, grid_block, grid_block, grid_block,
            whole(2, D),
            pl.BlockSpec((1, CHUNK, D), lambda f: (0, f, 0)),
            pl.BlockSpec((1, CHUNK, D), lambda f: (1, f, 0)),
            pl.BlockSpec(memory_space=pl.ANY),
            whole(3, 4, 4, KV),
        ],
        out_specs=[
            grid_block, grid_block,
            pl.BlockSpec((D, 2 * CHUNK), lambda f: (0, f)),
            whole(ROWS, D), whole(ROWS, D), whole(ROWS, KV), whole(ROWS, D), whole(ROWS, D),
            whole(3, 16, KV), whole(1, D),
        ],
        out_shape=[
            shape(half_one.shape, BF16), shape(half_one.shape, BF16),
            shape((D, 2 * FF), BF16),
            shape((ROWS, D), BF16), shape((ROWS, D), BF16), shape((ROWS, KV), BF16),
            shape((ROWS, D), BF16), shape((ROWS, D), BF16),
            shape((3, 16, KV), F32), shape((1, D), F32),
        ],
        scratch_shapes=[
            pltpu.VMEM((14, 16, D), BF16),
            pltpu.VMEM((ROWS, D), BF16),
            pltpu.VMEM((ROWS, D), BF16),
            pltpu.VMEM((2, D, ROWS), BF16),
            pltpu.VMEM((ROWS, D), F32),
            pltpu.VMEM((ROWS, D), F32),
            pltpu.VMEM((4, D, D), BF16),
            pltpu.VMEM((16, KV), F32),
            pltpu.SemaphoreType.DMA,
        ],
        compiler_params=pltpu.CompilerParams(
            dimension_semantics=("arbitrary",), vmem_limit_bytes=48 * MIB
        ),
        name="mlp_branch",
    )(half_one, half_two, grad_one, grad_two, norm_gain, mlp_weight, mlp_weight, attn_weight, pool_kernel)


class Links:
    def __init__(self, send, recv):
        self.send, self.recv, self.used, self.started = send, recv, 0, []

    def start(self, source, target, device):
        copy = pltpu.make_async_remote_copy(
            src_ref=source, dst_ref=target,
            send_sem=self.send.at[self.used], recv_sem=self.recv.at[self.used],
            device_id=device, device_id_type=MESH,
        )
        self.used += 1
        copy.start()
        self.started.append(copy)
        return copy


class Place:
    def __init__(self):
        clip, tm = lax.axis_index("clip"), lax.axis_index("tm")
        self.tm, self.clip = tm, clip
        self.core, high = clip % 2, clip // 2
        self.low = tm % 2
        self.at = (tm // 8, high * 2 + self.low, (tm // 2) % 4)

    def device(self, core, at):
        x, y, z = at
        return ((y // 2) * 2 + core, x * 8 + z * 2 + y % 2)

    def other_core(self):
        return self.device(1 - self.core, self.at)

    def along(self, axis, hop):
        at = list(self.at)
        at[axis] = (at[axis] + hop) % 4
        return self.device(self.core, at), at[axis]

    def pair(self):
        return (self.clip, self.tm - self.low + (1 - self.low))

    def frame(self, hop):
        return (self.clip, (self.tm + hop + 32) % 32)


class Reduction:
    def __init__(self, links, place, parts, full, held, base, landed, out, out_base):
        self.links, self.place, self.parts = links, place, parts
        self.full, self.held, self.base = full, held, base
        self.in0, self.in1, self.sum1, self.in2, self.sum2, self.in3 = landed
        self.out, self.out_base = out, out_base
        self.copies = {}

    def columns(self, part):
        return pl.ds(self.parts[part][0], self.parts[part][1])

    def blocks(self, part, width=512):
        first, count = self.parts[part]
        if count % width:
            width = count
        return [(first + k * width, width) for k in range(count // width)]

    def send0(self, part):
        cols = self.columns(part)
        rows = pl.ds(pl.multiple_of((1 - self.place.core) * HALF, HALF), HALF)
        self.copies[0, part] = [
            self.links.start(
                self.full.at[rows, cols], self.in0.at[:, cols], self.place.other_core()
            )
        ]

    def arrive(self, stage, part):
        for copy in self.copies[stage, part]:
            copy.wait_recv()

    def spread(self, stage, part, source, base, rows, target):
        axis = (part + stage - 1) % 3
        cols = self.columns(part)
        self.copies[stage, part] = []
        for hop in (2, 1, 3):
            device, at = self.place.along(axis, hop)
            window = pl.ds(pl.multiple_of(base + at * rows, rows), rows)
            self.copies[stage, part].append(
                self.links.start(source.at[window, cols], target.at[hop - 1, :, cols], device)
            )

    def send1(self, part):
        self.arrive(0, part)
        first, count = self.parts[part]

        def body(k, carry):
            rows = pl.ds(pl.multiple_of(k * 16, 16), 16)
            mine = pl.ds(pl.multiple_of(self.base + k * 16, 16), 16)
            cols = pl.ds(first, count)
            total = self.held[mine, cols].astype(F32) + self.in0[rows, cols].astype(F32)
            self.held[mine, cols] = total.astype(BF16)
            return carry

        lax.fori_loop(0, HALF // 16, body, 0)
        self.spread(1, part, self.held, self.base, 96, self.in1)

    def send2(self, part):
        self.arrive(1, part)
        mine = self.place.at[part % 3]
        rows = pl.ds(pl.multiple_of(self.base + mine * 96, 96), 96)
        place_row, place_col = iota((128, 96), 0), iota((128, 96), 1)
        owner = place_row >> 3
        inner = place_row & 7
        widen = jnp.where((inner < 6) & (place_col == owner * 6 + inner), 1.0, 0.0).astype(BF16)
        for first, count in self.blocks(part):
            cols = pl.ds(first, count)
            total = self.held[rows, cols].astype(F32)
            for slot in range(3):
                total = total + self.in1[slot, :, cols].astype(F32)
            self.sum1[:, cols] = dot(widen, total.astype(BF16)).astype(BF16)
        self.spread(2, part, self.sum1, 0, 32, self.in2)

    def send3(self, part):
        self.arrive(2, part)
        mine = self.place.at[(part + 1) % 3]
        rows = pl.ds(pl.multiple_of(mine * 32, 32), 32)
        for first, count in self.blocks(part):
            cols = pl.ds(first, count)
            total = self.sum1[rows, cols].astype(F32)
            for slot in range(3):
                total = total + self.in2[slot, :, cols].astype(F32)
            self.sum2[:, cols] = total
        self.spread(3, part, self.sum2, 0, 8, self.in3)

    def finish(self, part):
        self.arrive(3, part)
        mine = self.place.at[(part + 2) % 3]
        rows = pl.ds(pl.multiple_of(mine * 8, 8), 8)
        for first, count in self.blocks(part):
            cols = pl.ds(first, count)
            total = self.sum2[rows, cols]
            for slot in range(3):
                total = total + self.in3[slot, :, cols]
            self.out[:, pl.ds(self.out_base + first, count)] = total


MLP_PARTS = tuple((p * 2048, 2048) for p in range(3))
FIRST_PARTS = tuple((p * 512, 512) for p in range(3))
LAST_PARTS = ((0, 512), (512, 512), (1024, 640))
MLP_COLS, FIRST_COLS, LAST_COLS = 6144, 1536, 1664
N_COPIES = 3 * 30 + 2 * 14 + 4


def landing(cols):
    return [
        pltpu.VMEM((HALF, cols), BF16),
        pltpu.VMEM((3, 96, cols), BF16),
        pltpu.VMEM((128, cols), BF16),
        pltpu.VMEM((3, 32, cols), BF16),
        pltpu.VMEM((32, cols), F32),
        pltpu.VMEM((3, 8, cols), F32),
    ]


def attention_kernel(
    query_ref, keyval_ref, datt_ref, total_ref, normed_ref, parts_ref, gain_one_ref,
    one_ref, two_ref, cot_two_ref, gain_ref, pool_ref, attn_hbm, mlp_hbm,
    one_out, grad_two_out, sums_out,
    *scratch,
):
    scratch = list(scratch)

    def take(count):
        taken = scratch[:count]
        del scratch[:count]
        return taken

    send_sem, recv_sem, local_sem = take(3)
    mlp_own, mlp_land = take(1)[0], take(6)
    first_full, first_land = take(1)[0], take(6)
    last_full, last_land = take(1)[0], take(6)
    attn, spread, orders, pool, halo, pooled, pad = take(7)
    keys, values, d_keys, d_values = take(4)
    x_keys, z_keys, y_keys, x_values, z_values, y_values = take(6)
    key_sum, value_sum, key_pair, value_pair = take(4)
    d_pooled, d_halo = take(2)
    attended, d_query, extra, extra_gain = take(4)

    place = Place()
    links = Links(send_sem, recv_sem)
    x, y, z = place.at
    low = place.low

    barrier = pltpu.get_barrier_semaphore()
    partners = [place.other_core(), place.frame(1), place.frame(-1)]
    partners += [place.along(axis, hop)[0] for axis in range(3) for hop in (1, 2, 3)]
    for device in partners:
        pl.semaphore_signal(barrier, inc=1, device_id=device, device_id_type=MESH)
    pl.semaphore_wait(barrier, len(partners))

    halo_copies = [
        links.start(parts_ref.at[0], halo.at[0], place.frame(1)),
        links.start(parts_ref.at[2], halo.at[1], place.frame(-1)),
    ]
    mlp = Reduction(links, place, MLP_PARTS, mlp_hbm, mlp_own, 0, mlp_land, sums_out, 0)
    first = Reduction(
        links, place, FIRST_PARTS, first_full, first_full, place.core * HALF, first_land,
        sums_out, MLP_COLS,
    )
    last = Reduction(
        links, place, LAST_PARTS, last_full, last_full, place.core * HALF, last_land,
        sums_out, MLP_COLS + FIRST_COLS,
    )
    own_rows = pl.ds(pl.multiple_of(place.core * HALF, HALF), HALF)
    own_copies = []
    for part in range(3):
        mlp.send0(part)
        cols = mlp.columns(part)
        own_copies.append(
            pltpu.make_async_copy(
                mlp_hbm.at[own_rows, cols], mlp_own.at[:, cols], local_sem.at[part]
            )
        )
        own_copies[-1].start()
    attn_copy = pltpu.make_async_copy(attn_hbm, attn, local_sem.at[3])
    attn_copy.start()

    for copy in halo_copies:
        copy.wait_recv()
    from_left = jnp.where(place.tm > 0, halo[0], 0.0)
    from_right = jnp.where(place.tm < 31, halo[1], 0.0)
    pooled[...] = (parts_ref[1] + from_left + from_right).astype(BF16)
    at_low = pl.ds(pl.multiple_of(low * 16, 16), 16)
    keys[x, z, at_low, :] = pooled[:, 0:D]
    values[x, z, at_low, :] = pooled[:, D:]

    copies = [
        links.start(keys.at[x, z, at_low, :], keys.at[x, z, at_low, :], place.pair()),
        links.start(values.at[x, z, at_low, :], values.at[x, z, at_low, :], place.pair()),
    ]
    cells, blocks = cell_maps()
    for offset in range(3):
        for i in range(4):
            pool[4 * i : 4 * i + 4, :] = pool_ref[offset, i]
        spread[offset] = spread_kernel(cells, pool[...])
    for copy in copies:
        copy.wait_recv()
    copies = []
    for hop in (2, 1, 3):
        copies.append(links.start(keys.at[x, z], keys.at[x, z], place.along(2, hop)[0]))
        copies.append(links.start(values.at[x, z], values.at[x, z], place.along(0, hop)[0]))
    for part in range(3):
        orders[part] = permutation(part)
    for copy in copies:
        copy.wait_recv()
    copies = []
    for hop in (2, 1, 3):
        copies.append(links.start(keys.at[x], keys.at[x], place.along(0, hop)[0]))
        copies.append(links.start(values.at[:, z], values.at[:, z], place.along(2, hop)[0]))
    for copy in own_copies:
        copy.wait()
    for copy in copies:
        copy.wait_recv()
    for part in range(3):
        mlp.send1(part)

    def heads(pair, carry):
        lanes = pl.ds(pl.multiple_of(pair * 128, 128), 128)
        query = query_ref[:, lanes]
        d_att = datt_ref[:, lanes]
        key = keys[:, :, :, lanes].reshape(512, 128)
        value = values[:, :, :, lanes].reshape(512, 128)
        att = d_q = d_k = d_v = None
        for side in range(2):

            def only(array):
                lane = iota(array.shape, 1)
                keep = lane < 64 if side == 0 else lane >= 64
                return jnp.where(keep, array, jnp.zeros_like(array))

            query_h, d_att_h = only(query), only(d_att)
            weights = jnp.exp(dot_nt(query_h, key) * 0.125)
            probs = weights * (1.0 / jnp.sum(weights, axis=-1, keepdims=True))
            probs_b = probs.astype(BF16)
            d_probs = dot_nt(d_att_h, value)
            product = probs * d_probs
            d_scores = (product - probs * jnp.sum(product, axis=-1, keepdims=True)).astype(BF16)
            terms = (
                dot(probs_b, only(value)), dot(d_scores, only(key)),
                dot_tn(d_scores, query_h), dot_tn(probs_b, d_att_h),
            )
            if side == 0:
                att, d_q, d_k, d_v = terms
            else:
                att, d_q, d_k, d_v = (a + b for a, b in zip((att, d_q, d_k, d_v), terms))
        attended[:, lanes] = att.astype(BF16)
        d_query[:, lanes] = (d_q * 0.125).astype(BF16)
        d_keys[:, :, :, lanes] = (d_k * 0.125).astype(BF16).reshape(4, 4, 32, 128)
        d_values[:, :, :, lanes] = d_v.astype(BF16).reshape(4, 4, 32, 128)
        return carry

    lax.fori_loop(0, 6, heads, 0)

    copies = []
    for hop in (2, 1, 3):
        device, at = place.along(0, hop)
        copies.append(links.start(d_keys.at[at], x_keys.at[hop - 1], device))
        device, at = place.along(2, hop)
        copies.append(links.start(d_values.at[:, at], z_values.at[hop - 1], device))

    attn_copy.wait()
    branch = dot(attended[...], attn[3])
    store_grid(one_out, (load_padded(one_ref, pad).astype(F32) - branch).astype(BF16))
    for part in range(3):
        inside = pl.ds(part * 256, 256)
        lhs = dot_nt(orders[part], d_query[...]).astype(BF16)
        first_full[:, pl.ds(part * 512, 256)] = dot(lhs, normed_ref[:, inside]).astype(BF16)
        lhs = dot_nt(orders[part], total_ref[...]).astype(BF16)
        first_full[:, pl.ds(part * 512 + 256, 256)] = dot(lhs, attended[:, inside]).astype(BF16)
        first.send0(part)

    for copy in copies:
        copy.wait_recv()
    total = d_keys[x].astype(F32)
    total_v = d_values[:, z].astype(F32)
    for slot in range(3):
        total = total + x_keys[slot].astype(F32)
        total_v = total_v + z_values[slot].astype(F32)
    key_sum[...] = total.astype(BF16)
    value_sum[...] = total_v.astype(BF16)
    copies = []
    for hop in (2, 1, 3):
        device, at = place.along(2, hop)
        copies.append(links.start(key_sum.at[at], z_keys.at[hop - 1], device))
        device, at = place.along(0, hop)
        copies.append(links.start(value_sum.at[at], x_values.at[hop - 1], device))
    for copy in copies:
        copy.wait_recv()
    total = key_sum[z].astype(F32)
    total_v = value_sum[x].astype(F32)
    for slot in range(3):
        total = total + z_keys[slot].astype(F32)
        total_v = total_v + x_values[slot].astype(F32)
    key_pair[...] = total.astype(BF16)
    value_pair[...] = total_v.astype(BF16)
    at_other = pl.ds(pl.multiple_of((1 - low) * 16, 16), 16)
    copies = [
        links.start(key_pair.at[at_other, :], y_keys, place.pair()),
        links.start(value_pair.at[at_other, :], y_values, place.pair()),
    ]
    for part in range(3):
        mlp.send2(part)
    for copy in copies:
        copy.wait_recv()
    d_pooled[:, 0:D] = (key_pair[at_low, :].astype(F32) + y_keys[...].astype(F32)).astype(BF16)
    d_pooled[:, D:] = (value_pair[at_low, :].astype(F32) + y_values[...].astype(F32)).astype(BF16)
    copies = [
        links.start(d_pooled, d_halo.at[0], place.frame(1)),
        links.start(d_pooled, d_halo.at[1], place.frame(-1)),
    ]
    for part in range(3):
        first.send1(part)
    for copy in copies:
        copy.wait_recv()

    from_left = jnp.where(place.tm > 0, d_halo[0].astype(F32), 0.0).astype(BF16)
    from_right = jnp.where(place.tm < 31, d_halo[1].astype(F32), 0.0).astype(BF16)
    cells, blocks = cell_maps()
    keyval = keyval_ref[...].astype(F32)
    d_keyval = None
    extra[...] = jnp.zeros(extra.shape, BF16)
    for offset, source in enumerate((from_right, d_pooled[...], from_left)):
        expanded = dot(blocks, source)
        term = spread[offset] * expanded
        d_keyval = term if d_keyval is None else d_keyval + term
        d_kernel = gather_rows(cells[:, 0:16], keyval * expanded).astype(BF16)
        extra[0, 16 * offset : 16 * offset + 16, :] = d_kernel
        extra[1, 48 + 16 * offset : 64 + 16 * offset, :] = d_kernel
    d_keyval = d_keyval.astype(BF16)
    d_key_proj, d_value_proj = d_keyval[:, 0:D], d_keyval[:, D:]

    def last_part(part):
        inside = pl.ds(part * 256, 256)
        lhs = dot_nt(orders[part], d_key_proj).astype(BF16)
        last_full[:, pl.ds(part * 512, 256)] = dot(lhs, normed_ref[:, inside]).astype(BF16)
        lhs = dot_nt(orders[part], d_value_proj).astype(BF16)
        last_full[:, pl.ds(part * 512 + 256, 256)] = dot(lhs, normed_ref[:, inside]).astype(BF16)

    for part in range(2):
        last_part(part)
        last.send0(part)
    last_part(2)
    d_normed = dot_nt(d_query[...], attn[0])
    d_normed = d_normed + dot_nt(d_key_proj, attn[1]) + dot_nt(d_value_proj, attn[2])
    unit, scale = norm_stats(load_padded(two_ref, pad).astype(F32))
    d_second = norm_back(unit, scale, gain_ref[1:2, :], d_normed)
    d_gain = jnp.sum(d_normed * unit, axis=0, keepdims=True)
    extra_gain[...] = jnp.zeros(extra_gain.shape, F32)
    extra_gain[96:97, :] = gain_one_ref[...]
    extra_gain[97:98, :] = d_gain
    source = source_column(iota((D, 128), 0), 2)
    lanes = iota((D, 128), 1)
    block = dot_nt(orders[2], extra_gain[...].astype(BF16))
    for k in range(KV // 128):
        for side in range(2):
            pick = jnp.where(2 * source + side == lanes + 128 * k, 1.0, 0.0).astype(BF16)
            block = block + dot_nt(pick, extra[side, :, k * 128 : (k + 1) * 128])
    last_full[:, pl.ds(1536, 128)] = block.astype(BF16)
    last.send0(2)
    result = load_padded(cot_two_ref, pad).astype(F32) + d_second
    store_grid(grad_two_out, result.astype(BF16))

    for part in range(3):
        first.send2(part)
    for part in range(3):
        last.send1(part)
    for part in range(3):
        mlp.send3(part)
    for part in range(3):
        first.send3(part)
    for part in range(3):
        last.send2(part)
    for part in range(3):
        mlp.finish(part)
    for part in range(3):
        last.send3(part)
    for part in range(3):
        first.finish(part)
    for part in range(3):
        last.finish(part)
    for copy in links.started:
        copy.wait_send()


def run_attention(ready, half_one, input_two, grad_two, norm_gain, pool_kernel, attn_weight, mlp_sums):
    vmem = pl.BlockSpec(memory_space=pltpu.VMEM)
    hbm = pl.BlockSpec(memory_space=pl.ANY)
    shape = jax.ShapeDtypeStruct
    scratch = [
        pltpu.SemaphoreType.DMA((N_COPIES,)),
        pltpu.SemaphoreType.DMA((N_COPIES,)),
        pltpu.SemaphoreType.DMA((4,)),
        pltpu.VMEM((HALF, MLP_COLS), BF16), *landing(MLP_COLS),
        pltpu.VMEM((D, FIRST_COLS), BF16), *landing(FIRST_COLS),
        pltpu.VMEM((D, LAST_COLS), BF16), *landing(LAST_COLS),
        pltpu.VMEM((4, D, D), BF16),
        pltpu.VMEM((3, ROWS, KV), F32),
        pltpu.VMEM((3, D, D), BF16),
        pltpu.VMEM((16, KV), F32),
        pltpu.VMEM((2, 16, KV), F32),
        pltpu.VMEM((16, KV), BF16),
        pltpu.VMEM((14, 16, D), BF16),
        *[pltpu.VMEM((4, 4, 32, D), BF16) for _ in range(4)],
        pltpu.VMEM((3, 4, 32, D), BF16),
        pltpu.VMEM((3, 32, D), BF16),
        pltpu.VMEM((16, D), BF16),
        pltpu.VMEM((3, 32, D), BF16),
        pltpu.VMEM((3, 4, 32, D), BF16),
        pltpu.VMEM((16, D), BF16),
        pltpu.VMEM((4, 32, D), BF16),
        pltpu.VMEM((4, 32, D), BF16),
        pltpu.VMEM((32, D), BF16),
        pltpu.VMEM((32, D), BF16),
        pltpu.VMEM((16, KV), BF16),
        pltpu.VMEM((2, 16, KV), BF16),
        pltpu.VMEM((ROWS, D), BF16),
        pltpu.VMEM((ROWS, D), BF16),
        pltpu.VMEM((2, 128, KV), BF16),
        pltpu.VMEM((128, D), F32),
    ]
    return pl.pallas_call(
        attention_kernel,
        in_specs=[vmem] * 12 + [hbm] * 2,
        out_specs=[vmem] * 3,
        out_shape=[
            shape(half_one.shape, BF16), shape(half_one.shape, BF16),
            shape((8, MLP_COLS + FIRST_COLS + LAST_COLS), F32),
        ],
        scratch_shapes=scratch,
        compiler_params=pltpu.CompilerParams(
            collective_id=0, has_side_effects=True, vmem_limit_bytes=62 * MIB
        ),
        name="attention_branch",
    )(*ready, half_one, input_two, grad_two, norm_gain, pool_kernel, attn_weight, mlp_sums)


def shards(half_one, half_two, grad_one, grad_two, norm_gain, attn_weight, mlp_weight, pool_kernel):
    (input_two, total, mlp_sums, normed, query, keyval, d_att, total_pad, parts, gain_one) = run_mlp(
        half_one, half_two, grad_one, grad_two, norm_gain, attn_weight, mlp_weight, pool_kernel
    )
    input_one, input_grad_two, sums = run_attention(
        (query, keyval, d_att, total_pad, normed, parts, gain_one),
        half_one, input_two, grad_two, norm_gain, pool_kernel, attn_weight, mlp_sums,
    )
    sums = sums[0:6]
    mlp_grad = sums[:, 0:MLP_COLS].reshape(6, STEPS, 2, CHUNK)
    mlp_grad = mlp_grad.transpose(2, 1, 3, 0).reshape(2, FF, 6)
    first = sums[:, MLP_COLS : MLP_COLS + FIRST_COLS].reshape(6, 3, 2, 256)
    first = first.transpose(2, 1, 3, 0).reshape(2, D, 6)
    last = sums[:, MLP_COLS + FIRST_COLS :]
    rest = last[:, 1536:]
    last = last[:, 0:1536].reshape(6, 3, 2, 256).transpose(2, 1, 3, 0).reshape(2, D, 6)
    attn_grad = jnp.concatenate([first[0:1], last, first[1:2]], axis=0)
    kernel_grad = rest[:, 0:96].reshape(6, 2, 48).transpose(2, 0, 1).reshape(3, 4, 4, 12)
    gain_grad = rest[:, 96:98].T
    return (input_one, input_two, total, input_grad_two, attn_grad, mlp_grad, kernel_grad, gain_grad)


def solution(mesh):
    placed = (
        P("clip", "tm", None, None, None),
        P("clip", "tm", None, None, None),
        P("clip", "tm", None, None, None),
        P("clip", "tm", None, None, None),
        P(),
        P(),
        P(),
        P(),
    )
    return jax.shard_map(
        shards,
        mesh=mesh,
        in_specs=placed,
        out_specs=(
            P("clip", "tm", None, None, None),
            P("clip", "tm", None, None, None),
            P("clip", "tm", None, None, None),
            P("clip", "tm", None, None, None),
            P(None, None, ("clip", "tm")),
            P(None, None, ("clip", "tm")),
            P(None, None, None, ("clip", "tm")),
            P(None, ("clip", "tm")),
        ),
        check_vma=False,
    )
```

```python
from functools import partial

import jax
import jax.numpy as jnp
from jax import lax
from jax.experimental import pallas as pl
from jax.experimental.pallas import tpu as pltpu
from jax.sharding import PartitionSpec as P

D = 768
FF = 3072
KV = 2 * D
ROWS = 224
CHUNK = 512
STEPS = FF // CHUNK
HALF = 384
MIB = 1024 * 1024
F32 = jnp.float32
BF16 = jnp.bfloat16
MESH = pl.DeviceIdType.MESH


def dot(a, b):
    return lax.dot_general(a, b, (((1,), (0,)), ((), ())), preferred_element_type=F32)


def dot_nt(a, b):
    return lax.dot_general(a, b, (((1,), (1,)), ((), ())), preferred_element_type=F32)


def dot_tn(a, b):
    return lax.dot_general(a, b, (((0,), (0,)), ((), ())), preferred_element_type=F32)


def iota(shape, dim):
    return lax.broadcasted_iota(jnp.int32, shape, dim)


def source_column(rows, part):
    owner_at = (rows * 43691) >> 18
    inner = rows - owner_at * 6
    core = owner_at >> 6
    digits = ((owner_at >> 4) & 3, (owner_at >> 2) & 3, owner_at & 3)
    x, y, z = (digits[(axis - part) % 3] for axis in range(3))
    owner = (y >> 1) * 64 + core * 32 + x * 8 + z * 2 + (y & 1)
    return owner * 6 + inner


def permutation(part):
    source = source_column(iota((D, 128), 0), part)
    lanes = iota((D, 128), 1)
    pieces = [
        jnp.where(source == lanes + 128 * k, 1.0, 0.0).astype(BF16) for k in range(D // 128)
    ]
    return jnp.concatenate(pieces, axis=1)


def norm_stats(values):
    centre = jnp.mean(values, axis=-1, keepdims=True)
    centred = values - centre
    spread = jnp.mean(centred * centred, axis=-1, keepdims=True)
    scale = lax.rsqrt(spread + 1e-05)
    return centred * scale, scale


def norm_back(unit, scale, gain, cotangent):
    d_unit = cotangent * gain
    first = jnp.mean(d_unit, axis=-1, keepdims=True)
    second = jnp.mean(d_unit * unit, axis=-1, keepdims=True)
    return scale * (d_unit - first - unit * second)


def load_padded(ref, pad):
    pad[...] = jnp.zeros(pad.shape, pad.dtype)
    pad[:, 0:14, :] = ref[0, 0]
    return pad[...].reshape(ROWS, D)


def store_grid(ref, values):
    ref[0, 0] = values.reshape(14, 16, D)[:, 0:14, :]


def cell_maps():
    row = iota((ROWS, 48), 0)
    across, down = (row & 15) + 1, (row >> 4) + 1
    valid = across < 15
    cell = (down & 3) * 4 + (across & 3)
    lane = iota((ROWS, 48), 1)
    cells = jnp.where(valid & ((lane & 15) == cell), 1.0, 0.0).astype(BF16)
    row = iota((ROWS, 16), 0)
    across, down = (row & 15) + 1, (row >> 4) + 1
    block = (down >> 2) * 4 + (across >> 2)
    blocks = jnp.where((across < 15) & (iota((ROWS, 16), 1) == block), 1.0, 0.0).astype(BF16)
    return cells, blocks


def spread_kernel(cells, flat):
    high = flat.astype(BF16)
    rest = flat - high.astype(F32)
    middle = rest.astype(BF16)
    low = (rest - middle.astype(F32)).astype(BF16)
    return dot(cells, jnp.concatenate([high, middle, low], axis=0))


def gather_rows(one_hot, values):
    high = values.astype(BF16)
    low = (values - high.astype(F32)).astype(BF16)
    return dot_tn(one_hot, high) + dot_tn(one_hot, low)


class Links:
    def __init__(self, send, recv):
        self.send, self.recv, self.used, self.started = send, recv, 0, []

    def start(self, source, target, device, shift=0, slots=1):
        copy = pltpu.make_async_remote_copy(
            src_ref=source, dst_ref=target,
            send_sem=self.send.at[self.used], recv_sem=self.recv.at[self.used + shift],
            device_id=device, device_id_type=MESH,
        )
        self.used += slots
        copy.start()
        self.started.append(copy)
        return copy

    def arrival(self, target, number):
        pltpu.make_async_remote_copy(
            src_ref=target, dst_ref=target,
            send_sem=self.send.at[number], recv_sem=self.recv.at[number],
            device_id=(lax.axis_index("clip"), lax.axis_index("tm")), device_id_type=MESH,
        ).wait_recv()

    def sent(self, copy):
        copy.wait_send()
        self.started = [other for other in self.started if other is not copy]


class Place:
    def __init__(self):
        clip, tm = lax.axis_index("clip"), lax.axis_index("tm")
        self.tm, self.clip = tm, clip
        self.core, high = clip % 2, clip // 2
        self.low = tm % 2
        self.at = (tm // 8, high * 2 + self.low, (tm // 2) % 4)

    def device(self, core, at):
        x, y, z = at
        return ((y // 2) * 2 + core, x * 8 + z * 2 + y % 2)

    def other_core(self):
        return self.device(1 - self.core, self.at)

    def along(self, axis, hop):
        at = list(self.at)
        at[axis] = (at[axis] + hop) % 4
        return self.device(self.core, at), at[axis]

    def pair(self, hop, low):
        return (self.clip, (self.tm - self.low + 2 * hop + 32) % 32 + low)


class Reduction:
    def __init__(self, links, place, parts, held, base, offset, landed, store):
        self.links, self.place, self.parts = links, place, parts
        self.held, self.base, self.offset = held, base, offset
        self.in0, self.in1, self.sum1, self.in2, self.sum2, self.in3 = landed
        self.store = store
        self.copies = {}

    def columns(self, part, offset=0):
        return pl.ds(self.parts[part][0] + offset, self.parts[part][1])

    def blocks(self, part, width=512):
        first, count = self.parts[part]
        if count % width:
            width = count
        return [(first + k * width, width) for k in range(count // width)]

    def send0(self, part):
        cols = self.columns(part)
        rows = pl.ds(pl.multiple_of((1 - self.place.core) * HALF, HALF), HALF)
        self.copies[0, part] = [
            self.links.start(
                self.held.at[rows, self.columns(part, self.offset)], self.in0.at[:, cols],
                self.place.other_core(),
            )
        ]

    def arrive(self, stage, part):
        for copy in self.copies[stage, part]:
            copy.wait_recv()

    def spread(self, stage, part, source, base, offset, rows, target):
        axis = (part + stage - 1) % 3
        cols = self.columns(part)
        source_cols = self.columns(part, offset)
        self.copies[stage, part] = []
        for hop in (2, 1, 3):
            device, at = self.place.along(axis, hop)
            window = pl.ds(pl.multiple_of(base + at * rows, rows), rows)
            self.copies[stage, part].append(
                self.links.start(
                    source.at[window, source_cols], target.at[hop - 1, :, cols], device
                )
            )

    def send1(self, part):
        self.arrive(0, part)
        first, count = self.parts[part]

        def body(k, carry):
            rows = pl.ds(pl.multiple_of(k * 16, 16), 16)
            mine = pl.ds(pl.multiple_of(self.base + k * 16, 16), 16)
            cols, held_cols = pl.ds(first, count), pl.ds(first + self.offset, count)
            total = self.held[mine, held_cols].astype(F32) + self.in0[rows, cols].astype(F32)
            self.held[mine, held_cols] = total.astype(BF16)
            return carry

        lax.fori_loop(0, HALF // 16, body, 0)
        self.spread(1, part, self.held, self.base, self.offset, 96, self.in1)

    def send2(self, part):
        self.arrive(1, part)
        mine = self.place.at[part % 3]
        rows = pl.ds(pl.multiple_of(self.base + mine * 96, 96), 96)
        place_row, place_col = iota((128, 96), 0), iota((128, 96), 1)
        owner = place_row >> 3
        inner = place_row & 7
        widen = jnp.where((inner < 6) & (place_col == owner * 6 + inner), 1.0, 0.0).astype(BF16)
        for first, count in self.blocks(part):
            cols = pl.ds(first, count)
            total = self.held[rows, pl.ds(first + self.offset, count)].astype(F32)
            for slot in range(3):
                total = total + self.in1[slot, :, cols].astype(F32)
            self.sum1[:, cols] = dot(widen, total.astype(BF16)).astype(BF16)
        self.spread(2, part, self.sum1, 0, 0, 32, self.in2)

    def send3(self, part):
        self.arrive(2, part)
        mine = self.place.at[(part + 1) % 3]
        rows = pl.ds(pl.multiple_of(mine * 32, 32), 32)
        for first, count in self.blocks(part):
            cols = pl.ds(first, count)
            total = self.sum1[rows, cols].astype(F32)
            for slot in range(3):
                total = total + self.in2[slot, :, cols].astype(F32)
            self.sum2[:, cols] = total
        self.spread(3, part, self.sum2, 0, 0, 8, self.in3)

    def finish(self, part):
        self.arrive(3, part)
        mine = self.place.at[(part + 2) % 3]
        rows = pl.ds(pl.multiple_of(mine * 8, 8), 8)
        for first, count in self.blocks(part):
            cols = pl.ds(first, count)
            total = self.sum2[rows, cols]
            for slot in range(3):
                total = total + self.in3[slot, :, cols]
            self.store(part, (first - self.parts[part][0]) // 512, total)


MLP_PARTS = tuple((p * 2048, 2048) for p in range(3))
FIRST_PARTS = tuple((p * 512, 512) for p in range(3))
LAST_PARTS = ((0, 512), (512, 512), (1024, 640))
MLP_COLS, FIRST_COLS, LAST_COLS = 6144, 1536, 1664
CHUNK_ORDER = (0, 1, 4, 5, 2, 3)
N_COPIES = 6 + 3 * 9 + 2 * 30 + 6 + 12 + 18 + 6


def landing(cols):
    return [
        pltpu.VMEM((HALF, cols), BF16),
        pltpu.VMEM((3, 96, cols), BF16),
        pltpu.VMEM((128, cols), BF16),
        pltpu.VMEM((3, 32, cols), BF16),
        pltpu.VMEM((32, cols), F32),
        pltpu.VMEM((3, 8, cols), F32),
    ]


def block_kernel(
    one_hbm, two_hbm, cot_one_hbm, cot_two_hbm, gain_ref, attn_hbm, mlp_hbm, pool_hbm,
    one_out, two_out, total_out, grad_two_out, mlp_out, attn_out, rest_out,
    *scratch,
):
    scratch = list(scratch)

    def take(count):
        taken = scratch[:count]
        del scratch[:count]
        return taken

    send_sem, recv_sem, local_sem, weight_sem = take(4)
    one_in, two_in, cot_one_in, cot_two_in, pool_in = take(5)
    up_buf, down_buf, stage = take(3)
    mlp_own, mlp_land = take(1)[0], take(6)
    first_land, last_land = take(6), take(6)
    attn, orders, pool, pad = take(4)
    normed, cot, branch, d_normed = take(4)
    normed_two, query, keyval, d_att, total, lefts = take(6)
    parts, from_pair, from_edge = take(3)
    keys, values, d_keys, d_values = take(4)
    x_keys, z_keys, x_values, z_values = take(4)
    key_sum, value_sum, pair_sum, pair_land, edge_land = take(5)
    attended, d_query, extra, extra_gain = take(4)

    place = Place()
    links = Links(send_sem, recv_sem)
    x, y, z = place.at
    low = place.low

    sources = (one_hbm, cot_two_hbm, two_hbm, cot_one_hbm, pool_hbm, attn_hbm)
    targets = (one_in, cot_two_in, two_in, cot_one_in, pool_in, attn)
    fetches = [
        pltpu.make_async_copy(source, target, local_sem.at[k])
        for k, (source, target) in enumerate(zip(sources, targets))
    ]
    one_copy, cot_two_copy, two_copy, cot_one_copy, pool_copy, attn_copy = fetches

    def weight_copies(k):
        rows = pl.ds(CHUNK_ORDER[k] * CHUNK, CHUNK)
        return [
            pltpu.make_async_copy(mlp_hbm.at[0, rows], up_buf.at[k % 2], weight_sem.at[0, k % 2]),
            pltpu.make_async_copy(mlp_hbm.at[1, rows], down_buf.at[k % 2], weight_sem.at[1, k % 2]),
        ]

    one_copy.start()
    cot_two_copy.start()
    for k in range(2):
        for copy in weight_copies(k):
            copy.start()
    for copy in fetches[2:]:
        copy.start()

    barrier = pltpu.get_barrier_semaphore()
    partners = [place.other_core()]
    partners += [place.pair(hop, side) for hop in (-1, 1) for side in range(2)]
    partners += [place.along(axis, hop)[0] for axis in range(3) for hop in (1, 2, 3)]
    for device in partners:
        pl.semaphore_signal(barrier, inc=1, device_id=device, device_id_type=MESH)

    def store_mlp(part, block, values):
        at = pl.ds((2 * part + block // 2) * CHUNK, CHUNK)
        mlp_out[:, block % 2, at] = values[0:6]

    def store_first(part, block, values):
        at = pl.ds(part * 256, 256)
        attn_out[:, 0, at] = values[0:6, 0:256]
        attn_out[:, 3, at] = values[0:6, 256:512]

    def store_last(part, block, values):
        at = pl.ds(part * 256, 256)
        attn_out[:, 1, at] = values[0:6, 0:256]
        attn_out[:, 2, at] = values[0:6, 256:512]
        if part == 2:
            rest_out[...] = values[:, 512:640]

    own_base = pl.multiple_of(place.core * HALF, HALF)
    other_base = pl.multiple_of((1 - place.core) * HALF, HALF)
    mlp = Reduction(links, place, MLP_PARTS, mlp_own, 0, 0, mlp_land, store_mlp)
    first = Reduction(links, place, FIRST_PARTS, stage, own_base, 0, first_land, store_first)
    last = Reduction(links, place, LAST_PARTS, stage, own_base, FIRST_COLS, last_land, store_last)

    one_copy.wait()
    unit, scale = norm_stats(load_padded(one_in, pad).astype(F32))
    normed[...] = (unit * gain_ref[0:1, :]).astype(BF16)
    cot_two_copy.wait()
    cot[...] = load_padded(cot_two_in, pad)
    for k, chunk in enumerate(CHUNK_ORDER):
        part = chunk // 2
        if chunk % 2 == 0:
            orders[part] = permutation(part)
            lefts[0] = dot_nt(orders[part], normed[...]).astype(BF16)
            lefts[1] = dot_nt(orders[part], cot[...]).astype(BF16)
        for copy in weight_copies(k):
            copy.wait()
        up, down = up_buf[k % 2], down_buf[k % 2]
        hidden = dot_nt(normed[...], up)
        inner = 0.7978845608028654 * (hidden + 0.044715 * hidden * hidden * hidden)
        tanh = jnp.tanh(inner)
        half_sum = 0.5 * (1.0 + tanh)
        active = (hidden * half_sum).astype(BF16)
        slope = half_sum + 0.5 * hidden * (1.0 - tanh * tanh) * (
            0.7978845608028654 * (1.0 + 3.0 * 0.044715 * hidden * hidden)
        )
        d_hidden = (slope * dot_nt(cot[...], down)).astype(BF16)
        if k == 0:
            branch[...] = dot(active, down)
            d_normed[...] = dot(d_hidden, up)
        else:
            branch[...] += dot(active, down)
            d_normed[...] += dot(d_hidden, up)
        if k + 2 < STEPS:
            for copy in weight_copies(k + 2):
                copy.start()
        at = (chunk % 2) * HALF
        cols = part * 2 * CHUNK
        for side, values_in in enumerate((d_hidden, active)):
            rows = pl.ds(other_base, HALF)
            stage[pl.ds(at, HALF), pl.ds(cols + side * CHUNK, CHUNK)] = dot(
                lefts[side, rows], values_in
            ).astype(BF16)
        if k == 0:
            pl.semaphore_wait(barrier, len(partners))
        mlp.copies.setdefault((0, part), []).append(
            links.start(
                stage.at[pl.ds(at, HALF), pl.ds(cols, 2 * CHUNK)],
                mlp.in0.at[:, pl.ds(chunk * 2 * CHUNK, 2 * CHUNK)],
                place.other_core(),
            )
        )
        for side, values_in in enumerate((d_hidden, active)):
            rows = pl.ds(own_base, HALF)
            mlp_own[:, pl.ds(chunk * 2 * CHUNK + side * CHUNK, CHUNK)] = dot(
                lefts[side, rows], values_in
            ).astype(BF16)
        if k == 2:
            mlp.send1(0)
        if k == 4:
            mlp.send1(2)

    two_copy.wait()
    restored = (load_padded(two_in, pad).astype(F32) - branch[...]).astype(BF16)
    store_grid(two_out, restored)
    unit_two, scale_two = norm_stats(restored.astype(F32))
    normed_two[...] = (unit_two * gain_ref[1:2, :]).astype(BF16)
    attn_copy.wait()
    keyval[:, 0:D] = dot(normed_two[...], attn[1]).astype(BF16)
    keyval[:, D:] = dot(normed_two[...], attn[2]).astype(BF16)
    cells, blocks = cell_maps()
    pool_copy.wait()
    for offset in range(3):
        for i in range(4):
            pool[offset, 4 * i : 4 * i + 4, :] = pool_in[offset, i]
        weighted = spread_kernel(cells, pool[offset]) * keyval[...].astype(F32)
        parts[2 - offset] = gather_rows(blocks, weighted).astype(BF16)

    mine = pl.ds(1 - low, 2)
    pair_copy = links.start(parts.at[mine], from_pair, place.pair(0, 1 - low))
    edge_base = links.used
    for side in range(2):
        links.start(
            parts.at[2 * low], from_edge.at[1 - low],
            (place.clip, (place.tm - low + 4 * low - 2 + 32) % 32 + side),
            shift=1 - low if side == 0 else -low, slots=1,
        )
    mlp.send1(1)
    query[...] = dot(normed_two[...], attn[0]).astype(BF16)
    back = d_normed[...]
    unit, scale = norm_stats(load_padded(one_in, pad).astype(F32))
    d_gain_one = jnp.sum(back * unit, axis=0, keepdims=True)
    d_first = norm_back(unit, scale, gain_ref[0:1, :], back)
    cot_one_copy.wait()
    total[...] = (load_padded(cot_one_in, pad).astype(F32) + d_first).astype(BF16)
    store_grid(total_out, total[...])
    pair_copy.wait_recv()
    for slot in range(2):
        links.arrival(from_edge.at[slot], edge_base + slot)
    ends = (place.tm // 2 > 0, place.tm // 2 < 15)
    for slot in range(2):
        edge = jnp.where(ends[slot], from_edge[slot].astype(F32), 0.0)
        frame = parts[1 - low + slot].astype(F32) + from_pair[slot].astype(F32) + edge
        frame = frame.astype(BF16)
        keys[x, z, 16 * slot : 16 * slot + 16, :] = frame[:, 0:D]
        values[x, z, 16 * slot : 16 * slot + 16, :] = frame[:, D:]

    copies = []
    for hop in (2, 1, 3):
        copies.append(links.start(keys.at[x, z], keys.at[x, z], place.along(2, hop)[0]))
        copies.append(links.start(values.at[x, z], values.at[x, z], place.along(0, hop)[0]))
    d_att[...] = dot_nt(total[...], attn[3]).astype(BF16)
    for copy in copies:
        copy.wait_recv()
    copies = []
    for hop in (2, 1, 3):
        copies.append(links.start(keys.at[x], keys.at[x], place.along(0, hop)[0]))
        copies.append(links.start(values.at[:, z], values.at[:, z], place.along(2, hop)[0]))
    for part in range(3):
        lefts[part] = dot_nt(orders[part], total[...]).astype(BF16)
    for copy in copies:
        copy.wait_recv()

    def heads(pair, carry):
        lanes = pl.ds(pl.multiple_of(pair * 128, 128), 128)
        query_pair = query[:, lanes]
        d_att_pair = d_att[:, lanes]
        key = keys[:, :, :, lanes].reshape(512, 128)
        value = values[:, :, :, lanes].reshape(512, 128)
        att = d_q = d_k = d_v = None
        for side in range(2):

            def only(array):
                lane = iota(array.shape, 1)
                keep = lane < 64 if side == 0 else lane >= 64
                return jnp.where(keep, array, jnp.zeros_like(array))

            query_h, d_att_h = only(query_pair), only(d_att_pair)
            weights = jnp.exp(dot_nt(query_h, key) * 0.125)
            probs = weights * (1.0 / jnp.sum(weights, axis=-1, keepdims=True))
            probs_b = probs.astype(BF16)
            d_probs = dot_nt(d_att_h, value)
            product = probs * d_probs
            d_scores = (product - probs * jnp.sum(product, axis=-1, keepdims=True)).astype(BF16)
            terms = (
                dot(probs_b, only(value)), dot(d_scores, only(key)),
                dot_tn(d_scores, query_h), dot_tn(probs_b, d_att_h),
            )
            if side == 0:
                att, d_q, d_k, d_v = terms
            else:
                att, d_q, d_k, d_v = (a + b for a, b in zip((att, d_q, d_k, d_v), terms))
        attended[:, lanes] = att.astype(BF16)
        d_query[:, lanes] = (d_q * 0.125).astype(BF16)
        d_keys[:, :, :, lanes] = (d_k * 0.125).astype(BF16).reshape(4, 4, 32, 128)
        d_values[:, :, :, lanes] = d_v.astype(BF16).reshape(4, 4, 32, 128)
        return carry

    copies = []
    for group in range(2):
        lax.fori_loop(3 * group, 3 * group + 3, heads, 0)
        lanes = pl.ds(group * HALF, HALF)
        for hop in (2, 1, 3):
            device, at = place.along(0, hop)
            copies.append(
                links.start(d_keys.at[at, :, :, lanes], x_keys.at[hop - 1, :, :, lanes], device)
            )
            device, at = place.along(2, hop)
            copies.append(
                links.start(d_values.at[:, at, :, lanes], z_values.at[hop - 1, :, :, lanes], device)
            )

    for part in (0, 2):
        mlp.send2(part)
    for part in range(3):
        for copy in mlp.copies[0, part]:
            links.sent(copy)
    branch_f = dot(attended[...], attn[3])
    store_grid(one_out, (load_padded(one_in, pad).astype(F32) - branch_f).astype(BF16))
    for part in range(3):
        inside = pl.ds(part * 256, 256)
        lhs = dot_nt(orders[part], d_query[...]).astype(BF16)
        stage[:, pl.ds(part * 512, 256)] = dot(lhs, normed_two[:, inside]).astype(BF16)
        stage[:, pl.ds(part * 512 + 256, 256)] = dot(
            lefts[part], attended[:, inside]
        ).astype(BF16)
        first.send0(part)
    d_normed[...] = dot_nt(d_query[...], attn[0])

    for copy in copies:
        copy.wait_recv()
    sum_k = d_keys[x].astype(F32)
    sum_v = d_values[:, z].astype(F32)
    for slot in range(3):
        sum_k = sum_k + x_keys[slot].astype(F32)
        sum_v = sum_v + z_values[slot].astype(F32)
    key_sum[...] = sum_k.astype(BF16)
    value_sum[...] = sum_v.astype(BF16)
    copies = []
    for hop in (2, 1, 3):
        device, at = place.along(2, hop)
        copies.append(links.start(key_sum.at[at], z_keys.at[hop - 1], device))
        device, at = place.along(0, hop)
        copies.append(links.start(value_sum.at[at], x_values.at[hop - 1], device))
    mlp.send2(1)
    for copy in copies:
        copy.wait_recv()
    sum_k = key_sum[z].astype(F32)
    sum_v = value_sum[x].astype(F32)
    for slot in range(3):
        sum_k = sum_k + z_keys[slot].astype(F32)
        sum_v = sum_v + x_values[slot].astype(F32)
    pair_sum[:, 0:D] = sum_k.astype(BF16)
    pair_sum[:, D:] = sum_v.astype(BF16)

    pair_copy = links.start(pair_sum, pair_land, place.pair(0, 1 - low))
    edge_base = links.used
    for hop, rows in ((-1, pl.ds(0, 16)), (1, pl.ds(16, 16))):
        side = 1 if hop == -1 else 0
        links.start(
            pair_sum.at[rows, :], edge_land.at[low], place.pair(hop, side),
            shift=low if hop == -1 else low - 1, slots=1,
        )
    for part in range(3):
        first.send1(part)
    pair_copy.wait_recv()
    for slot in range(2):
        links.arrival(edge_land.at[slot], edge_base + slot)
    edge = edge_land[0].astype(F32) + edge_land[1].astype(F32)
    inside = (low == 0) & (place.tm > 0) | (low == 1) & (place.tm < 31)
    edge = jnp.where(inside, edge, 0.0).astype(BF16)
    pair_frames = (pair_sum[...].astype(F32) + pair_land[...].astype(F32)).astype(BF16)
    frame_0, frame_1 = pair_frames[0:16, :], pair_frames[16:32, :]
    before = jnp.where(low == 0, edge, frame_0)
    here = jnp.where(low == 0, frame_0, frame_1)
    after = jnp.where(low == 0, frame_1, edge)

    cells, blocks = cell_maps()
    keyval_f = keyval[...].astype(F32)
    d_keyval = None
    extra[...] = jnp.zeros(extra.shape, BF16)
    for offset, source in enumerate((after, here, before)):
        expanded = dot(blocks, source)
        term = spread_kernel(cells, pool[offset]) * expanded
        d_keyval = term if d_keyval is None else d_keyval + term
        d_kernel = gather_rows(cells[:, 0:16], keyval_f * expanded).astype(BF16)
        extra[0, 16 * offset : 16 * offset + 16, :] = d_kernel
        extra[1, 48 + 16 * offset : 64 + 16 * offset, :] = d_kernel
    d_keyval = d_keyval.astype(BF16)
    d_key_proj, d_value_proj = d_keyval[:, 0:D], d_keyval[:, D:]

    def last_part(part):
        inside = pl.ds(part * 256, 256)
        start = FIRST_COLS + part * 512
        lhs = dot_nt(orders[part], d_key_proj).astype(BF16)
        stage[:, pl.ds(start, 256)] = dot(lhs, normed_two[:, inside]).astype(BF16)
        lhs = dot_nt(orders[part], d_value_proj).astype(BF16)
        stage[:, pl.ds(start + 256, 256)] = dot(lhs, normed_two[:, inside]).astype(BF16)

    for part in range(2):
        last_part(part)
        last.send0(part)
    last_part(2)
    d_normed_two = d_normed[...] + dot_nt(d_key_proj, attn[1]) + dot_nt(d_value_proj, attn[2])
    d_second = norm_back(unit_two, scale_two, gain_ref[1:2, :], d_normed_two)
    extra_gain[...] = jnp.zeros(extra_gain.shape, F32)
    extra_gain[96:97, :] = d_gain_one
    extra_gain[97:98, :] = jnp.sum(d_normed_two * unit_two, axis=0, keepdims=True)
    source = source_column(iota((D, 128), 0), 2)
    lanes = iota((D, 128), 1)
    block = dot_nt(orders[2], extra_gain[...].astype(BF16))
    for k in range(KV // 128):
        for side in range(2):
            pick = jnp.where(2 * source + side == lanes + 128 * k, 1.0, 0.0).astype(BF16)
            block = block + dot_nt(pick, extra[side, :, k * 128 : (k + 1) * 128])
    stage[:, pl.ds(FIRST_COLS + 1536, 128)] = block.astype(BF16)
    last.send0(2)
    result = load_padded(cot_two_in, pad).astype(F32) + d_second
    store_grid(grad_two_out, result.astype(BF16))

    for part in range(3):
        first.send2(part)
    for part in range(3):
        last.send1(part)
    for part in range(3):
        mlp.send3(part)
    for part in range(3):
        first.send3(part)
    for part in range(3):
        last.send2(part)
    for part in range(3):
        mlp.finish(part)
    for part in range(3):
        last.send3(part)
    for part in range(3):
        first.finish(part)
    for part in range(3):
        last.finish(part)
    for copy in links.started:
        copy.wait_send()


def run_block(half_one, half_two, grad_one, grad_two, norm_gain, attn_weight, mlp_weight, pool_kernel):
    vmem = pl.BlockSpec(memory_space=pltpu.VMEM)
    hbm = pl.BlockSpec(memory_space=pl.ANY)
    shape = jax.ShapeDtypeStruct
    scratch = [
        pltpu.SemaphoreType.DMA((N_COPIES,)),
        pltpu.SemaphoreType.DMA((N_COPIES,)),
        pltpu.SemaphoreType.DMA((6,)),
        pltpu.SemaphoreType.DMA((2, 2)),
        *[pltpu.VMEM((1, 1, 14, 14, D), BF16) for _ in range(4)],
        pltpu.VMEM((3, 4, 4, KV), F32),
        pltpu.VMEM((2, CHUNK, D), BF16),
        pltpu.VMEM((2, CHUNK, D), BF16),
        pltpu.VMEM((D, FIRST_COLS + LAST_COLS), BF16),
        pltpu.VMEM((HALF, MLP_COLS), BF16), *landing(MLP_COLS),
        *landing(FIRST_COLS),
        *landing(LAST_COLS),
        pltpu.VMEM((4, D, D), BF16),
        pltpu.VMEM((3, D, D), BF16),
        pltpu.VMEM((3, 16, KV), F32),
        pltpu.VMEM((14, 16, D), BF16),
        pltpu.VMEM((ROWS, D), BF16),
        pltpu.VMEM((ROWS, D), BF16),
        pltpu.VMEM((ROWS, D), F32),
        pltpu.VMEM((ROWS, D), F32),
        pltpu.VMEM((ROWS, D), BF16),
        pltpu.VMEM((ROWS, D), BF16),
        pltpu.VMEM((ROWS, KV), BF16),
        pltpu.VMEM((ROWS, D), BF16),
        pltpu.VMEM((ROWS, D), BF16),
        pltpu.VMEM((3, D, ROWS), BF16),
        pltpu.VMEM((3, 16, KV), BF16),
        pltpu.VMEM((2, 16, KV), BF16),
        pltpu.VMEM((2, 16, KV), BF16),
        *[pltpu.VMEM((4, 4, 32, D), BF16) for _ in range(4)],
        pltpu.VMEM((3, 4, 32, D), BF16),
        pltpu.VMEM((3, 32, D), BF16),
        pltpu.VMEM((3, 32, D), BF16),
        pltpu.VMEM((3, 4, 32, D), BF16),
        pltpu.VMEM((4, 32, D), BF16),
        pltpu.VMEM((4, 32, D), BF16),
        pltpu.VMEM((32, KV), BF16),
        pltpu.VMEM((32, KV), BF16),
        pltpu.VMEM((2, 16, KV), BF16),
        pltpu.VMEM((ROWS, D), BF16),
        pltpu.VMEM((ROWS, D), BF16),
        pltpu.VMEM((2, 128, KV), BF16),
        pltpu.VMEM((128, D), F32),
    ]
    return pl.pallas_call(
        block_kernel,
        in_specs=[hbm, hbm, hbm, hbm, vmem, hbm, hbm, hbm],
        out_specs=[vmem] * 7,
        out_shape=[
            *[shape(half_one.shape, BF16) for _ in range(4)],
            shape((6, 2, FF), F32), shape((6, 4, D), F32), shape((8, 128), F32),
        ],
        scratch_shapes=scratch,
        compiler_params=pltpu.CompilerParams(
            collective_id=0, has_side_effects=True, vmem_limit_bytes=63 * MIB
        ),
        name="reversible_block",
    )(half_one, half_two, grad_one, grad_two, norm_gain, attn_weight, mlp_weight, pool_kernel)


def shards(half_one, half_two, grad_one, grad_two, norm_gain, attn_weight, mlp_weight, pool_kernel):
    input_one, input_two, total, input_grad_two, mlp_sums, attn_sums, rest = run_block(
        half_one, half_two, grad_one, grad_two, norm_gain, attn_weight, mlp_weight, pool_kernel
    )
    mlp_grad = mlp_sums.transpose(1, 2, 0)
    attn_grad = attn_sums.transpose(1, 2, 0)
    kernel_grad = rest[0:6, 0:96].reshape(6, 2, 48).transpose(2, 0, 1).reshape(3, 4, 4, 12)
    gain_grad = rest[0:6, 96:98].T
    return (input_one, input_two, total, input_grad_two, attn_grad, mlp_grad, kernel_grad, gain_grad)


def solution(mesh):
    placed = (
        P("clip", "tm", None, None, None),
        P("clip", "tm", None, None, None),
        P("clip", "tm", None, None, None),
        P("clip", "tm", None, None, None),
        P(),
        P(),
        P(),
        P(),
    )
    return jax.shard_map(
        shards,
        mesh=mesh,
        in_specs=placed,
        out_specs=(
            P("clip", "tm", None, None, None),
            P("clip", "tm", None, None, None),
            P("clip", "tm", None, None, None),
            P("clip", "tm", None, None, None),
            P(None, None, ("clip", "tm")),
            P(None, None, ("clip", "tm")),
            P(None, None, None, ("clip", "tm")),
            P(None, ("clip", "tm")),
        ),
        check_vma=False,
    )
```

```python
from functools import partial

import jax
import jax.numpy as jnp
from jax import lax
from jax.experimental import pallas as pl
from jax.experimental.pallas import tpu as pltpu
from jax.sharding import PartitionSpec as P

D = 768
FF = 3072
KV = 2 * D
ROWS = 224
CHUNK = 512
STEPS = FF // CHUNK
HALF = 384
MIB = 1024 * 1024
F32 = jnp.float32
BF16 = jnp.bfloat16
MESH = pl.DeviceIdType.MESH


def dot(a, b):
    return lax.dot_general(a, b, (((1,), (0,)), ((), ())), preferred_element_type=F32)


def dot_nt(a, b):
    return lax.dot_general(a, b, (((1,), (1,)), ((), ())), preferred_element_type=F32)


def dot_tn(a, b):
    return lax.dot_general(a, b, (((0,), (0,)), ((), ())), preferred_element_type=F32)


def iota(shape, dim):
    return lax.broadcasted_iota(jnp.int32, shape, dim)


def source_column(rows, part):
    owner_at = (rows * 43691) >> 18
    inner = rows - owner_at * 6
    core = owner_at >> 6
    digits = ((owner_at >> 4) & 3, (owner_at >> 2) & 3, owner_at & 3)
    x, y, z = (digits[(axis - part) % 3] for axis in range(3))
    owner = (y >> 1) * 64 + core * 32 + x * 8 + z * 2 + (y & 1)
    return owner * 6 + inner


def permutation(part):
    source = source_column(iota((D, 128), 0), part)
    lanes = iota((D, 128), 1)
    pieces = [
        jnp.where(source == lanes + 128 * k, 1.0, 0.0).astype(BF16) for k in range(D // 128)
    ]
    return jnp.concatenate(pieces, axis=1)


def norm_stats(values):
    centre = jnp.mean(values, axis=-1, keepdims=True)
    centred = values - centre
    spread = jnp.mean(centred * centred, axis=-1, keepdims=True)
    scale = lax.rsqrt(spread + 1e-05)
    return centred * scale, scale


def norm_back(unit, scale, gain, cotangent):
    d_unit = cotangent * gain
    first = jnp.mean(d_unit, axis=-1, keepdims=True)
    second = jnp.mean(d_unit * unit, axis=-1, keepdims=True)
    return scale * (d_unit - first - unit * second)


def load_padded(ref, pad):
    pad[...] = jnp.zeros(pad.shape, pad.dtype)
    pad[:, 0:14, :] = ref[0, 0]
    return pad[...].reshape(ROWS, D)


def store_grid(ref, values):
    ref[0, 0] = values.reshape(14, 16, D)[:, 0:14, :]


def cell_maps():
    row = iota((ROWS, 48), 0)
    across, down = (row & 15) + 1, (row >> 4) + 1
    valid = across < 15
    cell = (down & 3) * 4 + (across & 3)
    lane = iota((ROWS, 48), 1)
    cells = jnp.where(valid & ((lane & 15) == cell), 1.0, 0.0).astype(BF16)
    row = iota((ROWS, 16), 0)
    across, down = (row & 15) + 1, (row >> 4) + 1
    block = (down >> 2) * 4 + (across >> 2)
    blocks = jnp.where((across < 15) & (iota((ROWS, 16), 1) == block), 1.0, 0.0).astype(BF16)
    return cells, blocks


def spread_kernel(cells, flat):
    high = flat.astype(BF16)
    rest = flat - high.astype(F32)
    middle = rest.astype(BF16)
    low = (rest - middle.astype(F32)).astype(BF16)
    return dot(cells, jnp.concatenate([high, middle, low], axis=0))


def gather_rows(one_hot, values):
    high = values.astype(BF16)
    low = (values - high.astype(F32)).astype(BF16)
    return dot_tn(one_hot, high) + dot_tn(one_hot, low)


class Links:
    def __init__(self, send, recv):
        self.send, self.recv, self.used, self.started = send, recv, 0, []

    def start(self, source, target, device, shift=0, slots=1):
        copy = pltpu.make_async_remote_copy(
            src_ref=source, dst_ref=target,
            send_sem=self.send.at[self.used], recv_sem=self.recv.at[self.used + shift],
            device_id=device, device_id_type=MESH,
        )
        self.used += slots
        copy.start()
        self.started.append(copy)
        return copy

    def arrival(self, target, number):
        pltpu.make_async_remote_copy(
            src_ref=target, dst_ref=target,
            send_sem=self.send.at[number], recv_sem=self.recv.at[number],
            device_id=(lax.axis_index("clip"), lax.axis_index("tm")), device_id_type=MESH,
        ).wait_recv()

    def sent(self, copy):
        copy.wait_send()
        self.started = [other for other in self.started if other is not copy]


class Place:
    def __init__(self):
        clip, tm = lax.axis_index("clip"), lax.axis_index("tm")
        self.tm, self.clip = tm, clip
        self.core, high = clip % 2, clip // 2
        self.low = tm % 2
        self.at = (tm // 8, high * 2 + self.low, (tm // 2) % 4)

    def device(self, core, at):
        x, y, z = at
        return ((y // 2) * 2 + core, x * 8 + z * 2 + y % 2)

    def other_core(self):
        return self.device(1 - self.core, self.at)

    def along(self, axis, hop):
        at = list(self.at)
        at[axis] = (at[axis] + hop) % 4
        return self.device(self.core, at), at[axis]

    def pair(self, hop, low):
        return (self.clip, (self.tm - self.low + 2 * hop + 32) % 32 + low)


class Reduction:
    def __init__(self, links, place, parts, held, base, offset, landed, store):
        self.links, self.place, self.parts = links, place, parts
        self.held, self.base, self.offset = held, base, offset
        self.in0, self.in1, self.sum1, self.in2, self.sum2, self.in3 = landed
        self.store = store
        self.copies = {}

    def columns(self, part, offset=0):
        return pl.ds(self.parts[part][0] + offset, self.parts[part][1])

    def blocks(self, part, width=512):
        first, count = self.parts[part]
        if count % width:
            width = count
        return [(first + k * width, width) for k in range(count // width)]

    def send0(self, part):
        cols = self.columns(part)
        rows = pl.ds(pl.multiple_of((1 - self.place.core) * HALF, HALF), HALF)
        self.copies[0, part] = [
            self.links.start(
                self.held.at[rows, self.columns(part, self.offset)], self.in0.at[:, cols],
                self.place.other_core(),
            )
        ]

    def arrive(self, stage, part):
        for copy in self.copies[stage, part]:
            copy.wait_recv()

    def spread(self, stage, part, source, base, offset, rows, target):
        axis = (part + stage - 1) % 3
        cols = self.columns(part)
        source_cols = self.columns(part, offset)
        self.copies[stage, part] = []
        for hop in (2, 1, 3):
            device, at = self.place.along(axis, hop)
            window = pl.ds(pl.multiple_of(base + at * rows, rows), rows)
            self.copies[stage, part].append(
                self.links.start(
                    source.at[window, source_cols], target.at[hop - 1, :, cols], device
                )
            )

    def send1(self, part):
        self.arrive(0, part)
        first, count = self.parts[part]

        def body(k, carry):
            rows = pl.ds(pl.multiple_of(k * 16, 16), 16)
            mine = pl.ds(pl.multiple_of(self.base + k * 16, 16), 16)
            cols, held_cols = pl.ds(first, count), pl.ds(first + self.offset, count)
            total = self.held[mine, held_cols].astype(F32) + self.in0[rows, cols].astype(F32)
            self.held[mine, held_cols] = total.astype(BF16)
            return carry

        lax.fori_loop(0, HALF // 16, body, 0)
        self.spread(1, part, self.held, self.base, self.offset, 96, self.in1)

    def send2(self, part):
        self.arrive(1, part)
        mine = self.place.at[part % 3]
        rows = pl.ds(pl.multiple_of(self.base + mine * 96, 96), 96)
        place_row, place_col = iota((128, 96), 0), iota((128, 96), 1)
        owner = place_row >> 3
        inner = place_row & 7
        widen = jnp.where((inner < 6) & (place_col == owner * 6 + inner), 1.0, 0.0).astype(BF16)
        for first, count in self.blocks(part):
            cols = pl.ds(first, count)
            total = self.held[rows, pl.ds(first + self.offset, count)].astype(F32)
            for slot in range(3):
                total = total + self.in1[slot, :, cols].astype(F32)
            self.sum1[:, cols] = dot(widen, total.astype(BF16)).astype(BF16)
        self.spread(2, part, self.sum1, 0, 0, 32, self.in2)

    def send3(self, part):
        self.arrive(2, part)
        mine = self.place.at[(part + 1) % 3]
        rows = pl.ds(pl.multiple_of(mine * 32, 32), 32)
        for first, count in self.blocks(part):
            cols = pl.ds(first, count)
            total = self.sum1[rows, cols].astype(F32)
            for slot in range(3):
                total = total + self.in2[slot, :, cols].astype(F32)
            self.sum2[:, cols] = total
        self.spread(3, part, self.sum2, 0, 0, 8, self.in3)

    def finish(self, part):
        self.arrive(3, part)
        mine = self.place.at[(part + 2) % 3]
        rows = pl.ds(pl.multiple_of(mine * 8, 8), 8)
        for first, count in self.blocks(part):
            cols = pl.ds(first, count)
            total = self.sum2[rows, cols]
            for slot in range(3):
                total = total + self.in3[slot, :, cols]
            self.store(part, (first - self.parts[part][0]) // 512, total)


MLP_PARTS = tuple((p * 2048, 2048) for p in range(3))
FIRST_PARTS = tuple((p * 512, 512) for p in range(3))
LAST_PARTS = ((0, 512), (512, 512), (1024, 640))
MLP_COLS, FIRST_COLS, LAST_COLS = 6144, 1536, 1664
CHUNK_ORDER = (0, 1, 4, 5, 2, 3)
N_COPIES = 6 + 3 * 9 + 2 * 30 + 6 + 12 + 18 + 6


def landing(cols):
    return [
        pltpu.VMEM((HALF, cols), BF16),
        pltpu.VMEM((3, 96, cols), BF16),
        pltpu.VMEM((128, cols), BF16),
        pltpu.VMEM((3, 32, cols), BF16),
        pltpu.VMEM((32, cols), F32),
        pltpu.VMEM((3, 8, cols), F32),
    ]


def block_kernel(
    one_hbm, two_hbm, cot_one_hbm, cot_two_hbm, gain_ref, attn_hbm, mlp_hbm, pool_hbm,
    one_out, two_out, total_out, grad_two_out, mlp_out, attn_out, rest_out,
    *scratch,
):
    scratch = list(scratch)

    def take(count):
        taken = scratch[:count]
        del scratch[:count]
        return taken

    send_sem, recv_sem, local_sem, weight_sem = take(4)
    one_in, two_in, cot_one_in, cot_two_in, pool_in = take(5)
    up_buf, down_buf, stage = take(3)
    mlp_own, mlp_land = take(1)[0], take(6)
    first_land, last_land = take(6), take(6)
    attn, orders, pool, pad = take(4)
    normed, cot, branch, d_normed = take(4)
    normed_two, query, keyval, d_att, total, lefts = take(6)
    parts, from_pair, from_edge = take(3)
    keys, values, d_keys, d_values = take(4)
    x_keys, z_keys, x_values, z_values = take(4)
    key_sum, value_sum, pair_sum, pair_land, edge_land = take(5)
    attended, d_query, extra, extra_gain = take(4)
    mlp_sums, attn_sums, rest_sums, out_sem = take(4)

    place = Place()
    links = Links(send_sem, recv_sem)
    x, y, z = place.at
    low = place.low

    sources = (one_hbm, cot_two_hbm, two_hbm, cot_one_hbm, pool_hbm, attn_hbm)
    targets = (one_in, cot_two_in, two_in, cot_one_in, pool_in, attn)
    fetches = [
        pltpu.make_async_copy(source, target, local_sem.at[k])
        for k, (source, target) in enumerate(zip(sources, targets))
    ]
    one_copy, cot_two_copy, two_copy, cot_one_copy, pool_copy, attn_copy = fetches

    def weight_copies(k):
        rows = pl.ds(CHUNK_ORDER[k] * CHUNK, CHUNK)
        return [
            pltpu.make_async_copy(mlp_hbm.at[0, rows], up_buf.at[k % 2], weight_sem.at[0, k % 2]),
            pltpu.make_async_copy(mlp_hbm.at[1, rows], down_buf.at[k % 2], weight_sem.at[1, k % 2]),
        ]

    one_copy.start()
    cot_two_copy.start()
    for k in range(2):
        for copy in weight_copies(k):
            copy.start()
    for copy in fetches[2:]:
        copy.start()

    barrier = pltpu.get_barrier_semaphore()
    partners = [place.other_core()]
    partners += [place.pair(hop, side) for hop in (-1, 1) for side in range(2)]
    partners += [place.along(axis, hop)[0] for axis in range(3) for hop in (1, 2, 3)]
    for device in partners:
        pl.semaphore_signal(barrier, inc=1, device_id=device, device_id_type=MESH)

    writes = []

    def write(source, target):
        copy = pltpu.make_async_copy(source, target, out_sem.at[len(writes)])
        copy.start()
        writes.append(copy)

    def store_mlp(part, block, values):
        at = pl.ds((2 * part + block // 2) * CHUNK, CHUNK)
        mlp_sums[:, block % 2, at] = values[0:6]

    def store_first(part, block, values):
        at = pl.ds(part * 256, 256)
        attn_sums[:, 0, at] = values[0:6, 0:256]
        attn_sums[:, 3, at] = values[0:6, 256:512]

    def store_last(part, block, values):
        at = pl.ds(part * 256, 256)
        attn_sums[:, 1, at] = values[0:6, 0:256]
        attn_sums[:, 2, at] = values[0:6, 256:512]
        if part == 2:
            rest_sums[...] = values[:, 512:640]

    own_base = pl.multiple_of(place.core * HALF, HALF)
    other_base = pl.multiple_of((1 - place.core) * HALF, HALF)
    mlp = Reduction(links, place, MLP_PARTS, mlp_own, 0, 0, mlp_land, store_mlp)
    first = Reduction(links, place, FIRST_PARTS, stage, own_base, 0, first_land, store_first)
    last = Reduction(links, place, LAST_PARTS, stage, own_base, FIRST_COLS, last_land, store_last)

    one_copy.wait()
    unit, scale = norm_stats(load_padded(one_in, pad).astype(F32))
    normed[...] = (unit * gain_ref[0:1, :]).astype(BF16)
    cot_two_copy.wait()
    cot[...] = load_padded(cot_two_in, pad)
    for k, chunk in enumerate(CHUNK_ORDER):
        part = chunk // 2
        if chunk % 2 == 0:
            orders[part] = permutation(part)
            lefts[0] = dot_nt(orders[part], normed[...]).astype(BF16)
            lefts[1] = dot_nt(orders[part], cot[...]).astype(BF16)
        for copy in weight_copies(k):
            copy.wait()
        up, down = up_buf[k % 2], down_buf[k % 2]
        hidden = dot_nt(normed[...], up)
        inner = 0.7978845608028654 * (hidden + 0.044715 * hidden * hidden * hidden)
        tanh = jnp.tanh(inner)
        half_sum = 0.5 * (1.0 + tanh)
        active = (hidden * half_sum).astype(BF16)
        slope = half_sum + 0.5 * hidden * (1.0 - tanh * tanh) * (
            0.7978845608028654 * (1.0 + 3.0 * 0.044715 * hidden * hidden)
        )
        d_hidden = (slope * dot_nt(cot[...], down)).astype(BF16)
        if k == 0:
            branch[...] = dot(active, down)
            d_normed[...] = dot(d_hidden, up)
        else:
            branch[...] += dot(active, down)
            d_normed[...] += dot(d_hidden, up)
        if k + 2 < STEPS:
            for copy in weight_copies(k + 2):
                copy.start()
        at = (chunk % 2) * HALF
        cols = part * 2 * CHUNK
        for side, values_in in enumerate((d_hidden, active)):
            rows = pl.ds(other_base, HALF)
            stage[pl.ds(at, HALF), pl.ds(cols + side * CHUNK, CHUNK)] = dot(
                lefts[side, rows], values_in
            ).astype(BF16)
        if k == 0:
            pl.semaphore_wait(barrier, len(partners))
        mlp.copies.setdefault((0, part), []).append(
            links.start(
                stage.at[pl.ds(at, HALF), pl.ds(cols, 2 * CHUNK)],
                mlp.in0.at[:, pl.ds(chunk * 2 * CHUNK, 2 * CHUNK)],
                place.other_core(),
            )
        )
        for side, values_in in enumerate((d_hidden, active)):
            rows = pl.ds(own_base, HALF)
            mlp_own[:, pl.ds(chunk * 2 * CHUNK + side * CHUNK, CHUNK)] = dot(
                lefts[side, rows], values_in
            ).astype(BF16)
        if k == 2:
            mlp.send1(0)
        if k == 4:
            mlp.send1(2)

    two_copy.wait()
    restored = (load_padded(two_in, pad).astype(F32) - branch[...]).astype(BF16)
    store_grid(two_in, restored)
    write(two_in, two_out)
    unit_two, scale_two = norm_stats(restored.astype(F32))
    normed_two[...] = (unit_two * gain_ref[1:2, :]).astype(BF16)
    attn_copy.wait()
    keyval[:, 0:D] = dot(normed_two[...], attn[1]).astype(BF16)
    keyval[:, D:] = dot(normed_two[...], attn[2]).astype(BF16)
    cells, blocks = cell_maps()
    pool_copy.wait()
    for offset in range(3):
        for i in range(4):
            pool[offset, 4 * i : 4 * i + 4, :] = pool_in[offset, i]
        weighted = spread_kernel(cells, pool[offset]) * keyval[...].astype(F32)
        parts[2 - offset] = gather_rows(blocks, weighted).astype(BF16)

    mine = pl.ds(1 - low, 2)
    pair_copy = links.start(parts.at[mine], from_pair, place.pair(0, 1 - low))
    edge_base = links.used
    for side in range(2):
        links.start(
            parts.at[2 * low], from_edge.at[1 - low],
            (place.clip, (place.tm - low + 4 * low - 2 + 32) % 32 + side),
            shift=1 - low if side == 0 else -low, slots=1,
        )
    mlp.send1(1)
    query[...] = dot(normed_two[...], attn[0]).astype(BF16)
    back = d_normed[...]
    unit, scale = norm_stats(load_padded(one_in, pad).astype(F32))
    d_gain_one = jnp.sum(back * unit, axis=0, keepdims=True)
    d_first = norm_back(unit, scale, gain_ref[0:1, :], back)
    cot_one_copy.wait()
    total[...] = (load_padded(cot_one_in, pad).astype(F32) + d_first).astype(BF16)
    store_grid(cot_one_in, total[...])
    write(cot_one_in, total_out)
    pair_copy.wait_recv()
    for slot in range(2):
        links.arrival(from_edge.at[slot], edge_base + slot)
    ends = (place.tm // 2 > 0, place.tm // 2 < 15)
    for slot in range(2):
        edge = jnp.where(ends[slot], from_edge[slot].astype(F32), 0.0)
        frame = parts[1 - low + slot].astype(F32) + from_pair[slot].astype(F32) + edge
        frame = frame.astype(BF16)
        keys[x, z, 16 * slot : 16 * slot + 16, :] = frame[:, 0:D]
        values[x, z, 16 * slot : 16 * slot + 16, :] = frame[:, D:]

    copies = []
    for hop in (2, 1, 3):
        copies.append(links.start(keys.at[x, z], keys.at[x, z], place.along(2, hop)[0]))
        copies.append(links.start(values.at[x, z], values.at[x, z], place.along(0, hop)[0]))
    d_att[...] = dot_nt(total[...], attn[3]).astype(BF16)
    for copy in copies:
        copy.wait_recv()
    copies = []
    for hop in (2, 1, 3):
        copies.append(links.start(keys.at[x], keys.at[x], place.along(0, hop)[0]))
        copies.append(links.start(values.at[:, z], values.at[:, z], place.along(2, hop)[0]))
    for part in range(3):
        lefts[part] = dot_nt(orders[part], total[...]).astype(BF16)
    for copy in copies:
        copy.wait_recv()

    def heads(pair, carry):
        lanes = pl.ds(pl.multiple_of(pair * 128, 128), 128)
        query_pair = query[:, lanes]
        d_att_pair = d_att[:, lanes]
        key = keys[:, :, :, lanes].reshape(512, 128)
        value = values[:, :, :, lanes].reshape(512, 128)
        att = d_q = d_k = d_v = None
        for side in range(2):

            def only(array):
                lane = iota(array.shape, 1)
                keep = lane < 64 if side == 0 else lane >= 64
                return jnp.where(keep, array, jnp.zeros_like(array))

            query_h, d_att_h = only(query_pair), only(d_att_pair)
            weights = jnp.exp(dot_nt(query_h, key) * 0.125)
            probs = weights * (1.0 / jnp.sum(weights, axis=-1, keepdims=True))
            probs_b = probs.astype(BF16)
            d_probs = dot_nt(d_att_h, value)
            product = probs * d_probs
            d_scores = (product - probs * jnp.sum(product, axis=-1, keepdims=True)).astype(BF16)
            terms = (
                dot(probs_b, only(value)), dot(d_scores, only(key)),
                dot_tn(d_scores, query_h), dot_tn(probs_b, d_att_h),
            )
            if side == 0:
                att, d_q, d_k, d_v = terms
            else:
                att, d_q, d_k, d_v = (a + b for a, b in zip((att, d_q, d_k, d_v), terms))
        attended[:, lanes] = att.astype(BF16)
        d_query[:, lanes] = (d_q * 0.125).astype(BF16)
        d_keys[:, :, :, lanes] = (d_k * 0.125).astype(BF16).reshape(4, 4, 32, 128)
        d_values[:, :, :, lanes] = d_v.astype(BF16).reshape(4, 4, 32, 128)
        return carry

    copies = []
    for group in range(2):
        lax.fori_loop(3 * group, 3 * group + 3, heads, 0)
        lanes = pl.ds(group * HALF, HALF)
        for hop in (2, 1, 3):
            device, at = place.along(0, hop)
            copies.append(
                links.start(d_keys.at[at, :, :, lanes], x_keys.at[hop - 1, :, :, lanes], device)
            )
            device, at = place.along(2, hop)
            copies.append(
                links.start(d_values.at[:, at, :, lanes], z_values.at[hop - 1, :, :, lanes], device)
            )

    for part in (0, 2):
        mlp.send2(part)
    for part in range(3):
        for copy in mlp.copies[0, part]:
            links.sent(copy)
    branch_f = dot(attended[...], attn[3])
    store_grid(one_in, (load_padded(one_in, pad).astype(F32) - branch_f).astype(BF16))
    write(one_in, one_out)
    for part in range(3):
        inside = pl.ds(part * 256, 256)
        lhs = dot_nt(orders[part], d_query[...]).astype(BF16)
        stage[:, pl.ds(part * 512, 256)] = dot(lhs, normed_two[:, inside]).astype(BF16)
        stage[:, pl.ds(part * 512 + 256, 256)] = dot(
            lefts[part], attended[:, inside]
        ).astype(BF16)
        first.send0(part)
    d_normed[...] = dot_nt(d_query[...], attn[0])

    for copy in copies:
        copy.wait_recv()
    sum_k = d_keys[x].astype(F32)
    sum_v = d_values[:, z].astype(F32)
    for slot in range(3):
        sum_k = sum_k + x_keys[slot].astype(F32)
        sum_v = sum_v + z_values[slot].astype(F32)
    key_sum[...] = sum_k.astype(BF16)
    value_sum[...] = sum_v.astype(BF16)
    copies = []
    for hop in (2, 1, 3):
        device, at = place.along(2, hop)
        copies.append(links.start(key_sum.at[at], z_keys.at[hop - 1], device))
        device, at = place.along(0, hop)
        copies.append(links.start(value_sum.at[at], x_values.at[hop - 1], device))
    mlp.send2(1)
    for copy in copies:
        copy.wait_recv()
    sum_k = key_sum[z].astype(F32)
    sum_v = value_sum[x].astype(F32)
    for slot in range(3):
        sum_k = sum_k + z_keys[slot].astype(F32)
        sum_v = sum_v + x_values[slot].astype(F32)
    pair_sum[:, 0:D] = sum_k.astype(BF16)
    pair_sum[:, D:] = sum_v.astype(BF16)

    pair_copy = links.start(pair_sum, pair_land, place.pair(0, 1 - low))
    edge_base = links.used
    for hop, rows in ((-1, pl.ds(0, 16)), (1, pl.ds(16, 16))):
        side = 1 if hop == -1 else 0
        links.start(
            pair_sum.at[rows, :], edge_land.at[low], place.pair(hop, side),
            shift=low if hop == -1 else low - 1, slots=1,
        )
    for part in range(3):
        first.send1(part)
    pair_copy.wait_recv()
    for slot in range(2):
        links.arrival(edge_land.at[slot], edge_base + slot)
    edge = edge_land[0].astype(F32) + edge_land[1].astype(F32)
    inside = (low == 0) & (place.tm > 0) | (low == 1) & (place.tm < 31)
    edge = jnp.where(inside, edge, 0.0).astype(BF16)
    pair_frames = (pair_sum[...].astype(F32) + pair_land[...].astype(F32)).astype(BF16)
    frame_0, frame_1 = pair_frames[0:16, :], pair_frames[16:32, :]
    before = jnp.where(low == 0, edge, frame_0)
    here = jnp.where(low == 0, frame_0, frame_1)
    after = jnp.where(low == 0, frame_1, edge)

    cells, blocks = cell_maps()
    keyval_f = keyval[...].astype(F32)
    d_keyval = None
    extra[...] = jnp.zeros(extra.shape, BF16)
    for offset, source in enumerate((after, here, before)):
        expanded = dot(blocks, source)
        term = spread_kernel(cells, pool[offset]) * expanded
        d_keyval = term if d_keyval is None else d_keyval + term
        d_kernel = gather_rows(cells[:, 0:16], keyval_f * expanded).astype(BF16)
        extra[0, 16 * offset : 16 * offset + 16, :] = d_kernel
        extra[1, 48 + 16 * offset : 64 + 16 * offset, :] = d_kernel
    d_keyval = d_keyval.astype(BF16)
    d_key_proj, d_value_proj = d_keyval[:, 0:D], d_keyval[:, D:]

    def last_part(part):
        inside = pl.ds(part * 256, 256)
        start = FIRST_COLS + part * 512
        lhs = dot_nt(orders[part], d_key_proj).astype(BF16)
        stage[:, pl.ds(start, 256)] = dot(lhs, normed_two[:, inside]).astype(BF16)
        lhs = dot_nt(orders[part], d_value_proj).astype(BF16)
        stage[:, pl.ds(start + 256, 256)] = dot(lhs, normed_two[:, inside]).astype(BF16)

    for part in range(2):
        last_part(part)
        last.send0(part)
    last_part(2)
    d_normed_two = d_normed[...] + dot_nt(d_key_proj, attn[1]) + dot_nt(d_value_proj, attn[2])
    d_second = norm_back(unit_two, scale_two, gain_ref[1:2, :], d_normed_two)
    extra_gain[...] = jnp.zeros(extra_gain.shape, F32)
    extra_gain[96:97, :] = d_gain_one
    extra_gain[97:98, :] = jnp.sum(d_normed_two * unit_two, axis=0, keepdims=True)
    source = source_column(iota((D, 128), 0), 2)
    lanes = iota((D, 128), 1)
    block = dot_nt(orders[2], extra_gain[...].astype(BF16))
    for k in range(KV // 128):
        for side in range(2):
            pick = jnp.where(2 * source + side == lanes + 128 * k, 1.0, 0.0).astype(BF16)
            block = block + dot_nt(pick, extra[side, :, k * 128 : (k + 1) * 128])
    stage[:, pl.ds(FIRST_COLS + 1536, 128)] = block.astype(BF16)
    last.send0(2)
    result = load_padded(cot_two_in, pad).astype(F32) + d_second
    store_grid(cot_two_in, result.astype(BF16))
    write(cot_two_in, grad_two_out)

    for part in range(3):
        first.send2(part)
    for part in range(3):
        last.send1(part)
    for part in range(3):
        mlp.send3(part)
    for part in range(3):
        first.send3(part)
    for part in range(3):
        last.send2(part)
    for part in range(3):
        mlp.finish(part)
    write(mlp_sums, mlp_out)
    for part in range(3):
        last.send3(part)
    for part in range(3):
        first.finish(part)
    for part in range(3):
        last.finish(part)
    write(attn_sums, attn_out)
    write(rest_sums, rest_out)
    for copy in links.started:
        copy.wait_send()
    for copy in writes:
        copy.wait()


def run_block(half_one, half_two, grad_one, grad_two, norm_gain, attn_weight, mlp_weight, pool_kernel):
    vmem = pl.BlockSpec(memory_space=pltpu.VMEM)
    hbm = pl.BlockSpec(memory_space=pl.ANY)
    shape = jax.ShapeDtypeStruct
    scratch = [
        pltpu.SemaphoreType.DMA((N_COPIES,)),
        pltpu.SemaphoreType.DMA((N_COPIES,)),
        pltpu.SemaphoreType.DMA((6,)),
        pltpu.SemaphoreType.DMA((2, 2)),
        *[pltpu.VMEM((1, 1, 14, 14, D), BF16) for _ in range(4)],
        pltpu.VMEM((3, 4, 4, KV), F32),
        pltpu.VMEM((2, CHUNK, D), BF16),
        pltpu.VMEM((2, CHUNK, D), BF16),
        pltpu.VMEM((D, FIRST_COLS + LAST_COLS), BF16),
        pltpu.VMEM((HALF, MLP_COLS), BF16), *landing(MLP_COLS),
        *landing(FIRST_COLS),
        *landing(LAST_COLS),
        pltpu.VMEM((4, D, D), BF16),
        pltpu.VMEM((3, D, D), BF16),
        pltpu.VMEM((3, 16, KV), F32),
        pltpu.VMEM((14, 16, D), BF16),
        pltpu.VMEM((ROWS, D), BF16),
        pltpu.VMEM((ROWS, D), BF16),
        pltpu.VMEM((ROWS, D), F32),
        pltpu.VMEM((ROWS, D), F32),
        pltpu.VMEM((ROWS, D), BF16),
        pltpu.VMEM((ROWS, D), BF16),
        pltpu.VMEM((ROWS, KV), BF16),
        pltpu.VMEM((ROWS, D), BF16),
        pltpu.VMEM((ROWS, D), BF16),
        pltpu.VMEM((3, D, ROWS), BF16),
        pltpu.VMEM((3, 16, KV), BF16),
        pltpu.VMEM((2, 16, KV), BF16),
        pltpu.VMEM((2, 16, KV), BF16),
        *[pltpu.VMEM((4, 4, 32, D), BF16) for _ in range(4)],
        pltpu.VMEM((3, 4, 32, D), BF16),
        pltpu.VMEM((3, 32, D), BF16),
        pltpu.VMEM((3, 32, D), BF16),
        pltpu.VMEM((3, 4, 32, D), BF16),
        pltpu.VMEM((4, 32, D), BF16),
        pltpu.VMEM((4, 32, D), BF16),
        pltpu.VMEM((32, KV), BF16),
        pltpu.VMEM((32, KV), BF16),
        pltpu.VMEM((2, 16, KV), BF16),
        pltpu.VMEM((ROWS, D), BF16),
        pltpu.VMEM((ROWS, D), BF16),
        pltpu.VMEM((2, 128, KV), BF16),
        pltpu.VMEM((128, D), F32),
        pltpu.VMEM((6, 2, FF), F32),
        pltpu.VMEM((6, 4, D), F32),
        pltpu.VMEM((8, 128), F32),
        pltpu.SemaphoreType.DMA((7,)),
    ]
    return pl.pallas_call(
        block_kernel,
        in_specs=[hbm, hbm, hbm, hbm, vmem, hbm, hbm, hbm],
        out_specs=[hbm] * 7,
        out_shape=[
            *[shape(half_one.shape, BF16) for _ in range(4)],
            shape((6, 2, FF), F32), shape((6, 4, D), F32), shape((8, 128), F32),
        ],
        scratch_shapes=scratch,
        compiler_params=pltpu.CompilerParams(
            collective_id=0, has_side_effects=True, vmem_limit_bytes=63 * MIB
        ),
        name="reversible_block",
    )(half_one, half_two, grad_one, grad_two, norm_gain, attn_weight, mlp_weight, pool_kernel)


def hand_out_kernel(*refs):
    taken, rest_ref, given, kernel_out, gain_out, sem = refs[0:6], refs[6], refs[7:13], *refs[13:]
    copies = [
        pltpu.make_async_copy(source, target, sem.at[k])
        for k, (source, target) in enumerate(zip(taken, given))
    ]
    for copy in copies:
        copy.start()
    rest = rest_ref[...]

    def columns(width, step, side):
        row, lane = iota((8, width), 0), iota((8, width), 1)
        pick = jnp.where((row < 6) & (lane == step * row + side), 1.0, 0.0)
        return lax.dot_general(
            rest, pick, (((0,), (0,)), ((), ())),
            precision=lax.Precision.HIGHEST, preferred_element_type=F32,
        )

    kernel_grad = columns(12, 2, 0)[0:48] + columns(12, 2, 1)[48:96]
    for offset in range(3):
        for i in range(4):
            at = 16 * offset + 4 * i
            kernel_out[offset, i] = kernel_grad[at : at + 4]
    gain_out[...] = columns(6, 1, 0)[96:98]
    for copy in copies:
        copy.wait()


def hand_out(results, rest):
    vmem = pl.BlockSpec(memory_space=pltpu.VMEM)
    hbm = pl.BlockSpec(memory_space=pl.ANY)
    shape = jax.ShapeDtypeStruct
    return pl.pallas_call(
        hand_out_kernel,
        in_specs=[hbm] * 6 + [vmem],
        out_specs=[hbm] * 6 + [vmem] * 2,
        out_shape=[shape(array.shape, array.dtype) for array in results]
        + [shape((3, 4, 4, 12), F32), shape((2, 6), F32)],
        scratch_shapes=[pltpu.SemaphoreType.DMA((6,))],
        compiler_params=pltpu.CompilerParams(vmem_limit_bytes=62 * MIB),
        name="hand_out",
    )(*results, rest)


def shards(half_one, half_two, grad_one, grad_two, norm_gain, attn_weight, mlp_weight, pool_kernel):
    *results, rest = run_block(
        half_one, half_two, grad_one, grad_two, norm_gain, attn_weight, mlp_weight, pool_kernel
    )
    (input_one, input_two, total, input_grad_two, mlp_sums, attn_sums, kernel_grad, gain_grad) = (
        hand_out(results, rest)
    )
    mlp_grad = mlp_sums.transpose(1, 2, 0)
    attn_grad = attn_sums.transpose(1, 2, 0)
    return (input_one, input_two, total, input_grad_two, attn_grad, mlp_grad, kernel_grad, gain_grad)


def solution(mesh):
    placed = (
        P("clip", "tm", None, None, None),
        P("clip", "tm", None, None, None),
        P("clip", "tm", None, None, None),
        P("clip", "tm", None, None, None),
        P(),
        P(),
        P(),
        P(),
    )
    return jax.shard_map(
        shards,
        mesh=mesh,
        in_specs=placed,
        out_specs=(
            P("clip", "tm", None, None, None),
            P("clip", "tm", None, None, None),
            P("clip", "tm", None, None, None),
            P("clip", "tm", None, None, None),
            P(None, None, ("clip", "tm")),
            P(None, None, ("clip", "tm")),
            P(None, None, None, ("clip", "tm")),
            P(None, ("clip", "tm")),
        ),
        check_vma=False,
    )
```

```python
from functools import partial

import jax
import jax.numpy as jnp
from jax import lax
from jax.experimental import pallas as pl
from jax.experimental.pallas import tpu as pltpu
from jax.sharding import PartitionSpec as P

D = 768
FF = 3072
KV = 2 * D
ROWS = 224
CHUNK = 512
STEPS = FF // CHUNK
HALF = 384
MIB = 1024 * 1024
F32 = jnp.float32
BF16 = jnp.bfloat16
MESH = pl.DeviceIdType.MESH


def dot(a, b):
    return lax.dot_general(a, b, (((1,), (0,)), ((), ())), preferred_element_type=F32)


def dot_nt(a, b):
    return lax.dot_general(a, b, (((1,), (1,)), ((), ())), preferred_element_type=F32)


def dot_tn(a, b):
    return lax.dot_general(a, b, (((0,), (0,)), ((), ())), preferred_element_type=F32)


def iota(shape, dim):
    return lax.broadcasted_iota(jnp.int32, shape, dim)


def source_column(rows, part):
    owner_at = (rows * 43691) >> 18
    inner = rows - owner_at * 6
    core = owner_at >> 6
    digits = ((owner_at >> 4) & 3, (owner_at >> 2) & 3, owner_at & 3)
    x, y, z = (digits[(axis - part) % 3] for axis in range(3))
    owner = (y >> 1) * 64 + core * 32 + x * 8 + z * 2 + (y & 1)
    return owner * 6 + inner


def permutation(part):
    source = source_column(iota((D, 128), 0), part)
    lanes = iota((D, 128), 1)
    pieces = [
        jnp.where(source == lanes + 128 * k, 1.0, 0.0).astype(BF16) for k in range(D // 128)
    ]
    return jnp.concatenate(pieces, axis=1)


def norm_stats(values):
    centre = jnp.mean(values, axis=-1, keepdims=True)
    centred = values - centre
    spread = jnp.mean(centred * centred, axis=-1, keepdims=True)
    scale = lax.rsqrt(spread + 1e-05)
    return centred * scale, scale


def norm_back(unit, scale, gain, cotangent):
    d_unit = cotangent * gain
    first = jnp.mean(d_unit, axis=-1, keepdims=True)
    second = jnp.mean(d_unit * unit, axis=-1, keepdims=True)
    return scale * (d_unit - first - unit * second)


def load_padded(ref, pad):
    pad[...] = jnp.zeros(pad.shape, pad.dtype)
    pad[:, 0:14, :] = ref[0, 0]
    return pad[...].reshape(ROWS, D)


def store_grid(ref, values):
    ref[0, 0] = values.reshape(14, 16, D)[:, 0:14, :]


def cell_maps():
    row = iota((ROWS, 48), 0)
    across, down = (row & 15) + 1, (row >> 4) + 1
    valid = across < 15
    cell = (down & 3) * 4 + (across & 3)
    lane = iota((ROWS, 48), 1)
    cells = jnp.where(valid & ((lane & 15) == cell), 1.0, 0.0).astype(BF16)
    row = iota((ROWS, 16), 0)
    across, down = (row & 15) + 1, (row >> 4) + 1
    block = (down >> 2) * 4 + (across >> 2)
    blocks = jnp.where((across < 15) & (iota((ROWS, 16), 1) == block), 1.0, 0.0).astype(BF16)
    return cells, blocks


def spread_kernel(cells, flat):
    high = flat.astype(BF16)
    rest = flat - high.astype(F32)
    middle = rest.astype(BF16)
    low = (rest - middle.astype(F32)).astype(BF16)
    return dot(cells, jnp.concatenate([high, middle, low], axis=0))


def gather_rows(one_hot, values):
    high = values.astype(BF16)
    low = (values - high.astype(F32)).astype(BF16)
    return dot_tn(one_hot, high) + dot_tn(one_hot, low)


class Links:
    def __init__(self, send, recv):
        self.send, self.recv, self.used, self.started = send, recv, 0, []

    def start(self, source, target, device, shift=0, slots=1):
        copy = pltpu.make_async_remote_copy(
            src_ref=source, dst_ref=target,
            send_sem=self.send.at[self.used], recv_sem=self.recv.at[self.used + shift],
            device_id=device, device_id_type=MESH,
        )
        self.used += slots
        copy.start()
        self.started.append(copy)
        return copy

    def arrival(self, target, number):
        pltpu.make_async_remote_copy(
            src_ref=target, dst_ref=target,
            send_sem=self.send.at[number], recv_sem=self.recv.at[number],
            device_id=(lax.axis_index("clip"), lax.axis_index("tm")), device_id_type=MESH,
        ).wait_recv()

    def sent(self, copy):
        copy.wait_send()
        self.started = [other for other in self.started if other is not copy]


class Place:
    def __init__(self):
        clip, tm = lax.axis_index("clip"), lax.axis_index("tm")
        self.tm, self.clip = tm, clip
        self.core, high = clip % 2, clip // 2
        self.low = tm % 2
        self.at = (tm // 8, high * 2 + self.low, (tm // 2) % 4)

    def device(self, core, at):
        x, y, z = at
        return ((y // 2) * 2 + core, x * 8 + z * 2 + y % 2)

    def other_core(self):
        return self.device(1 - self.core, self.at)

    def along(self, axis, hop):
        at = list(self.at)
        at[axis] = (at[axis] + hop) % 4
        return self.device(self.core, at), at[axis]

    def pair(self, hop, low):
        return (self.clip, (self.tm - self.low + 2 * hop + 32) % 32 + low)


class Reduction:
    def __init__(self, links, place, parts, held, base, offset, landed, store):
        self.links, self.place, self.parts = links, place, parts
        self.held, self.base, self.offset = held, base, offset
        self.in0, self.in1, self.sum1, self.in2, self.sum2, self.in3 = landed
        self.store = store
        self.copies = {}

    def columns(self, part, offset=0):
        return pl.ds(self.parts[part][0] + offset, self.parts[part][1])

    def blocks(self, part, width=512):
        first, count = self.parts[part]
        if count % width:
            width = count
        return [(first + k * width, width) for k in range(count // width)]

    def send0(self, part):
        cols = self.columns(part)
        rows = pl.ds(pl.multiple_of((1 - self.place.core) * HALF, HALF), HALF)
        self.copies[0, part] = [
            self.links.start(
                self.held.at[rows, self.columns(part, self.offset)], self.in0.at[:, cols],
                self.place.other_core(),
            )
        ]

    def arrive(self, stage, part):
        for copy in self.copies[stage, part]:
            copy.wait_recv()

    def spread(self, stage, part, source, base, offset, rows, target):
        axis = (part + stage - 1) % 3
        cols = self.columns(part)
        source_cols = self.columns(part, offset)
        self.copies[stage, part] = []
        for hop in (2, 1, 3):
            device, at = self.place.along(axis, hop)
            window = pl.ds(pl.multiple_of(base + at * rows, rows), rows)
            self.copies[stage, part].append(
                self.links.start(
                    source.at[window, source_cols], target.at[hop - 1, :, cols], device
                )
            )

    def send1(self, part):
        self.arrive(0, part)
        first, count = self.parts[part]

        def body(k, carry):
            rows = pl.ds(pl.multiple_of(k * 16, 16), 16)
            mine = pl.ds(pl.multiple_of(self.base + k * 16, 16), 16)
            cols, held_cols = pl.ds(first, count), pl.ds(first + self.offset, count)
            total = self.held[mine, held_cols].astype(F32) + self.in0[rows, cols].astype(F32)
            self.held[mine, held_cols] = total.astype(BF16)
            return carry

        lax.fori_loop(0, HALF // 16, body, 0)
        self.spread(1, part, self.held, self.base, self.offset, 96, self.in1)

    def send2(self, part):
        self.arrive(1, part)
        mine = self.place.at[part % 3]
        rows = pl.ds(pl.multiple_of(self.base + mine * 96, 96), 96)
        place_row, place_col = iota((128, 96), 0), iota((128, 96), 1)
        owner = place_row >> 3
        inner = place_row & 7
        widen = jnp.where((inner < 6) & (place_col == owner * 6 + inner), 1.0, 0.0).astype(BF16)
        for first, count in self.blocks(part):
            cols = pl.ds(first, count)
            total = self.held[rows, pl.ds(first + self.offset, count)].astype(F32)
            for slot in range(3):
                total = total + self.in1[slot, :, cols].astype(F32)
            self.sum1[:, cols] = dot(widen, total.astype(BF16)).astype(BF16)
        self.spread(2, part, self.sum1, 0, 0, 32, self.in2)

    def send3(self, part):
        self.arrive(2, part)
        mine = self.place.at[(part + 1) % 3]
        rows = pl.ds(pl.multiple_of(mine * 32, 32), 32)
        for first, count in self.blocks(part):
            cols = pl.ds(first, count)
            total = self.sum1[rows, cols].astype(F32)
            for slot in range(3):
                total = total + self.in2[slot, :, cols].astype(F32)
            self.sum2[:, cols] = total
        self.spread(3, part, self.sum2, 0, 0, 8, self.in3)

    def finish(self, part):
        self.arrive(3, part)
        mine = self.place.at[(part + 2) % 3]
        rows = pl.ds(pl.multiple_of(mine * 8, 8), 8)
        for first, count in self.blocks(part):
            cols = pl.ds(first, count)
            total = self.sum2[rows, cols]
            for slot in range(3):
                total = total + self.in3[slot, :, cols]
            self.store(part, (first - self.parts[part][0]) // 512, total)


MLP_PARTS = ((3072, 1536), (0, 3072), (4608, 1536))
FIRST_PARTS = tuple((p * 512, 512) for p in range(3))
LAST_PARTS = ((0, 512), (512, 512), (1024, 640))
MLP_COLS, FIRST_COLS, LAST_COLS = 6144, 1536, 1664
PIECES = ((1, 0, 0, 512), (1, 1, 0, 512), (1, 2, 0, 512), (0, 3, 0, 512), (2, 4, 0, 512),
          (2, 5, 256, 256), (0, 5, 0, 256))
N_COPIES = 6 + 3 * 9 + 2 * 30 + 6 + 12 + 18 + 6


def landing(cols):
    return [
        pltpu.VMEM((HALF, cols), BF16),
        pltpu.VMEM((3, 96, cols), BF16),
        pltpu.VMEM((128, cols), BF16),
        pltpu.VMEM((3, 32, cols), BF16),
        pltpu.VMEM((32, cols), F32),
        pltpu.VMEM((3, 8, cols), F32),
    ]


def block_kernel(
    one_hbm, two_hbm, cot_one_hbm, cot_two_hbm, gain_ref, attn_hbm, mlp_hbm, pool_hbm,
    one_out, two_out, total_out, grad_two_out, mlp_out, attn_out, rest_out,
    *scratch,
):
    scratch = list(scratch)

    def take(count):
        taken = scratch[:count]
        del scratch[:count]
        return taken

    send_sem, recv_sem, local_sem, weight_sem = take(4)
    one_in, two_in, cot_one_in, cot_two_in, pool_in = take(5)
    up_buf, down_buf, stage = take(3)
    mlp_own, mlp_land = take(1)[0], take(6)
    first_land, last_land = take(6), take(6)
    attn, orders, pool, pad = take(4)
    normed, cot, branch = take(3)
    normed_two, query, keyval, d_att, total, lefts = take(6)
    parts, from_pair, from_edge = take(3)
    keys, values, d_keys, d_values = take(4)
    x_keys, z_keys, x_values, z_values = take(4)
    key_sum, value_sum, pair_sum, pair_land, edge_land = take(5)
    attended, d_query, extra, extra_gain = take(4)
    mlp_sums, attn_sums, rest_sums, out_sem = take(4)

    place = Place()
    links = Links(send_sem, recv_sem)
    x, y, z = place.at
    low = place.low

    sources = (one_hbm, cot_two_hbm, two_hbm, cot_one_hbm, pool_hbm, attn_hbm)
    targets = (one_in, cot_two_in, two_in, cot_one_in, pool_in, attn)
    fetches = [
        pltpu.make_async_copy(source, target, local_sem.at[k])
        for k, (source, target) in enumerate(zip(sources, targets))
    ]
    one_copy, cot_two_copy, two_copy, cot_one_copy, pool_copy, attn_copy = fetches

    def weight_copies(k):
        rows = pl.ds(k % STEPS * CHUNK, CHUNK)
        return [
            pltpu.make_async_copy(mlp_hbm.at[0, rows], up_buf.at[k % 2], weight_sem.at[0, k % 2]),
            pltpu.make_async_copy(mlp_hbm.at[1, rows], down_buf.at[k % 2], weight_sem.at[1, k % 2]),
        ]

    one_copy.start()
    cot_two_copy.start()
    for k in range(2):
        for copy in weight_copies(k):
            copy.start()
    for copy in fetches[2:]:
        copy.start()

    barrier = pltpu.get_barrier_semaphore()
    partners = [place.other_core()]
    partners += [place.pair(hop, side) for hop in (-1, 1) for side in range(2)]
    partners += [place.along(axis, hop)[0] for axis in range(3) for hop in (1, 2, 3)]
    for device in partners:
        pl.semaphore_signal(barrier, inc=1, device_id=device, device_id_type=MESH)

    writes = []

    def write(source, target):
        copy = pltpu.make_async_copy(source, target, out_sem.at[len(writes)])
        copy.start()
        writes.append(copy)

    def store_mlp(part, block, values):
        _, chunk, begin, units = [piece for piece in PIECES if piece[0] == part][block // 2]
        at = pl.ds(chunk * CHUNK + begin, units)
        if units == CHUNK:
            mlp_sums[:, block % 2, at] = values[0:6]
        else:
            for side in range(2):
                mlp_sums[:, side, at] = values[0:6, side * units : (side + 1) * units]

    def store_first(part, block, values):
        at = pl.ds(part * 256, 256)
        attn_sums[:, 0, at] = values[0:6, 0:256]
        attn_sums[:, 3, at] = values[0:6, 256:512]

    def store_last(part, block, values):
        at = pl.ds(part * 256, 256)
        attn_sums[:, 1, at] = values[0:6, 0:256]
        attn_sums[:, 2, at] = values[0:6, 256:512]
        if part == 2:
            rest_sums[...] = values[:, 512:640]

    own_base = pl.multiple_of(place.core * HALF, HALF)
    other_base = pl.multiple_of((1 - place.core) * HALF, HALF)
    mlp = Reduction(links, place, MLP_PARTS, mlp_own, 0, 0, mlp_land, store_mlp)
    first = Reduction(links, place, FIRST_PARTS, stage, own_base, 0, first_land, store_first)
    last = Reduction(links, place, LAST_PARTS, stage, own_base, FIRST_COLS, last_land, store_last)

    def kept(chunk):
        if chunk == STEPS - 1:
            return attended.at[:, pl.ds(0, CHUNK)], d_query.at[:, pl.ds(0, CHUNK)]
        at = chunk * 2 * CHUNK
        rows = pl.ds(0, ROWS)
        return mlp_own.at[rows, pl.ds(at, CHUNK)], mlp_own.at[rows, pl.ds(at + CHUNK, CHUNK)]

    def next_weights(k):
        if k + 2 < 2 * STEPS:
            for copy in weight_copies(k + 2):
                copy.start()

    for part in (1, 0, 2):
        orders[part] = permutation(part)
    one_copy.wait()
    unit, scale = norm_stats(load_padded(one_in, pad).astype(F32))
    normed[...] = (unit * gain_ref[0:1, :]).astype(BF16)
    for k in range(STEPS):
        for copy in weight_copies(k):
            copy.wait()
        hidden = dot_nt(normed[...], up_buf[k % 2])
        inner = 0.7978845608028654 * (hidden + 0.044715 * hidden * hidden * hidden)
        tanh = jnp.tanh(inner)
        half_sum = 0.5 * (1.0 + tanh)
        active = (hidden * half_sum).astype(BF16)
        slope = half_sum + 0.5 * hidden * (1.0 - tanh * tanh) * (
            0.7978845608028654 * (1.0 + 3.0 * 0.044715 * hidden * hidden)
        )
        active_at, slope_at = kept(k)
        active_at[...] = active
        slope_at[...] = slope.astype(BF16)
        if k == 0:
            branch[...] = dot(active, down_buf[k % 2])
        else:
            branch[...] += dot(active, down_buf[k % 2])
        next_weights(k)

    def back(chunk):
        k = STEPS + chunk
        for copy in weight_copies(k):
            copy.wait()
        up, down = up_buf[k % 2], down_buf[k % 2]
        active_at, slope_at = kept(chunk)
        active = active_at[...]
        d_hidden = (slope_at[...].astype(F32) * dot_nt(cot[...], down)).astype(BF16)
        if chunk == 0:
            branch[...] = dot(d_hidden, up)
        else:
            branch[...] += dot(d_hidden, up)
        next_weights(k)
        for number, (part, at_chunk, begin, units) in enumerate(PIECES):
            if at_chunk != chunk:
                continue
            if number == 0 or PIECES[number - 1][0] != part:
                lefts[0] = dot_nt(orders[part], normed[...]).astype(BF16)
                lefts[1] = dot_nt(orders[part], cot[...]).astype(BF16)
            row = 0 if number in (0, 2, 4) else HALF
            col = 2560 if number == 6 else (number // 2) * 2 * CHUNK
            first_col = MLP_PARTS[part][0]
            for piece in PIECES[:number]:
                first_col += 2 * piece[3] if piece[0] == part else 0
            for side, values_in in enumerate((d_hidden, active)):
                values_in = values_in[:, begin : begin + units]
                stage[pl.ds(row, HALF), pl.ds(col + side * units, units)] = dot(
                    lefts[side, pl.ds(other_base, HALF)], values_in
                ).astype(BF16)
                mlp_own[:, pl.ds(first_col + side * units, units)] = dot(
                    lefts[side, pl.ds(own_base, HALF)], values_in
                ).astype(BF16)
            mlp.copies.setdefault((0, part), []).append(
                links.start(
                    stage.at[pl.ds(row, HALF), pl.ds(col, 2 * units)],
                    mlp.in0.at[:, pl.ds(first_col, 2 * units)],
                    place.other_core(),
                )
            )

    two_copy.wait()
    restored = (load_padded(two_in, pad).astype(F32) - branch[...]).astype(BF16)
    store_grid(two_in, restored)
    write(two_in, two_out)
    unit_two, scale_two = norm_stats(restored.astype(F32))
    normed_two[...] = (unit_two * gain_ref[1:2, :]).astype(BF16)
    attn_copy.wait()
    keyval[:, 0:D] = dot(normed_two[...], attn[1]).astype(BF16)
    keyval[:, D:] = dot(normed_two[...], attn[2]).astype(BF16)
    cells, blocks = cell_maps()
    pool_copy.wait()
    for offset in range(3):
        for i in range(4):
            pool[offset, 4 * i : 4 * i + 4, :] = pool_in[offset, i]
        weighted = spread_kernel(cells, pool[offset]) * keyval[...].astype(F32)
        parts[2 - offset] = gather_rows(blocks, weighted).astype(BF16)

    mine = pl.ds(1 - low, 2)
    pl.semaphore_wait(barrier, len(partners))
    pair_copy = links.start(parts.at[mine], from_pair, place.pair(0, 1 - low))
    edge_base = links.used
    for side in range(2):
        links.start(
            parts.at[2 * low], from_edge.at[1 - low],
            (place.clip, (place.tm - low + 4 * low - 2 + 32) % 32 + side),
            shift=1 - low if side == 0 else -low, slots=1,
        )
    query[...] = dot(normed_two[...], attn[0]).astype(BF16)
    cot_two_copy.wait()
    cot[...] = load_padded(cot_two_in, pad)
    back(0)
    pair_copy.wait_recv()
    for slot in range(2):
        links.arrival(from_edge.at[slot], edge_base + slot)
    ends = (place.tm // 2 > 0, place.tm // 2 < 15)
    for slot in range(2):
        edge = jnp.where(ends[slot], from_edge[slot].astype(F32), 0.0)
        frame = parts[1 - low + slot].astype(F32) + from_pair[slot].astype(F32) + edge
        frame = frame.astype(BF16)
        keys[x, z, 16 * slot : 16 * slot + 16, :] = frame[:, 0:D]
        values[x, z, 16 * slot : 16 * slot + 16, :] = frame[:, D:]

    copies = []
    for hop in (2, 1, 3):
        copies.append(links.start(keys.at[x, z], keys.at[x, z], place.along(2, hop)[0]))
        copies.append(links.start(values.at[x, z], values.at[x, z], place.along(0, hop)[0]))
    back(1)
    for copy in copies:
        copy.wait_recv()
    copies = []
    for hop in (2, 1, 3):
        copies.append(links.start(keys.at[x], keys.at[x], place.along(0, hop)[0]))
        copies.append(links.start(values.at[:, z], values.at[:, z], place.along(2, hop)[0]))
    for chunk in range(2, STEPS):
        back(chunk)
        if chunk == 3:
            mlp.send1(1)
    unit, scale = norm_stats(load_padded(one_in, pad).astype(F32))
    d_gain_one = jnp.sum(branch[...] * unit, axis=0, keepdims=True)
    d_first = norm_back(unit, scale, gain_ref[0:1, :], branch[...])
    cot_one_copy.wait()
    total[...] = (load_padded(cot_one_in, pad).astype(F32) + d_first).astype(BF16)
    store_grid(cot_one_in, total[...])
    write(cot_one_in, total_out)
    d_att[...] = dot_nt(total[...], attn[3]).astype(BF16)
    for part in range(3):
        lefts[part] = dot_nt(orders[part], total[...]).astype(BF16)
    for copy in copies:
        copy.wait_recv()
    mlp.send1(0)
    mlp.send1(2)

    def heads(pair, carry):
        lanes = pl.ds(pl.multiple_of(pair * 128, 128), 128)
        query_pair = query[:, lanes]
        d_att_pair = d_att[:, lanes]
        key = keys[:, :, :, lanes].reshape(512, 128)
        value = values[:, :, :, lanes].reshape(512, 128)
        att = d_q = d_k = d_v = None
        for side in range(2):

            def only(array):
                lane = iota(array.shape, 1)
                keep = lane < 64 if side == 0 else lane >= 64
                return jnp.where(keep, array, jnp.zeros_like(array))

            query_h, d_att_h = only(query_pair), only(d_att_pair)
            weights = jnp.exp(dot_nt(query_h, key) * 0.125)
            probs = weights * (1.0 / jnp.sum(weights, axis=-1, keepdims=True))
            probs_b = probs.astype(BF16)
            d_probs = dot_nt(d_att_h, value)
            product = probs * d_probs
            d_scores = (product - probs * jnp.sum(product, axis=-1, keepdims=True)).astype(BF16)
            terms = (
                dot(probs_b, only(value)), dot(d_scores, only(key)),
                dot_tn(d_scores, query_h), dot_tn(probs_b, d_att_h),
            )
            if side == 0:
                att, d_q, d_k, d_v = terms
            else:
                att, d_q, d_k, d_v = (a + b for a, b in zip((att, d_q, d_k, d_v), terms))
        attended[:, lanes] = att.astype(BF16)
        d_query[:, lanes] = (d_q * 0.125).astype(BF16)
        d_keys[:, :, :, lanes] = (d_k * 0.125).astype(BF16).reshape(4, 4, 32, 128)
        d_values[:, :, :, lanes] = d_v.astype(BF16).reshape(4, 4, 32, 128)
        return carry

    copies = []
    for group in range(2):
        lax.fori_loop(3 * group, 3 * group + 3, heads, 0)
        lanes = pl.ds(group * HALF, HALF)
        for hop in (2, 1, 3):
            device, at = place.along(0, hop)
            copies.append(
                links.start(d_keys.at[at, :, :, lanes], x_keys.at[hop - 1, :, :, lanes], device)
            )
            device, at = place.along(2, hop)
            copies.append(
                links.start(d_values.at[:, at, :, lanes], z_values.at[hop - 1, :, :, lanes], device)
            )

    for part in range(3):
        for copy in mlp.copies[0, part]:
            links.sent(copy)
    branch_f = dot(attended[...], attn[3])
    store_grid(one_in, (load_padded(one_in, pad).astype(F32) - branch_f).astype(BF16))
    write(one_in, one_out)
    for part in range(3):
        inside = pl.ds(part * 256, 256)
        lhs = dot_nt(orders[part], d_query[...]).astype(BF16)
        stage[:, pl.ds(part * 512, 256)] = dot(lhs, normed_two[:, inside]).astype(BF16)
        stage[:, pl.ds(part * 512 + 256, 256)] = dot(
            lefts[part], attended[:, inside]
        ).astype(BF16)
        first.send0(part)
    branch[...] = dot_nt(d_query[...], attn[0])

    for copy in copies:
        copy.wait_recv()
    sum_k = d_keys[x].astype(F32)
    sum_v = d_values[:, z].astype(F32)
    for slot in range(3):
        sum_k = sum_k + x_keys[slot].astype(F32)
        sum_v = sum_v + z_values[slot].astype(F32)
    key_sum[...] = sum_k.astype(BF16)
    value_sum[...] = sum_v.astype(BF16)
    copies = []
    for hop in (2, 1, 3):
        device, at = place.along(2, hop)
        copies.append(links.start(key_sum.at[at], z_keys.at[hop - 1], device))
        device, at = place.along(0, hop)
        copies.append(links.start(value_sum.at[at], x_values.at[hop - 1], device))
    mlp.send2(0)
    mlp.send2(2)
    for copy in copies:
        copy.wait_recv()
    sum_k = key_sum[z].astype(F32)
    sum_v = value_sum[x].astype(F32)
    for slot in range(3):
        sum_k = sum_k + z_keys[slot].astype(F32)
        sum_v = sum_v + x_values[slot].astype(F32)
    pair_sum[:, 0:D] = sum_k.astype(BF16)
    pair_sum[:, D:] = sum_v.astype(BF16)

    pair_copy = links.start(pair_sum, pair_land, place.pair(0, 1 - low))
    edge_base = links.used
    for hop, rows in ((-1, pl.ds(0, 16)), (1, pl.ds(16, 16))):
        side = 1 if hop == -1 else 0
        links.start(
            pair_sum.at[rows, :], edge_land.at[low], place.pair(hop, side),
            shift=low if hop == -1 else low - 1, slots=1,
        )
    for part in range(3):
        first.send1(part)
    mlp.send2(1)
    pair_copy.wait_recv()
    for slot in range(2):
        links.arrival(edge_land.at[slot], edge_base + slot)
    edge = edge_land[0].astype(F32) + edge_land[1].astype(F32)
    inside = (low == 0) & (place.tm > 0) | (low == 1) & (place.tm < 31)
    edge = jnp.where(inside, edge, 0.0).astype(BF16)
    pair_frames = (pair_sum[...].astype(F32) + pair_land[...].astype(F32)).astype(BF16)
    frame_0, frame_1 = pair_frames[0:16, :], pair_frames[16:32, :]
    before = jnp.where(low == 0, edge, frame_0)
    here = jnp.where(low == 0, frame_0, frame_1)
    after = jnp.where(low == 0, frame_1, edge)

    cells, blocks = cell_maps()
    keyval_f = keyval[...].astype(F32)
    d_keyval = None
    extra[...] = jnp.zeros(extra.shape, BF16)
    for offset, source in enumerate((after, here, before)):
        expanded = dot(blocks, source)
        term = spread_kernel(cells, pool[offset]) * expanded
        d_keyval = term if d_keyval is None else d_keyval + term
        d_kernel = gather_rows(cells[:, 0:16], keyval_f * expanded).astype(BF16)
        extra[0, 16 * offset : 16 * offset + 16, :] = d_kernel
        extra[1, 48 + 16 * offset : 64 + 16 * offset, :] = d_kernel
    d_keyval = d_keyval.astype(BF16)
    d_key_proj, d_value_proj = d_keyval[:, 0:D], d_keyval[:, D:]

    def last_part(part):
        inside = pl.ds(part * 256, 256)
        start = FIRST_COLS + part * 512
        lhs = dot_nt(orders[part], d_key_proj).astype(BF16)
        stage[:, pl.ds(start, 256)] = dot(lhs, normed_two[:, inside]).astype(BF16)
        lhs = dot_nt(orders[part], d_value_proj).astype(BF16)
        stage[:, pl.ds(start + 256, 256)] = dot(lhs, normed_two[:, inside]).astype(BF16)

    for part in range(2):
        last_part(part)
        last.send0(part)
    last_part(2)
    d_normed_two = branch[...] + dot_nt(d_key_proj, attn[1]) + dot_nt(d_value_proj, attn[2])
    d_second = norm_back(unit_two, scale_two, gain_ref[1:2, :], d_normed_two)
    extra_gain[...] = jnp.zeros(extra_gain.shape, F32)
    extra_gain[96:97, :] = d_gain_one
    extra_gain[97:98, :] = jnp.sum(d_normed_two * unit_two, axis=0, keepdims=True)
    source = source_column(iota((D, 128), 0), 2)
    lanes = iota((D, 128), 1)
    block = dot_nt(orders[2], extra_gain[...].astype(BF16))
    for k in range(KV // 128):
        for side in range(2):
            pick = jnp.where(2 * source + side == lanes + 128 * k, 1.0, 0.0).astype(BF16)
            block = block + dot_nt(pick, extra[side, :, k * 128 : (k + 1) * 128])
    stage[:, pl.ds(FIRST_COLS + 1536, 128)] = block.astype(BF16)
    last.send0(2)
    result = load_padded(cot_two_in, pad).astype(F32) + d_second
    store_grid(cot_two_in, result.astype(BF16))
    write(cot_two_in, grad_two_out)

    for part in range(3):
        first.send2(part)
    for part in range(3):
        last.send1(part)
    for part in range(3):
        mlp.send3(part)
    for part in range(3):
        first.send3(part)
    for part in range(3):
        last.send2(part)
    for part in range(3):
        mlp.finish(part)
    write(mlp_sums, mlp_out)
    for part in range(3):
        last.send3(part)
    for part in range(3):
        first.finish(part)
    for part in range(3):
        last.finish(part)
    write(attn_sums, attn_out)
    write(rest_sums, rest_out)
    for copy in links.started:
        copy.wait_send()
    for copy in writes:
        copy.wait()


def run_block(half_one, half_two, grad_one, grad_two, norm_gain, attn_weight, mlp_weight, pool_kernel):
    vmem = pl.BlockSpec(memory_space=pltpu.VMEM)
    hbm = pl.BlockSpec(memory_space=pl.ANY)
    shape = jax.ShapeDtypeStruct
    scratch = [
        pltpu.SemaphoreType.DMA((N_COPIES,)),
        pltpu.SemaphoreType.DMA((N_COPIES,)),
        pltpu.SemaphoreType.DMA((6,)),
        pltpu.SemaphoreType.DMA((2, 2)),
        *[pltpu.VMEM((1, 1, 14, 14, D), BF16) for _ in range(4)],
        pltpu.VMEM((3, 4, 4, KV), F32),
        pltpu.VMEM((2, CHUNK, D), BF16),
        pltpu.VMEM((2, CHUNK, D), BF16),
        pltpu.VMEM((D, FIRST_COLS + LAST_COLS), BF16),
        pltpu.VMEM((HALF, MLP_COLS), BF16), *landing(MLP_COLS),
        *landing(FIRST_COLS),
        *landing(LAST_COLS),
        pltpu.VMEM((4, D, D), BF16),
        pltpu.VMEM((3, D, D), BF16),
        pltpu.VMEM((3, 16, KV), F32),
        pltpu.VMEM((14, 16, D), BF16),
        pltpu.VMEM((ROWS, D), BF16),
        pltpu.VMEM((ROWS, D), BF16),
        pltpu.VMEM((ROWS, D), F32),
        pltpu.VMEM((ROWS, D), BF16),
        pltpu.VMEM((ROWS, D), BF16),
        pltpu.VMEM((ROWS, KV), BF16),
        pltpu.VMEM((ROWS, D), BF16),
        pltpu.VMEM((ROWS, D), BF16),
        pltpu.VMEM((3, D, ROWS), BF16),
        pltpu.VMEM((3, 16, KV), BF16),
        pltpu.VMEM((2, 16, KV), BF16),
        pltpu.VMEM((2, 16, KV), BF16),
        *[pltpu.VMEM((4, 4, 32, D), BF16) for _ in range(4)],
        pltpu.VMEM((3, 4, 32, D), BF16),
        pltpu.VMEM((3, 32, D), BF16),
        pltpu.VMEM((3, 32, D), BF16),
        pltpu.VMEM((3, 4, 32, D), BF16),
        pltpu.VMEM((4, 32, D), BF16),
        pltpu.VMEM((4, 32, D), BF16),
        pltpu.VMEM((32, KV), BF16),
        pltpu.VMEM((32, KV), BF16),
        pltpu.VMEM((2, 16, KV), BF16),
        pltpu.VMEM((ROWS, D), BF16),
        pltpu.VMEM((ROWS, D), BF16),
        pltpu.VMEM((2, 128, KV), BF16),
        pltpu.VMEM((128, D), F32),
        pltpu.VMEM((6, 2, FF), F32),
        pltpu.VMEM((6, 4, D), F32),
        pltpu.VMEM((8, 128), F32),
        pltpu.SemaphoreType.DMA((7,)),
    ]
    return pl.pallas_call(
        block_kernel,
        in_specs=[hbm, hbm, hbm, hbm, vmem, hbm, hbm, hbm],
        out_specs=[hbm] * 7,
        out_shape=[
            *[shape(half_one.shape, BF16) for _ in range(4)],
            shape((6, 2, FF), F32), shape((6, 4, D), F32), shape((8, 128), F32),
        ],
        scratch_shapes=scratch,
        compiler_params=pltpu.CompilerParams(
            collective_id=0, has_side_effects=True, vmem_limit_bytes=63 * MIB
        ),
        name="reversible_block",
    )(half_one, half_two, grad_one, grad_two, norm_gain, attn_weight, mlp_weight, pool_kernel)


def hand_out_kernel(*refs):
    taken, rest_ref, given, kernel_out, gain_out = refs[0:6], refs[6], refs[7:13], *refs[13:15]
    held, in_sem, out_sem = refs[15:21], *refs[21:]
    loads = [
        pltpu.make_async_copy(source, target, in_sem.at[k])
        for k, (source, target) in enumerate(zip(taken, held))
    ]
    copies = [
        pltpu.make_async_copy(source, target, out_sem.at[k])
        for k, (source, target) in enumerate(zip(held, given))
    ]
    for load in loads:
        load.start()
    for load, copy in zip(loads, copies):
        load.wait()
        copy.start()
    rest = rest_ref[...]

    def columns(width, step, side):
        row, lane = iota((8, width), 0), iota((8, width), 1)
        pick = jnp.where((row < 6) & (lane == step * row + side), 1.0, 0.0)
        return lax.dot_general(
            rest, pick, (((0,), (0,)), ((), ())),
            precision=lax.Precision.HIGHEST, preferred_element_type=F32,
        )

    kernel_grad = columns(12, 2, 0)[0:48] + columns(12, 2, 1)[48:96]
    for offset in range(3):
        for i in range(4):
            at = 16 * offset + 4 * i
            kernel_out[offset, i] = kernel_grad[at : at + 4]
    gain_out[...] = columns(6, 1, 0)[96:98]
    for copy in copies:
        copy.wait()


def hand_out(results, rest):
    vmem = pl.BlockSpec(memory_space=pltpu.VMEM)
    hbm = pl.BlockSpec(memory_space=pl.ANY)
    shape = jax.ShapeDtypeStruct
    return pl.pallas_call(
        hand_out_kernel,
        in_specs=[hbm] * 6 + [vmem],
        out_specs=[hbm] * 6 + [vmem] * 2,
        out_shape=[shape(array.shape, array.dtype) for array in results]
        + [shape((3, 4, 4, 12), F32), shape((2, 6), F32)],
        scratch_shapes=[pltpu.VMEM(array.shape, array.dtype) for array in results]
        + [pltpu.SemaphoreType.DMA((6,)), pltpu.SemaphoreType.DMA((6,))],
        compiler_params=pltpu.CompilerParams(vmem_limit_bytes=62 * MIB),
        name="hand_out",
    )(*results, rest)


def shards(half_one, half_two, grad_one, grad_two, norm_gain, attn_weight, mlp_weight, pool_kernel):
    *results, rest = run_block(
        half_one, half_two, grad_one, grad_two, norm_gain, attn_weight, mlp_weight, pool_kernel
    )
    (input_one, input_two, total, input_grad_two, mlp_sums, attn_sums, kernel_grad, gain_grad) = (
        hand_out(results, rest)
    )
    mlp_grad = mlp_sums.transpose(1, 2, 0)
    attn_grad = attn_sums.transpose(1, 2, 0)
    return (input_one, input_two, total, input_grad_two, attn_grad, mlp_grad, kernel_grad, gain_grad)


def solution(mesh):
    placed = (
        P("clip", "tm", None, None, None),
        P("clip", "tm", None, None, None),
        P("clip", "tm", None, None, None),
        P("clip", "tm", None, None, None),
        P(),
        P(),
        P(),
        P(),
    )
    return jax.shard_map(
        shards,
        mesh=mesh,
        in_specs=placed,
        out_specs=(
            P("clip", "tm", None, None, None),
            P("clip", "tm", None, None, None),
            P("clip", "tm", None, None, None),
            P("clip", "tm", None, None, None),
            P(None, None, ("clip", "tm")),
            P(None, None, ("clip", "tm")),
            P(None, None, None, ("clip", "tm")),
            P(None, ("clip", "tm")),
        ),
        check_vma=False,
    )
```

```python
from functools import partial

import jax
import jax.numpy as jnp
from jax import lax
from jax.experimental import pallas as pl
from jax.experimental.pallas import tpu as pltpu
from jax.sharding import PartitionSpec as P

D = 768
FF = 3072
KV = 2 * D
ROWS = 224
CHUNK = 512
STEPS = FF // CHUNK
HALF = 384
MIB = 1024 * 1024
F32 = jnp.float32
BF16 = jnp.bfloat16
MESH = pl.DeviceIdType.MESH


def dot(a, b):
    return lax.dot_general(a, b, (((1,), (0,)), ((), ())), preferred_element_type=F32)


def dot_nt(a, b):
    return lax.dot_general(a, b, (((1,), (1,)), ((), ())), preferred_element_type=F32)


def dot_tn(a, b):
    return lax.dot_general(a, b, (((0,), (0,)), ((), ())), preferred_element_type=F32)


def iota(shape, dim):
    return lax.broadcasted_iota(jnp.int32, shape, dim)


def source_column(rows, axes):
    owner_at = (rows * 43691) >> 18
    inner = rows - owner_at * 6
    core = owner_at >> 6
    digits = ((owner_at >> 4) & 3, (owner_at >> 2) & 3, owner_at & 3)
    x, y, z = (digits[axes.index(axis)] for axis in range(3))
    owner = (y >> 1) * 64 + core * 32 + x * 8 + z * 2 + (y & 1)
    return owner * 6 + inner


def permutation(axes):
    source = source_column(iota((D, 128), 0), axes)
    lanes = iota((D, 128), 1)
    pieces = [
        jnp.where(source == lanes + 128 * k, 1.0, 0.0).astype(BF16) for k in range(D // 128)
    ]
    return jnp.concatenate(pieces, axis=1)


def norm_stats(values):
    centre = jnp.mean(values, axis=-1, keepdims=True)
    centred = values - centre
    spread = jnp.mean(centred * centred, axis=-1, keepdims=True)
    scale = lax.rsqrt(spread + 1e-05)
    return centred * scale, scale


def norm_back(unit, scale, gain, cotangent):
    d_unit = cotangent * gain
    first = jnp.mean(d_unit, axis=-1, keepdims=True)
    second = jnp.mean(d_unit * unit, axis=-1, keepdims=True)
    return scale * (d_unit - first - unit * second)


def load_padded(ref, pad):
    pad[...] = jnp.zeros(pad.shape, pad.dtype)
    pad[:, 0:14, :] = ref[0, 0]
    return pad[...].reshape(ROWS, D)


def store_grid(ref, values):
    ref[0, 0] = values.reshape(14, 16, D)[:, 0:14, :]


def cell_maps():
    row = iota((ROWS, 48), 0)
    across, down = (row & 15) + 1, (row >> 4) + 1
    valid = across < 15
    cell = (down & 3) * 4 + (across & 3)
    lane = iota((ROWS, 48), 1)
    cells = jnp.where(valid & ((lane & 15) == cell), 1.0, 0.0).astype(BF16)
    row = iota((ROWS, 16), 0)
    across, down = (row & 15) + 1, (row >> 4) + 1
    block = (down >> 2) * 4 + (across >> 2)
    blocks = jnp.where((across < 15) & (iota((ROWS, 16), 1) == block), 1.0, 0.0).astype(BF16)
    return cells, blocks


def spread_kernel(cells, flat):
    high = flat.astype(BF16)
    rest = flat - high.astype(F32)
    middle = rest.astype(BF16)
    low = (rest - middle.astype(F32)).astype(BF16)
    return dot(cells, jnp.concatenate([high, middle, low], axis=0))


def gather_rows(one_hot, values):
    return dot_tn(one_hot, values.astype(BF16))


class Links:
    def __init__(self, send, recv):
        self.send, self.recv, self.used, self.started = send, recv, 0, []

    def start(self, source, target, device, shift=0, slots=1):
        copy = pltpu.make_async_remote_copy(
            src_ref=source, dst_ref=target,
            send_sem=self.send.at[self.used], recv_sem=self.recv.at[self.used + shift],
            device_id=device, device_id_type=MESH,
        )
        self.used += slots
        copy.start()
        self.started.append(copy)
        return copy

    def arrival(self, target, number):
        pltpu.make_async_remote_copy(
            src_ref=target, dst_ref=target,
            send_sem=self.send.at[number], recv_sem=self.recv.at[number],
            device_id=(lax.axis_index("clip"), lax.axis_index("tm")), device_id_type=MESH,
        ).wait_recv()

    def sent(self, copy):
        copy.wait_send()
        self.started = [other for other in self.started if other is not copy]


class Place:
    def __init__(self):
        clip, tm = lax.axis_index("clip"), lax.axis_index("tm")
        self.tm, self.clip = tm, clip
        self.core, high = clip % 2, clip // 2
        self.low = tm % 2
        self.at = (tm // 8, high * 2 + self.low, (tm // 2) % 4)

    def device(self, core, at):
        x, y, z = at
        return ((y // 2) * 2 + core, x * 8 + z * 2 + y % 2)

    def other_core(self):
        return self.device(1 - self.core, self.at)

    def along(self, axis, hop):
        at = list(self.at)
        at[axis] = (at[axis] + hop) % 4
        return self.device(self.core, at), at[axis]

    def pair(self, hop, low):
        return (self.clip, (self.tm - self.low + 2 * hop + 32) % 32 + low)


class Reduction:
    def __init__(self, links, place, parts, orders, held, base, offset, landed, store):
        self.links, self.place, self.parts = links, place, parts
        self.axes = [ORDERS[order] for order in orders]
        self.held, self.base, self.offset = held, base, offset
        self.in0, self.in1, self.sum1, self.in2, self.sum2, self.in3 = landed
        self.store = store
        self.copies = {}

    def columns(self, part, offset=0):
        return pl.ds(self.parts[part][0] + offset, self.parts[part][1])

    def blocks(self, part, width=512):
        first, count = self.parts[part]
        if count % width:
            width = count
        return [(first + k * width, width) for k in range(count // width)]

    def send0(self, part):
        cols = self.columns(part)
        rows = pl.ds(pl.multiple_of((1 - self.place.core) * HALF, HALF), HALF)
        self.copies[0, part] = [
            self.links.start(
                self.held.at[rows, self.columns(part, self.offset)], self.in0.at[:, cols],
                self.place.other_core(),
            )
        ]

    def arrive(self, stage, part):
        for copy in self.copies[stage, part]:
            copy.wait_recv()

    def spread(self, stage, part, source, base, offset, rows, target):
        axis = self.axes[part][stage - 1]
        cols = self.columns(part)
        source_cols = self.columns(part, offset)
        self.copies[stage, part] = []
        for hop in (2, 1, 3):
            device, at = self.place.along(axis, hop)
            window = pl.ds(pl.multiple_of(base + at * rows, rows), rows)
            self.copies[stage, part].append(
                self.links.start(
                    source.at[window, source_cols], target.at[hop - 1, :, cols], device
                )
            )

    def send1(self, part):
        self.arrive(0, part)
        first, count = self.parts[part]

        def body(k, carry):
            rows = pl.ds(pl.multiple_of(k * 16, 16), 16)
            mine = pl.ds(pl.multiple_of(self.base + k * 16, 16), 16)
            cols, held_cols = pl.ds(first, count), pl.ds(first + self.offset, count)
            total = self.held[mine, held_cols].astype(F32) + self.in0[rows, cols].astype(F32)
            self.held[mine, held_cols] = total.astype(BF16)
            return carry

        lax.fori_loop(0, HALF // 16, body, 0)
        self.spread(1, part, self.held, self.base, self.offset, 96, self.in1)

    def send2(self, part):
        self.arrive(1, part)
        mine = self.place.at[self.axes[part][0]]
        rows = pl.ds(pl.multiple_of(self.base + mine * 96, 96), 96)
        place_row, place_col = iota((128, 96), 0), iota((128, 96), 1)
        owner = place_row >> 3
        inner = place_row & 7
        widen = jnp.where((inner < 6) & (place_col == owner * 6 + inner), 1.0, 0.0).astype(BF16)
        for first, count in self.blocks(part):
            cols = pl.ds(first, count)
            total = self.held[rows, pl.ds(first + self.offset, count)].astype(F32)
            for slot in range(3):
                total = total + self.in1[slot, :, cols].astype(F32)
            self.sum1[:, cols] = dot(widen, total.astype(BF16)).astype(BF16)
        self.spread(2, part, self.sum1, 0, 0, 32, self.in2)

    def send3(self, part):
        self.arrive(2, part)
        mine = self.place.at[self.axes[part][1]]
        rows = pl.ds(pl.multiple_of(mine * 32, 32), 32)
        for first, count in self.blocks(part):
            cols = pl.ds(first, count)
            total = self.sum1[rows, cols].astype(F32)
            for slot in range(3):
                total = total + self.in2[slot, :, cols].astype(F32)
            self.sum2[:, cols] = total
        self.spread(3, part, self.sum2, 0, 0, 8, self.in3)

    def finish(self, part):
        self.arrive(3, part)
        mine = self.place.at[self.axes[part][2]]
        rows = pl.ds(pl.multiple_of(mine * 8, 8), 8)
        for first, count in self.blocks(part):
            cols = pl.ds(first, count)
            total = self.sum2[rows, cols]
            for slot in range(3):
                total = total + self.in3[slot, :, cols]
            self.store(part, (first - self.parts[part][0]) // 512, total)


ORDERS = ((0, 1, 2), (1, 2, 0), (2, 0, 1), (1, 0, 2))
MLP_ORDERS = (1, 1, 3, 3, 0, 2)
MLP_PARTS = tuple((k * 1024, 1024) for k in range(STEPS))
FIRST_PARTS = tuple((p * 512, 512) for p in range(3))
LAST_PARTS = ((0, 512), (512, 512), (1024, 640))
MLP_COLS, FIRST_COLS, LAST_COLS = 6144, 1536, 1664
N_COPIES = 6 * 10 + 2 * 30 + 3 + 12 + 24 + 3


def landing(cols):
    return [
        pltpu.VMEM((HALF, cols), BF16),
        pltpu.VMEM((3, 96, cols), BF16),
        pltpu.VMEM((128, cols), BF16),
        pltpu.VMEM((3, 32, cols), BF16),
        pltpu.VMEM((32, cols), F32),
        pltpu.VMEM((3, 8, cols), F32),
    ]


def block_kernel(
    one_hbm, two_hbm, cot_one_hbm, cot_two_hbm, gain_ref, attn_hbm, mlp_hbm, pool_hbm,
    one_out, two_out, total_out, grad_two_out, mlp_out, attn_out, rest_out,
    *scratch,
):
    scratch = list(scratch)

    def take(count):
        taken = scratch[:count]
        del scratch[:count]
        return taken

    send_sem, recv_sem, local_sem, weight_sem = take(4)
    one_in, two_in, cot_one_in, cot_two_in, pool_in = take(5)
    up_buf, down_buf, stage = take(3)
    mlp_own, mlp_land = take(1)[0], take(6)
    first_land, last_land = take(6), take(6)
    attn, orders, pool, pad = take(4)
    normed, cot, branch = take(3)
    normed_two, query, keyval, d_att, total, lefts = take(6)
    parts, from_pair, from_edge = take(3)
    keys, values, d_keys, d_values = take(4)
    x_keys, z_keys, x_values, z_values = take(4)
    key_sum, value_sum, pair_sum, pair_land, edge_land = take(5)
    attended, d_query, extra, extra_gain = take(4)
    mlp_sums, attn_sums, rest_sums, out_sem = take(4)

    place = Place()
    links = Links(send_sem, recv_sem)
    x, y, z = place.at
    low = place.low

    sources = (one_hbm, cot_two_hbm, two_hbm, cot_one_hbm, pool_hbm, attn_hbm)
    targets = (one_in, cot_two_in, two_in, cot_one_in, pool_in, attn)
    fetches = [
        pltpu.make_async_copy(source, target, local_sem.at[k])
        for k, (source, target) in enumerate(zip(sources, targets))
    ]
    one_copy, cot_two_copy, two_copy, cot_one_copy, pool_copy, attn_copy = fetches

    def weight_copies(k):
        rows = pl.ds(k % STEPS * CHUNK, CHUNK)
        return [
            pltpu.make_async_copy(mlp_hbm.at[0, rows], up_buf.at[k % 3], weight_sem.at[0, k % 3]),
            pltpu.make_async_copy(mlp_hbm.at[1, rows], down_buf.at[k % 3], weight_sem.at[1, k % 3]),
        ]

    one_copy.start()
    for k in range(3):
        for copy in weight_copies(k):
            copy.start()

    barrier = pltpu.get_barrier_semaphore()
    partners = [place.other_core()]
    partners += [place.pair(hop, side) for hop in (-1, 1) for side in range(2)]
    partners += [place.along(axis, hop)[0] for axis in range(3) for hop in (1, 2, 3)]
    for device in partners:
        pl.semaphore_signal(barrier, inc=1, device_id=device, device_id_type=MESH)

    writes = []

    def write(source, target):
        copy = pltpu.make_async_copy(source, target, out_sem.at[len(writes)])
        copy.start()
        writes.append(copy)

    def store_mlp(part, block, values):
        mlp_sums[:, block, pl.ds(part * CHUNK, CHUNK)] = values[0:6]

    def store_first(part, block, values):
        at = pl.ds(part * 256, 256)
        attn_sums[:, 0, at] = values[0:6, 0:256]
        attn_sums[:, 3, at] = values[0:6, 256:512]

    def store_last(part, block, values):
        at = pl.ds(part * 256, 256)
        attn_sums[:, 1, at] = values[0:6, 0:256]
        attn_sums[:, 2, at] = values[0:6, 256:512]
        if part == 2:
            rest_sums[...] = values[:, 512:640]

    own_base = pl.multiple_of(place.core * HALF, HALF)
    other_base = pl.multiple_of((1 - place.core) * HALF, HALF)
    mlp = Reduction(links, place, MLP_PARTS, MLP_ORDERS, mlp_own, 0, 0, mlp_land, store_mlp)
    first = Reduction(links, place, FIRST_PARTS, (0, 1, 2), stage, own_base, 0, first_land, store_first)
    last = Reduction(links, place, LAST_PARTS, (0, 1, 2), stage, own_base, FIRST_COLS, last_land, store_last)

    def kept(chunk):
        at = chunk * 2 * CHUNK
        rows = pl.ds(0, ROWS)
        return mlp_own.at[rows, pl.ds(at, CHUNK)], mlp_own.at[rows, pl.ds(at + CHUNK, CHUNK)]

    def next_weights(k):
        if k + 3 < 2 * STEPS:
            for copy in weight_copies(k + 3):
                copy.start()

    for k, axes in enumerate(ORDERS):
        orders[k] = permutation(axes)
    one_copy.wait()
    unit, scale = norm_stats(load_padded(one_in, pad).astype(F32))
    normed[...] = (unit * gain_ref[0:1, :]).astype(BF16)
    for k in range(STEPS):
        for copy in weight_copies(k):
            copy.wait()
        hidden = dot_nt(normed[...], up_buf[k % 3])
        inner = 0.7978845608028654 * (hidden + 0.044715 * hidden * hidden * hidden)
        tanh = jnp.tanh(inner)
        half_sum = 0.5 * (1.0 + tanh)
        active = (hidden * half_sum).astype(BF16)
        slope = half_sum + 0.5 * hidden * (1.0 - tanh * tanh) * (
            0.7978845608028654 * (1.0 + 3.0 * 0.044715 * hidden * hidden)
        )
        active_at, slope_at = kept(k)
        active_at[...] = active
        slope_at[...] = slope.astype(BF16)
        if k == 0:
            branch[...] = dot(active, down_buf[k % 3])
        else:
            branch[...] += dot(active, down_buf[k % 3])
        next_weights(k)
        if k == 2:
            two_copy.start()
            pool_copy.start()
            attn_copy.start()
            cot_two_copy.start()
            cot_one_copy.start()

    def back(chunk):
        k = STEPS + chunk
        for copy in weight_copies(k):
            copy.wait()
        up, down = up_buf[k % 3], down_buf[k % 3]
        active_at, slope_at = kept(chunk)
        active = active_at[...]
        d_hidden = (slope_at[...].astype(F32) * dot_nt(cot[...], down)).astype(BF16)
        if chunk == 0:
            branch[...] = dot(d_hidden, up)
        else:
            branch[...] += dot(d_hidden, up)
        next_weights(k)
        order = MLP_ORDERS[chunk]
        if chunk == 0 or MLP_ORDERS[chunk - 1] != order:
            lefts[0] = dot_nt(orders[order], normed[...]).astype(BF16)
            lefts[1] = dot_nt(orders[order], cot[...]).astype(BF16)
        row = chunk % 2 * HALF
        col = chunk // 2 * 2 * CHUNK
        first_col = chunk * 2 * CHUNK
        for side, values_in in enumerate((d_hidden, active)):
            stage[pl.ds(row, HALF), pl.ds(col + side * CHUNK, CHUNK)] = dot(
                lefts[side, pl.ds(other_base, HALF)], values_in
            ).astype(BF16)
        mlp.copies[0, chunk] = [
            links.start(
                stage.at[pl.ds(row, HALF), pl.ds(col, 2 * CHUNK)],
                mlp.in0.at[:, pl.ds(first_col, 2 * CHUNK)],
                place.other_core(),
            )
        ]
        for side, values_in in enumerate((d_hidden, active)):
            mlp_own[:, pl.ds(first_col + side * CHUNK, CHUNK)] = dot(
                lefts[side, pl.ds(own_base, HALF)], values_in
            ).astype(BF16)

    two_copy.wait()
    restored = (load_padded(two_in, pad).astype(F32) - branch[...]).astype(BF16)
    store_grid(two_in, restored)
    write(two_in, two_out)
    unit_two, scale_two = norm_stats(restored.astype(F32))
    normed_two[...] = (unit_two * gain_ref[1:2, :]).astype(BF16)
    attn_copy.wait()
    keyval[:, 0:D] = dot(normed_two[...], attn[1]).astype(BF16)
    keyval[:, D:] = dot(normed_two[...], attn[2]).astype(BF16)
    cells, blocks = cell_maps()
    pool_copy.wait()
    for offset in range(3):
        for i in range(4):
            pool[offset, 4 * i : 4 * i + 4, :] = pool_in[offset, i]
        weighted = spread_kernel(cells, pool[offset]) * keyval[...].astype(F32)
        parts[2 - offset] = gather_rows(blocks, weighted).astype(BF16)

    mine = pl.ds(1 - low, 2)
    pl.semaphore_wait(barrier, len(partners))
    pair_copy = links.start(parts.at[mine], from_pair, place.pair(0, 1 - low))
    edge_base = links.used
    for side in range(2):
        links.start(
            parts.at[2 * low], from_edge.at[1 - low],
            (place.clip, (place.tm - low + 4 * low - 2 + 32) % 32 + side),
            shift=1 - low if side == 0 else -low, slots=1,
        )
    query[...] = dot(normed_two[...], attn[0]).astype(BF16)
    cot_two_copy.wait()
    cot[...] = load_padded(cot_two_in, pad)
    back(0)
    pair_copy.wait_recv()
    for slot in range(2):
        links.arrival(from_edge.at[slot], edge_base + slot)
    ends = (place.tm // 2 > 0, place.tm // 2 < 15)
    for slot in range(2):
        edge = jnp.where(ends[slot], from_edge[slot].astype(F32), 0.0)
        frame = parts[1 - low + slot].astype(F32) + from_pair[slot].astype(F32) + edge
        frame = frame.astype(BF16)
        keys[x, z, 16 * slot : 16 * slot + 16, :] = frame[:, 0:D]
        values[x, z, 16 * slot : 16 * slot + 16, :] = frame[:, D:]

    copies = []
    for hop in (2, 1, 3):
        copies.append(links.start(keys.at[x, z], keys.at[x, z], place.along(2, hop)[0]))
        copies.append(links.start(values.at[x, z], values.at[x, z], place.along(0, hop)[0]))
    back(1)
    for copy in copies:
        copy.wait_recv()
    copies = []
    for hop in (2, 1, 3):
        copies.append(links.start(keys.at[x], keys.at[x], place.along(0, hop)[0]))
        copies.append(links.start(values.at[:, z], values.at[:, z], place.along(2, hop)[0]))
    for chunk in range(2, STEPS):
        mlp.send1(chunk - 2)
        back(chunk)
    unit, scale = norm_stats(load_padded(one_in, pad).astype(F32))
    d_gain_one = jnp.sum(branch[...] * unit, axis=0, keepdims=True)
    d_first = norm_back(unit, scale, gain_ref[0:1, :], branch[...])
    cot_one_copy.wait()
    total[...] = (load_padded(cot_one_in, pad).astype(F32) + d_first).astype(BF16)
    store_grid(cot_one_in, total[...])
    write(cot_one_in, total_out)
    d_att[...] = dot_nt(total[...], attn[3]).astype(BF16)
    for part in range(3):
        lefts[part] = dot_nt(orders[part], total[...]).astype(BF16)
    for copy in copies:
        copy.wait_recv()
    mlp.send1(4)
    mlp.send1(5)

    def heads(pair):
        lanes = pl.ds(pair * 128, 128)
        query_pair = query[:, lanes] * jnp.asarray(0.125, BF16)
        d_att_pair = d_att[:, lanes]
        key = keys[:, :, :, lanes].reshape(512, 128)
        value = values[:, :, :, lanes].reshape(512, 128)
        queries, d_atts, keys_h, values_h, probs_h, d_scores_h = [], [], [], [], [], []
        for side in range(2):

            def only(array):
                lane = iota(array.shape, 1)
                keep = lane < 64 if side == 0 else lane >= 64
                return jnp.where(keep, array, jnp.zeros_like(array))

            queries.append(only(query_pair))
            d_atts.append(only(d_att_pair))
            keys_h.append(only(key))
            values_h.append(only(value))
            weights = jnp.exp(dot_nt(queries[side], key))
            probs = weights * (1.0 / jnp.sum(weights, axis=-1, keepdims=True))
            product = probs * dot_nt(d_atts[side], value)
            d_scores = product - probs * jnp.sum(product, axis=-1, keepdims=True)
            probs_h.append(probs.astype(BF16))
            d_scores_h.append(d_scores.astype(BF16))

        def joined(pieces, axis):
            return jnp.concatenate(pieces, axis=axis)

        att = dot(joined(probs_h, 1), joined(values_h, 0))
        d_q = dot(joined(d_scores_h, 1), joined(keys_h, 0)) * 0.125
        d_k = dot_tn(joined(d_scores_h, 0), joined(queries, 0))
        d_v = dot_tn(joined(probs_h, 0), joined(d_atts, 0))
        attended[:, lanes] = att.astype(BF16)
        d_query[:, lanes] = d_q.astype(BF16)
        d_keys[:, :, :, lanes] = d_k.astype(BF16).reshape(4, 4, 32, 128)
        d_values[:, :, :, lanes] = d_v.astype(BF16).reshape(4, 4, 32, 128)

    copies = []
    for group in range(3):
        for pair in range(2 * group, 2 * group + 2):
            heads(pair)
        lanes = pl.ds(group * 256, 256)
        for hop in (2, 1, 3):
            device, at = place.along(0, hop)
            copies.append(
                links.start(d_keys.at[at, :, :, lanes], x_keys.at[hop - 1, :, :, lanes], device)
            )
            device, at = place.along(2, hop)
            copies.append(
                links.start(d_values.at[:, at, :, lanes], z_values.at[hop - 1, :, :, lanes], device)
            )

    for part in range(STEPS):
        for copy in mlp.copies[0, part]:
            links.sent(copy)
    branch_f = dot(attended[...], attn[3])
    store_grid(one_in, (load_padded(one_in, pad).astype(F32) - branch_f).astype(BF16))
    write(one_in, one_out)
    for part in range(3):
        inside = pl.ds(part * 256, 256)
        lhs = dot_nt(orders[part], d_query[...]).astype(BF16)
        stage[:, pl.ds(part * 512, 256)] = dot(lhs, normed_two[:, inside]).astype(BF16)
        stage[:, pl.ds(part * 512 + 256, 256)] = dot(
            lefts[part], attended[:, inside]
        ).astype(BF16)
        first.send0(part)
    branch[...] = dot_nt(d_query[...], attn[0])

    for copy in copies:
        copy.wait_recv()
    sum_k = d_keys[x].astype(F32)
    sum_v = d_values[:, z].astype(F32)
    for slot in range(3):
        sum_k = sum_k + x_keys[slot].astype(F32)
        sum_v = sum_v + z_values[slot].astype(F32)
    key_sum[...] = sum_k.astype(BF16)
    value_sum[...] = sum_v.astype(BF16)
    copies = []
    for hop in (2, 1, 3):
        device, at = place.along(2, hop)
        copies.append(links.start(key_sum.at[at], z_keys.at[hop - 1], device))
        device, at = place.along(0, hop)
        copies.append(links.start(value_sum.at[at], x_values.at[hop - 1], device))
    for part in (0, 1, 4, 5):
        mlp.send2(part)
    for copy in copies:
        copy.wait_recv()
    sum_k = key_sum[z].astype(F32)
    sum_v = value_sum[x].astype(F32)
    for slot in range(3):
        sum_k = sum_k + z_keys[slot].astype(F32)
        sum_v = sum_v + x_values[slot].astype(F32)
    pair_sum[:, 0:D] = sum_k.astype(BF16)
    pair_sum[:, D:] = sum_v.astype(BF16)

    pair_copy = links.start(pair_sum, pair_land, place.pair(0, 1 - low))
    edge_base = links.used
    for hop, rows in ((-1, pl.ds(0, 16)), (1, pl.ds(16, 16))):
        side = 1 if hop == -1 else 0
        links.start(
            pair_sum.at[rows, :], edge_land.at[low], place.pair(hop, side),
            shift=low if hop == -1 else low - 1, slots=1,
        )
    for part in range(3):
        first.send1(part)
    mlp.send2(2)
    mlp.send2(3)
    pair_copy.wait_recv()
    for slot in range(2):
        links.arrival(edge_land.at[slot], edge_base + slot)
    edge = edge_land[0].astype(F32) + edge_land[1].astype(F32)
    inside = (low == 0) & (place.tm > 0) | (low == 1) & (place.tm < 31)
    edge = jnp.where(inside, edge, 0.0).astype(BF16)
    pair_frames = (pair_sum[...].astype(F32) + pair_land[...].astype(F32)).astype(BF16)
    frame_0, frame_1 = pair_frames[0:16, :], pair_frames[16:32, :]
    before = jnp.where(low == 0, edge, frame_0)
    here = jnp.where(low == 0, frame_0, frame_1)
    after = jnp.where(low == 0, frame_1, edge)

    cells, blocks = cell_maps()
    keyval_f = keyval[...].astype(F32)
    d_keyval = None
    for offset, source in enumerate((after, here, before)):
        expanded = dot(blocks, source)
        term = spread_kernel(cells, pool[offset]) * expanded
        d_keyval = term if d_keyval is None else d_keyval + term
        d_kernel = gather_rows(cells[:, 0:16], keyval_f * expanded).astype(BF16)
        extra[16 * offset : 16 * offset + 16, :] = d_kernel
    d_keyval = d_keyval.astype(BF16)
    d_key_proj, d_value_proj = d_keyval[:, 0:D], d_keyval[:, D:]

    def last_part(part):
        inside = pl.ds(part * 256, 256)
        start = FIRST_COLS + part * 512
        lhs = dot_nt(orders[part], d_key_proj).astype(BF16)
        stage[:, pl.ds(start, 256)] = dot(lhs, normed_two[:, inside]).astype(BF16)
        lhs = dot_nt(orders[part], d_value_proj).astype(BF16)
        stage[:, pl.ds(start + 256, 256)] = dot(lhs, normed_two[:, inside]).astype(BF16)

    for part in range(2):
        last_part(part)
        last.send0(part)
    last_part(2)
    d_normed_two = branch[...] + dot_nt(d_key_proj, attn[1]) + dot_nt(d_value_proj, attn[2])
    row, lane = iota((256, 256), 0), iota((256, 256), 1)
    parted = jnp.where(row == 2 * (lane & 127) + (lane >> 7), 1.0, 0.0).astype(BF16)
    extra_gain[...] = jnp.zeros(extra_gain.shape, F32)
    for k in range(6):
        lanes = pl.ds(k * 128, 128)
        sides = dot(extra[:, pl.ds(k * 256, 256)], parted)
        extra_gain[0:48, lanes] = sides[:, 0:128]
        extra_gain[48:96, lanes] = sides[:, 128:256]
    extra_gain[96:97, :] = d_gain_one
    extra_gain[97:98, :] = jnp.sum(d_normed_two * unit_two, axis=0, keepdims=True)
    block = dot_nt(orders[2], extra_gain[...].astype(BF16))
    stage[:, pl.ds(FIRST_COLS + 1536, 128)] = block.astype(BF16)
    last.send0(2)
    last.send1(0)
    last.send1(1)
    d_second = norm_back(unit_two, scale_two, gain_ref[1:2, :], d_normed_two)
    result = load_padded(cot_two_in, pad).astype(F32) + d_second
    store_grid(cot_two_in, result.astype(BF16))
    write(cot_two_in, grad_two_out)
    last.send1(2)

    for part in range(3):
        first.send2(part)
    for part in (0, 1, 4, 5):
        mlp.send3(part)
    for part in range(3):
        last.send2(part)
    for part in range(3):
        first.send3(part)
    mlp.send3(2)
    mlp.send3(3)
    for part in (0, 1, 4, 5):
        mlp.finish(part)
    for part in range(3):
        last.send3(part)
    for part in range(3):
        first.finish(part)
    mlp.finish(2)
    mlp.finish(3)
    write(mlp_sums, mlp_out)
    for part in range(3):
        last.finish(part)
    write(attn_sums, attn_out)
    write(rest_sums, rest_out)
    for copy in links.started:
        copy.wait_send()
    for copy in writes:
        copy.wait()


def run_block(half_one, half_two, grad_one, grad_two, norm_gain, attn_weight, mlp_weight, pool_kernel):
    vmem = pl.BlockSpec(memory_space=pltpu.VMEM)
    hbm = pl.BlockSpec(memory_space=pl.ANY)
    shape = jax.ShapeDtypeStruct
    scratch = [
        pltpu.SemaphoreType.DMA((N_COPIES,)),
        pltpu.SemaphoreType.DMA((N_COPIES,)),
        pltpu.SemaphoreType.DMA((6,)),
        pltpu.SemaphoreType.DMA((2, 3)),
        *[pltpu.VMEM((1, 1, 14, 14, D), BF16) for _ in range(4)],
        pltpu.VMEM((3, 4, 4, KV), F32),
        pltpu.VMEM((3, CHUNK, D), BF16),
        pltpu.VMEM((3, CHUNK, D), BF16),
        pltpu.VMEM((D, FIRST_COLS + LAST_COLS), BF16),
        pltpu.VMEM((HALF, MLP_COLS), BF16), *landing(MLP_COLS),
        *landing(FIRST_COLS),
        *landing(LAST_COLS),
        pltpu.VMEM((4, D, D), BF16),
        pltpu.VMEM((4, D, D), BF16),
        pltpu.VMEM((3, 16, KV), F32),
        pltpu.VMEM((14, 16, D), BF16),
        pltpu.VMEM((ROWS, D), BF16),
        pltpu.VMEM((ROWS, D), BF16),
        pltpu.VMEM((ROWS, D), F32),
        pltpu.VMEM((ROWS, D), BF16),
        pltpu.VMEM((ROWS, D), BF16),
        pltpu.VMEM((ROWS, KV), BF16),
        pltpu.VMEM((ROWS, D), BF16),
        pltpu.VMEM((ROWS, D), BF16),
        pltpu.VMEM((3, D, ROWS), BF16),
        pltpu.VMEM((3, 16, KV), BF16),
        pltpu.VMEM((2, 16, KV), BF16),
        pltpu.VMEM((2, 16, KV), BF16),
        *[pltpu.VMEM((4, 4, 32, D), BF16) for _ in range(4)],
        pltpu.VMEM((3, 4, 32, D), BF16),
        pltpu.VMEM((3, 32, D), BF16),
        pltpu.VMEM((3, 32, D), BF16),
        pltpu.VMEM((3, 4, 32, D), BF16),
        pltpu.VMEM((4, 32, D), BF16),
        pltpu.VMEM((4, 32, D), BF16),
        pltpu.VMEM((32, KV), BF16),
        pltpu.VMEM((32, KV), BF16),
        pltpu.VMEM((2, 16, KV), BF16),
        pltpu.VMEM((ROWS, D), BF16),
        pltpu.VMEM((ROWS, D), BF16),
        pltpu.VMEM((48, KV), BF16),
        pltpu.VMEM((128, D), F32),
        pltpu.VMEM((6, 2, FF), F32),
        pltpu.VMEM((6, 4, D), F32),
        pltpu.VMEM((8, 128), F32),
        pltpu.SemaphoreType.DMA((7,)),
    ]
    return pl.pallas_call(
        block_kernel,
        in_specs=[hbm, hbm, hbm, hbm, vmem, hbm, hbm, hbm],
        out_specs=[hbm] * 7,
        out_shape=[
            *[shape(half_one.shape, BF16) for _ in range(4)],
            shape((6, 2, FF), F32), shape((6, 4, D), F32), shape((8, 128), F32),
        ],
        scratch_shapes=scratch,
        compiler_params=pltpu.CompilerParams(
            collective_id=0, has_side_effects=True, vmem_limit_bytes=63 * MIB
        ),
        name="reversible_block",
    )(half_one, half_two, grad_one, grad_two, norm_gain, attn_weight, mlp_weight, pool_kernel)


def hand_out_kernel(*refs):
    taken, rest_ref, given, kernel_out, gain_out = refs[0:6], refs[6], refs[7:13], *refs[13:15]
    held, in_sem, out_sem = refs[15:21], *refs[21:]
    loads = [
        pltpu.make_async_copy(source, target, in_sem.at[k])
        for k, (source, target) in enumerate(zip(taken, held))
    ]
    copies = [
        pltpu.make_async_copy(source, target, out_sem.at[k])
        for k, (source, target) in enumerate(zip(held, given))
    ]
    for load in loads:
        load.start()
    for load, copy in zip(loads, copies):
        load.wait()
        copy.start()
    rest = rest_ref[...]

    def columns(width, step, side):
        row, lane = iota((8, width), 0), iota((8, width), 1)
        pick = jnp.where((row < 6) & (lane == step * row + side), 1.0, 0.0)
        return lax.dot_general(
            rest, pick, (((0,), (0,)), ((), ())),
            precision=lax.Precision.HIGHEST, preferred_element_type=F32,
        )

    kernel_grad = columns(12, 2, 0)[0:48] + columns(12, 2, 1)[48:96]
    for offset in range(3):
        for i in range(4):
            at = 16 * offset + 4 * i
            kernel_out[offset, i] = kernel_grad[at : at + 4]
    gain_out[...] = columns(6, 1, 0)[96:98]
    for copy in copies:
        copy.wait()


def hand_out(results, rest):
    vmem = pl.BlockSpec(memory_space=pltpu.VMEM)
    hbm = pl.BlockSpec(memory_space=pl.ANY)
    shape = jax.ShapeDtypeStruct
    return pl.pallas_call(
        hand_out_kernel,
        in_specs=[hbm] * 6 + [vmem],
        out_specs=[hbm] * 6 + [vmem] * 2,
        out_shape=[shape(array.shape, array.dtype) for array in results]
        + [shape((3, 4, 4, 12), F32), shape((2, 6), F32)],
        scratch_shapes=[pltpu.VMEM(array.shape, array.dtype) for array in results]
        + [pltpu.SemaphoreType.DMA((6,)), pltpu.SemaphoreType.DMA((6,))],
        compiler_params=pltpu.CompilerParams(vmem_limit_bytes=62 * MIB),
        name="hand_out",
    )(*results, rest)


def shards(half_one, half_two, grad_one, grad_two, norm_gain, attn_weight, mlp_weight, pool_kernel):
    *results, rest = run_block(
        half_one, half_two, grad_one, grad_two, norm_gain, attn_weight, mlp_weight, pool_kernel
    )
    (input_one, input_two, total, input_grad_two, mlp_sums, attn_sums, kernel_grad, gain_grad) = (
        hand_out(results, rest)
    )
    mlp_grad = mlp_sums.transpose(1, 2, 0)
    attn_grad = attn_sums.transpose(1, 2, 0)
    return (input_one, input_two, total, input_grad_two, attn_grad, mlp_grad, kernel_grad, gain_grad)


def solution(mesh):
    placed = (
        P("clip", "tm", None, None, None),
        P("clip", "tm", None, None, None),
        P("clip", "tm", None, None, None),
        P("clip", "tm", None, None, None),
        P(),
        P(),
        P(),
        P(),
    )
    return jax.shard_map(
        shards,
        mesh=mesh,
        in_specs=placed,
        out_specs=(
            P("clip", "tm", None, None, None),
            P("clip", "tm", None, None, None),
            P("clip", "tm", None, None, None),
            P("clip", "tm", None, None, None),
            P(None, None, ("clip", "tm")),
            P(None, None, ("clip", "tm")),
            P(None, None, None, ("clip", "tm")),
            P(None, ("clip", "tm")),
        ),
        check_vma=False,
    )
```

```python
from functools import partial

import jax
import jax.numpy as jnp
from jax import lax
from jax.experimental import pallas as pl
from jax.experimental.pallas import tpu as pltpu
from jax.sharding import PartitionSpec as P

D = 768
FF = 3072
KV = 2 * D
ROWS = 224
CHUNK = 512
STEPS = FF // CHUNK
HALF = 384
MIB = 1024 * 1024
F32 = jnp.float32
BF16 = jnp.bfloat16
MESH = pl.DeviceIdType.MESH


def dot(a, b):
    return lax.dot_general(a, b, (((1,), (0,)), ((), ())), preferred_element_type=F32)


def dot_nt(a, b):
    return lax.dot_general(a, b, (((1,), (1,)), ((), ())), preferred_element_type=F32)


def dot_tn(a, b):
    return lax.dot_general(a, b, (((0,), (0,)), ((), ())), preferred_element_type=F32)


def iota(shape, dim):
    return lax.broadcasted_iota(jnp.int32, shape, dim)


def source_column(rows, axes):
    owner_at = (rows * 43691) >> 18
    inner = rows - owner_at * 6
    core = owner_at >> 6
    digits = ((owner_at >> 4) & 3, (owner_at >> 2) & 3, owner_at & 3)
    x, y, z = (digits[axes.index(axis)] for axis in range(3))
    owner = (y >> 1) * 64 + core * 32 + x * 8 + z * 2 + (y & 1)
    return owner * 6 + inner


def permutation(axes):
    source = source_column(iota((D, 128), 0), axes)
    lanes = iota((D, 128), 1)
    pieces = [
        jnp.where(source == lanes + 128 * k, 1.0, 0.0).astype(BF16) for k in range(D // 128)
    ]
    return jnp.concatenate(pieces, axis=1)


def norm_stats(values):
    centre = jnp.mean(values, axis=-1, keepdims=True)
    centred = values - centre
    spread = jnp.mean(centred * centred, axis=-1, keepdims=True)
    scale = lax.rsqrt(spread + 1e-05)
    return centred * scale, scale


def norm_back(unit, scale, gain, cotangent):
    d_unit = cotangent * gain
    first = jnp.mean(d_unit, axis=-1, keepdims=True)
    second = jnp.mean(d_unit * unit, axis=-1, keepdims=True)
    return scale * (d_unit - first - unit * second)


def load_padded(ref, pad):
    pad[...] = jnp.zeros(pad.shape, pad.dtype)
    pad[:, 0:14, :] = ref[0, 0]
    return pad[...].reshape(ROWS, D)


def store_grid(ref, values):
    ref[0, 0] = values.reshape(14, 16, D)[:, 0:14, :]


def spread_kernel(flat):
    row, lane = iota((64, 48), 0), iota((64, 48), 1)
    cell = (row >> 4) * 4 + (((row & 15) + 1) & 3)
    cells = jnp.where(((row & 15) < 14) & ((lane & 15) == cell), 1.0, 0.0).astype(BF16)
    high = flat.astype(BF16)
    rest = flat - high.astype(F32)
    middle = rest.astype(BF16)
    low = (rest - middle.astype(F32)).astype(BF16)
    table = dot(cells, jnp.concatenate([high, middle, low], axis=0))
    return [table[16 * i : 16 * i + 16] for i in range(4)]


def spread_blocks(frame):
    row, lane = iota((64, 16), 0), iota((64, 16), 1)
    block = (row >> 4) * 4 + (((row & 15) + 1) >> 2)
    blocks = jnp.where(((row & 15) < 14) & (lane == block), 1.0, 0.0).astype(BF16)
    table = dot(blocks, frame)
    return [table[16 * a : 16 * a + 16] for a in range(4)]


def sum_columns(tables, group):
    row, lane = iota((48, 192), 0), iota((48, 192), 1)
    across = lane & 15
    same = (row >> 2 == lane >> 4) & (across < 14) & (group(across + 1) == (row & 3))
    pick = jnp.where(same, 1.0, 0.0).astype(BF16)
    stacked = jnp.concatenate([table.astype(BF16) for table in tables], axis=0)
    return dot(pick, stacked)


def add_to(tables, at, value):
    tables[at] = value if tables[at] is None else tables[at] + value


class Links:
    def __init__(self, send, recv):
        self.send, self.recv, self.used, self.started = send, recv, 0, []

    def start(self, source, target, device, shift=0, slots=1):
        copy = pltpu.make_async_remote_copy(
            src_ref=source, dst_ref=target,
            send_sem=self.send.at[self.used], recv_sem=self.recv.at[self.used + shift],
            device_id=device, device_id_type=MESH,
        )
        self.used += slots
        copy.start()
        self.started.append(copy)
        return copy

    def arrival(self, target, number):
        pltpu.make_async_remote_copy(
            src_ref=target, dst_ref=target,
            send_sem=self.send.at[number], recv_sem=self.recv.at[number],
            device_id=(lax.axis_index("clip"), lax.axis_index("tm")), device_id_type=MESH,
        ).wait_recv()

    def sent(self, copy):
        copy.wait_send()
        self.started = [other for other in self.started if other is not copy]


class Place:
    def __init__(self):
        clip, tm = lax.axis_index("clip"), lax.axis_index("tm")
        self.tm, self.clip = tm, clip
        self.core, high = clip % 2, clip // 2
        self.low = tm % 2
        self.at = (tm // 8, high * 2 + self.low, (tm // 2) % 4)

    def device(self, core, at):
        x, y, z = at
        return ((y // 2) * 2 + core, x * 8 + z * 2 + y % 2)

    def other_core(self):
        return self.device(1 - self.core, self.at)

    def along(self, axis, hop):
        at = list(self.at)
        at[axis] = (at[axis] + hop) % 4
        return self.device(self.core, at), at[axis]

    def pair(self, hop, low):
        return (self.clip, (self.tm - self.low + 2 * hop + 32) % 32 + low)


class Reduction:
    def __init__(self, links, place, parts, orders, held, base, offset, landed, store):
        self.links, self.place, self.parts = links, place, parts
        self.axes = [ORDERS[order] for order in orders]
        self.held, self.base, self.offset = held, base, offset
        self.in0, self.in1, self.sum1, self.in2, self.sum2, self.in3 = landed
        self.store = store
        self.copies = {}

    def columns(self, part, offset=0):
        return pl.ds(self.parts[part][0] + offset, self.parts[part][1])

    def blocks(self, part, width=512):
        first, count = self.parts[part]
        if count % width:
            width = count
        return [(first + k * width, width) for k in range(count // width)]

    def send0(self, part):
        cols = self.columns(part)
        rows = pl.ds(pl.multiple_of((1 - self.place.core) * HALF, HALF), HALF)
        self.copies[0, part] = [
            self.links.start(
                self.held.at[rows, self.columns(part, self.offset)], self.in0.at[:, cols],
                self.place.other_core(),
            )
        ]

    def arrive(self, stage, part):
        for copy in self.copies[stage, part]:
            copy.wait_recv()

    def spread(self, stage, part, source, base, offset, rows, target):
        axis = self.axes[part][stage - 1]
        cols = self.columns(part)
        source_cols = self.columns(part, offset)
        self.copies[stage, part] = []
        for hop in (2, 1, 3):
            device, at = self.place.along(axis, hop)
            window = pl.ds(pl.multiple_of(base + at * rows, rows), rows)
            self.copies[stage, part].append(
                self.links.start(
                    source.at[window, source_cols], target.at[hop - 1, :, cols], device
                )
            )

    def send1(self, part):
        self.arrive(0, part)
        first, count = self.parts[part]

        def body(k, carry):
            rows = pl.ds(pl.multiple_of(k * 16, 16), 16)
            mine = pl.ds(pl.multiple_of(self.base + k * 16, 16), 16)
            cols, held_cols = pl.ds(first, count), pl.ds(first + self.offset, count)
            total = self.held[mine, held_cols].astype(F32) + self.in0[rows, cols].astype(F32)
            self.held[mine, held_cols] = total.astype(BF16)
            return carry

        lax.fori_loop(0, HALF // 16, body, 0)
        self.spread(1, part, self.held, self.base, self.offset, 96, self.in1)

    def send2(self, part):
        self.arrive(1, part)
        mine = self.place.at[self.axes[part][0]]
        rows = pl.ds(pl.multiple_of(self.base + mine * 96, 96), 96)
        place_row, place_col = iota((128, 96), 0), iota((128, 96), 1)
        owner = place_row >> 3
        inner = place_row & 7
        widen = jnp.where((inner < 6) & (place_col == owner * 6 + inner), 1.0, 0.0).astype(BF16)
        for first, count in self.blocks(part):
            cols = pl.ds(first, count)
            total = self.held[rows, pl.ds(first + self.offset, count)].astype(F32)
            for slot in range(3):
                total = total + self.in1[slot, :, cols].astype(F32)
            self.sum1[:, cols] = dot(widen, total.astype(BF16)).astype(BF16)
        self.spread(2, part, self.sum1, 0, 0, 32, self.in2)

    def send3(self, part):
        self.arrive(2, part)
        mine = self.place.at[self.axes[part][1]]
        rows = pl.ds(pl.multiple_of(mine * 32, 32), 32)
        for first, count in self.blocks(part):
            cols = pl.ds(first, count)
            total = self.sum1[rows, cols].astype(F32)
            for slot in range(3):
                total = total + self.in2[slot, :, cols].astype(F32)
            self.sum2[:, cols] = total
        self.spread(3, part, self.sum2, 0, 0, 8, self.in3)

    def finish(self, part):
        self.arrive(3, part)
        mine = self.place.at[self.axes[part][2]]
        rows = pl.ds(pl.multiple_of(mine * 8, 8), 8)
        for first, count in self.blocks(part):
            cols = pl.ds(first, count)
            total = self.sum2[rows, cols]
            for slot in range(3):
                total = total + self.in3[slot, :, cols]
            self.store(part, (first - self.parts[part][0]) // 512, total)


ORDERS = ((0, 1, 2), (1, 2, 0), (2, 0, 1), (1, 0, 2))
MLP_ORDERS = (1, 1, 3, 3, 0, 2)
MLP_PARTS = tuple((k * 1024, 1024) for k in range(STEPS))
FIRST_PARTS = tuple((p * 512, 512) for p in range(3))
LAST_PARTS = ((0, 512), (512, 512), (1024, 640))
MLP_COLS, FIRST_COLS, LAST_COLS = 6144, 1536, 1664
N_COPIES = 6 * 10 + 2 * 30 + 3 + 12 + 24 + 3


def landing(cols):
    return [
        pltpu.VMEM((HALF, cols), BF16),
        pltpu.VMEM((3, 96, cols), BF16),
        pltpu.VMEM((128, cols), BF16),
        pltpu.VMEM((3, 32, cols), BF16),
        pltpu.VMEM((32, cols), F32),
        pltpu.VMEM((3, 8, cols), F32),
    ]


def block_kernel(
    one_hbm, two_hbm, cot_one_hbm, cot_two_hbm, gain_ref, attn_hbm, mlp_hbm, pool_hbm,
    one_out, two_out, total_out, grad_two_out, mlp_out, attn_out, rest_out,
    *scratch,
):
    scratch = list(scratch)

    def take(count):
        taken = scratch[:count]
        del scratch[:count]
        return taken

    send_sem, recv_sem, local_sem, weight_sem = take(4)
    one_in, two_in, cot_one_in, cot_two_in, pool_in = take(5)
    up_buf, down_buf, stage = take(3)
    mlp_own, mlp_land = take(1)[0], take(6)
    first_land, last_land = take(6), take(6)
    attn, orders, pool, pad = take(4)
    normed, cot, branch = take(3)
    normed_two, query, keyval, d_att, total, lefts = take(6)
    parts, from_pair, from_edge = take(3)
    keys, values, d_keys, d_values = take(4)
    x_keys, z_keys, x_values, z_values = take(4)
    key_sum, value_sum, pair_sum, pair_land, edge_land = take(5)
    attended, d_query, extra, extra_gain, d_proj = take(5)
    mlp_sums, attn_sums, rest_sums, out_sem = take(4)

    place = Place()
    links = Links(send_sem, recv_sem)
    x, y, z = place.at
    low = place.low

    sources = (one_hbm, cot_two_hbm, two_hbm, cot_one_hbm, pool_hbm, attn_hbm)
    targets = (one_in, cot_two_in, two_in, cot_one_in, pool_in, attn)
    fetches = [
        pltpu.make_async_copy(source, target, local_sem.at[k])
        for k, (source, target) in enumerate(zip(sources, targets))
    ]
    one_copy, cot_two_copy, two_copy, cot_one_copy, pool_copy, attn_copy = fetches

    def weight_copies(k):
        rows = pl.ds(k % STEPS * CHUNK, CHUNK)
        return [
            pltpu.make_async_copy(mlp_hbm.at[0, rows], up_buf.at[k % 3], weight_sem.at[0, k % 3]),
            pltpu.make_async_copy(mlp_hbm.at[1, rows], down_buf.at[k % 3], weight_sem.at[1, k % 3]),
        ]

    one_copy.start()
    for k in range(3):
        for copy in weight_copies(k):
            copy.start()

    barrier = pltpu.get_barrier_semaphore()
    partners = [place.other_core()]
    partners += [place.pair(hop, side) for hop in (-1, 1) for side in range(2)]
    partners += [place.along(axis, hop)[0] for axis in range(3) for hop in (1, 2, 3)]
    for device in partners:
        pl.semaphore_signal(barrier, inc=1, device_id=device, device_id_type=MESH)

    writes = []

    def write(source, target):
        copy = pltpu.make_async_copy(source, target, out_sem.at[len(writes)])
        copy.start()
        writes.append(copy)

    def store_mlp(part, block, values):
        mlp_sums[:, block, pl.ds(part * CHUNK, CHUNK)] = values[0:6]

    def store_first(part, block, values):
        at = pl.ds(part * 256, 256)
        attn_sums[:, 0, at] = values[0:6, 0:256]
        attn_sums[:, 3, at] = values[0:6, 256:512]

    def store_last(part, block, values):
        at = pl.ds(part * 256, 256)
        attn_sums[:, 1, at] = values[0:6, 0:256]
        attn_sums[:, 2, at] = values[0:6, 256:512]
        if part == 2:
            rest_sums[...] = values[:, 512:640]

    own_base = pl.multiple_of(place.core * HALF, HALF)
    other_base = pl.multiple_of((1 - place.core) * HALF, HALF)
    mlp = Reduction(links, place, MLP_PARTS, MLP_ORDERS, mlp_own, 0, 0, mlp_land, store_mlp)
    first = Reduction(links, place, FIRST_PARTS, (0, 1, 2), stage, own_base, 0, first_land, store_first)
    last = Reduction(links, place, LAST_PARTS, (0, 1, 2), stage, own_base, FIRST_COLS, last_land, store_last)

    def kept(chunk):
        at = chunk * 2 * CHUNK
        rows = pl.ds(0, ROWS)
        return mlp_own.at[rows, pl.ds(at, CHUNK)], mlp_own.at[rows, pl.ds(at + CHUNK, CHUNK)]

    def next_weights(k):
        if k + 3 < 2 * STEPS:
            for copy in weight_copies(k + 3):
                copy.start()

    orders[1] = permutation(ORDERS[1])
    one_copy.wait()
    unit, scale = norm_stats(load_padded(one_in, pad).astype(F32))
    normed[...] = (unit * gain_ref[0:1, :]).astype(BF16)
    for k in range(STEPS):
        for copy in weight_copies(k):
            copy.wait()
        hidden = dot_nt(normed[...], up_buf[k % 3])
        inner = 0.7978845608028654 * (hidden + 0.044715 * hidden * hidden * hidden)
        tanh = jnp.tanh(inner)
        half_sum = 0.5 * (1.0 + tanh)
        active = (hidden * half_sum).astype(BF16)
        slope = half_sum + 0.5 * hidden * (1.0 - tanh * tanh) * (
            0.7978845608028654 * (1.0 + 3.0 * 0.044715 * hidden * hidden)
        )
        active_at, slope_at = kept(k)
        active_at[...] = active
        slope_at[...] = slope.astype(BF16)
        if k == 0:
            branch[...] = dot(active, down_buf[k % 3])
        else:
            branch[...] += dot(active, down_buf[k % 3])
        next_weights(k)
        if k == 2:
            two_copy.start()
            pool_copy.start()
            attn_copy.start()
            cot_two_copy.start()
            cot_one_copy.start()

    def back(chunk):
        k = STEPS + chunk
        for copy in weight_copies(k):
            copy.wait()
        up, down = up_buf[k % 3], down_buf[k % 3]
        active_at, slope_at = kept(chunk)
        active = active_at[...]
        d_hidden = (slope_at[...].astype(F32) * dot_nt(cot[...], down)).astype(BF16)
        if chunk == 0:
            branch[...] = dot(d_hidden, up)
        else:
            branch[...] += dot(d_hidden, up)
        next_weights(k)
        order = MLP_ORDERS[chunk]
        if chunk == 0 or MLP_ORDERS[chunk - 1] != order:
            lefts[0] = dot_nt(orders[order], normed[...]).astype(BF16)
            lefts[1] = dot_nt(orders[order], cot[...]).astype(BF16)
        row = chunk % 2 * HALF
        col = chunk // 2 * 2 * CHUNK
        first_col = chunk * 2 * CHUNK
        for side, values_in in enumerate((d_hidden, active)):
            stage[pl.ds(row, HALF), pl.ds(col + side * CHUNK, CHUNK)] = dot(
                lefts[side, pl.ds(other_base, HALF)], values_in
            ).astype(BF16)
        mlp.copies[0, chunk] = [
            links.start(
                stage.at[pl.ds(row, HALF), pl.ds(col, 2 * CHUNK)],
                mlp.in0.at[:, pl.ds(first_col, 2 * CHUNK)],
                place.other_core(),
            )
        ]
        for side, values_in in enumerate((d_hidden, active)):
            mlp_own[:, pl.ds(first_col + side * CHUNK, CHUNK)] = dot(
                lefts[side, pl.ds(own_base, HALF)], values_in
            ).astype(BF16)

    two_copy.wait()
    restored = (load_padded(two_in, pad).astype(F32) - branch[...]).astype(BF16)
    store_grid(two_in, restored)
    write(two_in, two_out)
    unit_two, scale_two = norm_stats(restored.astype(F32))
    normed_two[...] = (unit_two * gain_ref[1:2, :]).astype(BF16)
    attn_copy.wait()
    keyval[:, 0:D] = dot(normed_two[...], attn[1]).astype(BF16)
    keyval[:, D:] = dot(normed_two[...], attn[2]).astype(BF16)
    pool_copy.wait()
    sums = [None] * 12
    for offset in range(3):
        for i in range(4):
            pool[offset, 4 * i : 4 * i + 4, :] = pool_in[offset, i]
        table = spread_kernel(pool[offset])
        for y_at in range(14):
            row = keyval[16 * y_at : 16 * y_at + 16, :].astype(F32)
            at = (2 - offset) * 4 + (y_at + 1) // 4
            add_to(sums, at, table[(y_at + 1) % 4] * row)
    pooled_parts = sum_columns(sums, lambda across: across >> 2).astype(BF16)
    for k in range(3):
        parts[k] = pooled_parts[16 * k : 16 * k + 16]

    mine = pl.ds(1 - low, 2)
    pl.semaphore_wait(barrier, len(partners))
    pair_copy = links.start(parts.at[mine], from_pair, place.pair(0, 1 - low))
    edge_base = links.used
    for side in range(2):
        links.start(
            parts.at[2 * low], from_edge.at[1 - low],
            (place.clip, (place.tm - low + 4 * low - 2 + 32) % 32 + side),
            shift=1 - low if side == 0 else -low, slots=1,
        )
    query[...] = dot(normed_two[...], attn[0]).astype(BF16)
    cot_two_copy.wait()
    cot[...] = load_padded(cot_two_in, pad)
    back(0)
    orders[3] = permutation(ORDERS[3])
    orders[0] = permutation(ORDERS[0])
    pair_copy.wait_recv()
    for slot in range(2):
        links.arrival(from_edge.at[slot], edge_base + slot)
    ends = (place.tm // 2 > 0, place.tm // 2 < 15)
    for slot in range(2):
        edge = jnp.where(ends[slot], from_edge[slot].astype(F32), 0.0)
        frame = parts[1 - low + slot].astype(F32) + from_pair[slot].astype(F32) + edge
        frame = frame.astype(BF16)
        keys[x, z, 16 * slot : 16 * slot + 16, :] = frame[:, 0:D]
        values[x, z, 16 * slot : 16 * slot + 16, :] = frame[:, D:]

    copies = []
    for hop in (2, 1, 3):
        copies.append(links.start(keys.at[x, z], keys.at[x, z], place.along(2, hop)[0]))
        copies.append(links.start(values.at[x, z], values.at[x, z], place.along(0, hop)[0]))
    back(1)
    orders[2] = permutation(ORDERS[2])
    for copy in copies:
        copy.wait_recv()
    copies = []
    for hop in (2, 1, 3):
        copies.append(links.start(keys.at[x], keys.at[x], place.along(0, hop)[0]))
        copies.append(links.start(values.at[:, z], values.at[:, z], place.along(2, hop)[0]))
    for chunk in range(2, STEPS):
        mlp.send1(chunk - 2)
        back(chunk)
    unit, scale = norm_stats(load_padded(one_in, pad).astype(F32))
    d_gain_one = jnp.sum(branch[...] * unit, axis=0, keepdims=True)
    d_first = norm_back(unit, scale, gain_ref[0:1, :], branch[...])
    cot_one_copy.wait()
    total[...] = (load_padded(cot_one_in, pad).astype(F32) + d_first).astype(BF16)
    store_grid(cot_one_in, total[...])
    write(cot_one_in, total_out)
    d_att[...] = dot_nt(total[...], attn[3]).astype(BF16)
    for part in range(3):
        lefts[part] = dot_nt(orders[part], total[...]).astype(BF16)
    for copy in copies:
        copy.wait_recv()
    mlp.send1(4)
    mlp.send1(5)

    def heads(pair):
        lanes = pl.ds(pair * 128, 128)
        query_pair = query[:, lanes] * jnp.asarray(0.125, BF16)
        d_att_pair = d_att[:, lanes]
        key = keys[:, :, :, lanes].reshape(512, 128)
        value = values[:, :, :, lanes].reshape(512, 128)
        queries, d_atts, keys_h, values_h, probs_h, d_scores_h = [], [], [], [], [], []
        for side in range(2):

            def only(array):
                lane = iota(array.shape, 1)
                keep = lane < 64 if side == 0 else lane >= 64
                return jnp.where(keep, array, jnp.zeros_like(array))

            queries.append(only(query_pair))
            d_atts.append(only(d_att_pair))
            keys_h.append(only(key))
            values_h.append(only(value))
            weights = jnp.exp(dot_nt(queries[side], key))
            probs = weights * (1.0 / jnp.sum(weights, axis=-1, keepdims=True))
            product = probs * dot_nt(d_atts[side], value)
            d_scores = product - probs * jnp.sum(product, axis=-1, keepdims=True)
            probs_h.append(probs.astype(BF16))
            d_scores_h.append(d_scores.astype(BF16))

        def joined(pieces, axis):
            return jnp.concatenate(pieces, axis=axis)

        att = dot(joined(probs_h, 1), joined(values_h, 0))
        d_q = dot(joined(d_scores_h, 1), joined(keys_h, 0)) * 0.125
        d_k = dot_tn(joined(d_scores_h, 0), joined(queries, 0))
        d_v = dot_tn(joined(probs_h, 0), joined(d_atts, 0))
        attended[:, lanes] = att.astype(BF16)
        d_query[:, lanes] = d_q.astype(BF16)
        d_keys[:, :, :, lanes] = d_k.astype(BF16).reshape(4, 4, 32, 128)
        d_values[:, :, :, lanes] = d_v.astype(BF16).reshape(4, 4, 32, 128)

    copies = []
    for group in range(3):
        for pair in range(2 * group, 2 * group + 2):
            heads(pair)
        lanes = pl.ds(group * 256, 256)
        for hop in (2, 1, 3):
            device, at = place.along(0, hop)
            copies.append(
                links.start(d_keys.at[at, :, :, lanes], x_keys.at[hop - 1, :, :, lanes], device)
            )
            device, at = place.along(2, hop)
            copies.append(
                links.start(d_values.at[:, at, :, lanes], z_values.at[hop - 1, :, :, lanes], device)
            )

    for part in range(STEPS):
        for copy in mlp.copies[0, part]:
            links.sent(copy)
    branch_f = dot(attended[...], attn[3])
    store_grid(one_in, (load_padded(one_in, pad).astype(F32) - branch_f).astype(BF16))
    write(one_in, one_out)
    for part in range(3):
        inside = pl.ds(part * 256, 256)
        lhs = dot_nt(orders[part], d_query[...]).astype(BF16)
        stage[:, pl.ds(part * 512, 256)] = dot(lhs, normed_two[:, inside]).astype(BF16)
        stage[:, pl.ds(part * 512 + 256, 256)] = dot(
            lefts[part], attended[:, inside]
        ).astype(BF16)
        first.send0(part)
    branch[...] = dot_nt(d_query[...], attn[0])

    for copy in copies:
        copy.wait_recv()
    sum_k = d_keys[x].astype(F32)
    sum_v = d_values[:, z].astype(F32)
    for slot in range(3):
        sum_k = sum_k + x_keys[slot].astype(F32)
        sum_v = sum_v + z_values[slot].astype(F32)
    key_sum[...] = sum_k.astype(BF16)
    value_sum[...] = sum_v.astype(BF16)
    copies = []
    for hop in (2, 1, 3):
        device, at = place.along(2, hop)
        copies.append(links.start(key_sum.at[at], z_keys.at[hop - 1], device))
        device, at = place.along(0, hop)
        copies.append(links.start(value_sum.at[at], x_values.at[hop - 1], device))
    for part in (0, 1, 4, 5):
        mlp.send2(part)
    for copy in copies:
        copy.wait_recv()
    sum_k = key_sum[z].astype(F32)
    sum_v = value_sum[x].astype(F32)
    for slot in range(3):
        sum_k = sum_k + z_keys[slot].astype(F32)
        sum_v = sum_v + x_values[slot].astype(F32)
    pair_sum[:, 0:D] = sum_k.astype(BF16)
    pair_sum[:, D:] = sum_v.astype(BF16)

    pair_copy = links.start(pair_sum, pair_land, place.pair(0, 1 - low))
    edge_base = links.used
    for hop, rows in ((-1, pl.ds(0, 16)), (1, pl.ds(16, 16))):
        side = 1 if hop == -1 else 0
        links.start(
            pair_sum.at[rows, :], edge_land.at[low], place.pair(hop, side),
            shift=low if hop == -1 else low - 1, slots=1,
        )
    for part in range(3):
        first.send1(part)
    mlp.send2(2)
    mlp.send2(3)
    pair_copy.wait_recv()
    for slot in range(2):
        links.arrival(edge_land.at[slot], edge_base + slot)
    edge = edge_land[0].astype(F32) + edge_land[1].astype(F32)
    inside = (low == 0) & (place.tm > 0) | (low == 1) & (place.tm < 31)
    edge = jnp.where(inside, edge, 0.0).astype(BF16)
    pair_frames = (pair_sum[...].astype(F32) + pair_land[...].astype(F32)).astype(BF16)
    frame_0, frame_1 = pair_frames[0:16, :], pair_frames[16:32, :]
    before = jnp.where(low == 0, edge, frame_0)
    here = jnp.where(low == 0, frame_0, frame_1)
    after = jnp.where(low == 0, frame_1, edge)

    sums = [None] * 12
    d_rows = [None] * 14
    for offset, source in enumerate((after, here, before)):
        table = spread_kernel(pool[offset])
        expanded = spread_blocks(source)
        for y_at in range(14):
            i, block = (y_at + 1) % 4, (y_at + 1) // 4
            row = keyval[16 * y_at : 16 * y_at + 16, :].astype(F32)
            add_to(d_rows, y_at, table[i] * expanded[block])
            add_to(sums, offset * 4 + i, row * expanded[block])
    extra[...] = sum_columns(sums, lambda across: across & 3).astype(BF16)
    for y_at in range(14):
        d_proj[16 * y_at : 16 * y_at + 16, :] = d_rows[y_at].astype(BF16)
    d_keyval = d_proj[...]
    d_key_proj, d_value_proj = d_keyval[:, 0:D], d_keyval[:, D:]

    def last_part(part):
        inside = pl.ds(part * 256, 256)
        start = FIRST_COLS + part * 512
        lhs = dot_nt(orders[part], d_key_proj).astype(BF16)
        stage[:, pl.ds(start, 256)] = dot(lhs, normed_two[:, inside]).astype(BF16)
        lhs = dot_nt(orders[part], d_value_proj).astype(BF16)
        stage[:, pl.ds(start + 256, 256)] = dot(lhs, normed_two[:, inside]).astype(BF16)

    for part in range(2):
        last_part(part)
        last.send0(part)
    last_part(2)
    last.send1(0)
    d_normed_two = branch[...] + dot_nt(d_key_proj, attn[1]) + dot_nt(d_value_proj, attn[2])
    row, lane = iota((256, 256), 0), iota((256, 256), 1)
    parted = jnp.where(row == 2 * (lane & 127) + (lane >> 7), 1.0, 0.0).astype(BF16)
    extra_gain[...] = jnp.zeros(extra_gain.shape, F32)
    for k in range(6):
        lanes = pl.ds(k * 128, 128)
        sides = dot(extra[:, pl.ds(k * 256, 256)], parted)
        extra_gain[0:48, lanes] = sides[:, 0:128]
        extra_gain[48:96, lanes] = sides[:, 128:256]
    extra_gain[96:97, :] = d_gain_one
    extra_gain[97:98, :] = jnp.sum(d_normed_two * unit_two, axis=0, keepdims=True)
    block = dot_nt(orders[2], extra_gain[...].astype(BF16))
    stage[:, pl.ds(FIRST_COLS + 1536, 128)] = block.astype(BF16)
    last.send0(2)
    last.send1(1)
    d_second = norm_back(unit_two, scale_two, gain_ref[1:2, :], d_normed_two)
    result = load_padded(cot_two_in, pad).astype(F32) + d_second
    store_grid(cot_two_in, result.astype(BF16))
    write(cot_two_in, grad_two_out)
    last.send1(2)

    for part in range(3):
        first.send2(part)
    for part in (0, 1, 4, 5):
        mlp.send3(part)
    for part in range(3):
        last.send2(part)
    for part in range(3):
        first.send3(part)
    mlp.send3(2)
    mlp.send3(3)
    for part in (0, 1, 4, 5):
        mlp.finish(part)
    for part in range(3):
        last.send3(part)
    for part in range(3):
        first.finish(part)
    mlp.finish(2)
    mlp.finish(3)
    write(mlp_sums, mlp_out)
    for part in range(3):
        last.finish(part)
    write(attn_sums, attn_out)
    write(rest_sums, rest_out)
    for copy in links.started:
        copy.wait_send()
    for copy in writes:
        copy.wait()


def run_block(half_one, half_two, grad_one, grad_two, norm_gain, attn_weight, mlp_weight, pool_kernel):
    vmem = pl.BlockSpec(memory_space=pltpu.VMEM)
    hbm = pl.BlockSpec(memory_space=pl.ANY)
    shape = jax.ShapeDtypeStruct
    scratch = [
        pltpu.SemaphoreType.DMA((N_COPIES,)),
        pltpu.SemaphoreType.DMA((N_COPIES,)),
        pltpu.SemaphoreType.DMA((6,)),
        pltpu.SemaphoreType.DMA((2, 3)),
        *[pltpu.VMEM((1, 1, 14, 14, D), BF16) for _ in range(4)],
        pltpu.VMEM((3, 4, 4, KV), F32),
        pltpu.VMEM((3, CHUNK, D), BF16),
        pltpu.VMEM((3, CHUNK, D), BF16),
        pltpu.VMEM((D, FIRST_COLS + LAST_COLS), BF16),
        pltpu.VMEM((HALF, MLP_COLS), BF16), *landing(MLP_COLS),
        *landing(FIRST_COLS),
        *landing(LAST_COLS),
        pltpu.VMEM((4, D, D), BF16),
        pltpu.VMEM((4, D, D), BF16),
        pltpu.VMEM((3, 16, KV), F32),
        pltpu.VMEM((14, 16, D), BF16),
        pltpu.VMEM((ROWS, D), BF16),
        pltpu.VMEM((ROWS, D), BF16),
        pltpu.VMEM((ROWS, D), F32),
        pltpu.VMEM((ROWS, D), BF16),
        pltpu.VMEM((ROWS, D), BF16),
        pltpu.VMEM((ROWS, KV), BF16),
        pltpu.VMEM((ROWS, D), BF16),
        pltpu.VMEM((ROWS, D), BF16),
        pltpu.VMEM((3, D, ROWS), BF16),
        pltpu.VMEM((3, 16, KV), BF16),
        pltpu.VMEM((2, 16, KV), BF16),
        pltpu.VMEM((2, 16, KV), BF16),
        *[pltpu.VMEM((4, 4, 32, D), BF16) for _ in range(4)],
        pltpu.VMEM((3, 4, 32, D), BF16),
        pltpu.VMEM((3, 32, D), BF16),
        pltpu.VMEM((3, 32, D), BF16),
        pltpu.VMEM((3, 4, 32, D), BF16),
        pltpu.VMEM((4, 32, D), BF16),
        pltpu.VMEM((4, 32, D), BF16),
        pltpu.VMEM((32, KV), BF16),
        pltpu.VMEM((32, KV), BF16),
        pltpu.VMEM((2, 16, KV), BF16),
        pltpu.VMEM((ROWS, D), BF16),
        pltpu.VMEM((ROWS, D), BF16),
        pltpu.VMEM((48, KV), BF16),
        pltpu.VMEM((128, D), F32),
        pltpu.VMEM((ROWS, KV), BF16),
        pltpu.VMEM((6, 2, FF), F32),
        pltpu.VMEM((6, 4, D), F32),
        pltpu.VMEM((8, 128), F32),
        pltpu.SemaphoreType.DMA((7,)),
    ]
    return pl.pallas_call(
        block_kernel,
        in_specs=[hbm, hbm, hbm, hbm, vmem, hbm, hbm, hbm],
        out_specs=[hbm] * 7,
        out_shape=[
            *[shape(half_one.shape, BF16) for _ in range(4)],
            shape((6, 2, FF), F32), shape((6, 4, D), F32), shape((8, 128), F32),
        ],
        scratch_shapes=scratch,
        compiler_params=pltpu.CompilerParams(
            collective_id=0, has_side_effects=True, vmem_limit_bytes=63 * MIB
        ),
        name="reversible_block",
    )(half_one, half_two, grad_one, grad_two, norm_gain, attn_weight, mlp_weight, pool_kernel)


def hand_out_kernel(*refs):
    taken, rest_ref, given, kernel_out, gain_out = refs[0:6], refs[6], refs[7:13], *refs[13:15]
    held, in_sem, out_sem = refs[15:21], *refs[21:]
    loads = [
        pltpu.make_async_copy(source, target, in_sem.at[k])
        for k, (source, target) in enumerate(zip(taken, held))
    ]
    copies = [
        pltpu.make_async_copy(source, target, out_sem.at[k])
        for k, (source, target) in enumerate(zip(held, given))
    ]
    for load in loads:
        load.start()
    for load, copy in zip(loads, copies):
        load.wait()
        copy.start()
    rest = rest_ref[...]

    def columns(width, step, side):
        row, lane = iota((8, width), 0), iota((8, width), 1)
        pick = jnp.where((row < 6) & (lane == step * row + side), 1.0, 0.0)
        return lax.dot_general(
            rest, pick, (((0,), (0,)), ((), ())),
            precision=lax.Precision.HIGHEST, preferred_element_type=F32,
        )

    kernel_grad = columns(12, 2, 0)[0:48] + columns(12, 2, 1)[48:96]
    for offset in range(3):
        for i in range(4):
            at = 16 * offset + 4 * i
            kernel_out[offset, i] = kernel_grad[at : at + 4]
    gain_out[...] = columns(6, 1, 0)[96:98]
    for copy in copies:
        copy.wait()


def hand_out(results, rest):
    vmem = pl.BlockSpec(memory_space=pltpu.VMEM)
    hbm = pl.BlockSpec(memory_space=pl.ANY)
    shape = jax.ShapeDtypeStruct
    return pl.pallas_call(
        hand_out_kernel,
        in_specs=[hbm] * 6 + [vmem],
        out_specs=[hbm] * 6 + [vmem] * 2,
        out_shape=[shape(array.shape, array.dtype) for array in results]
        + [shape((3, 4, 4, 12), F32), shape((2, 6), F32)],
        scratch_shapes=[pltpu.VMEM(array.shape, array.dtype) for array in results]
        + [pltpu.SemaphoreType.DMA((6,)), pltpu.SemaphoreType.DMA((6,))],
        compiler_params=pltpu.CompilerParams(vmem_limit_bytes=62 * MIB),
        name="hand_out",
    )(*results, rest)


def shards(half_one, half_two, grad_one, grad_two, norm_gain, attn_weight, mlp_weight, pool_kernel):
    *results, rest = run_block(
        half_one, half_two, grad_one, grad_two, norm_gain, attn_weight, mlp_weight, pool_kernel
    )
    (input_one, input_two, total, input_grad_two, mlp_sums, attn_sums, kernel_grad, gain_grad) = (
        hand_out(results, rest)
    )
    mlp_grad = mlp_sums.transpose(1, 2, 0)
    attn_grad = attn_sums.transpose(1, 2, 0)
    return (input_one, input_two, total, input_grad_two, attn_grad, mlp_grad, kernel_grad, gain_grad)


def solution(mesh):
    placed = (
        P("clip", "tm", None, None, None),
        P("clip", "tm", None, None, None),
        P("clip", "tm", None, None, None),
        P("clip", "tm", None, None, None),
        P(),
        P(),
        P(),
        P(),
    )
    return jax.shard_map(
        shards,
        mesh=mesh,
        in_specs=placed,
        out_specs=(
            P("clip", "tm", None, None, None),
            P("clip", "tm", None, None, None),
            P("clip", "tm", None, None, None),
            P("clip", "tm", None, None, None),
            P(None, None, ("clip", "tm")),
            P(None, None, ("clip", "tm")),
            P(None, None, None, ("clip", "tm")),
            P(None, ("clip", "tm")),
        ),
        check_vma=False,
    )
```

```python
from functools import partial

import jax
import jax.numpy as jnp
from jax import lax
from jax.experimental import pallas as pl
from jax.experimental.pallas import tpu as pltpu
from jax.sharding import PartitionSpec as P

D = 768
FF = 3072
KV = 2 * D
ROWS = 224
CHUNK = 512
STEPS = FF // CHUNK
HALF = 384
MIB = 1024 * 1024
F32 = jnp.float32
BF16 = jnp.bfloat16
MESH = pl.DeviceIdType.MESH


def dot(a, b):
    return lax.dot_general(a, b, (((1,), (0,)), ((), ())), preferred_element_type=F32)


def dot_nt(a, b):
    return lax.dot_general(a, b, (((1,), (1,)), ((), ())), preferred_element_type=F32)


def dot_tn(a, b):
    return lax.dot_general(a, b, (((0,), (0,)), ((), ())), preferred_element_type=F32)


def iota(shape, dim):
    return lax.broadcasted_iota(jnp.int32, shape, dim)


def source_column(rows, axes):
    owner_at = (rows * 43691) >> 18
    inner = rows - owner_at * 6
    core = owner_at >> 6
    digits = ((owner_at >> 4) & 3, (owner_at >> 2) & 3, owner_at & 3)
    x, y, z = (digits[axes.index(axis)] for axis in range(3))
    owner = (y >> 1) * 64 + core * 32 + x * 8 + z * 2 + (y & 1)
    return owner * 6 + inner


def permutation(axes):
    source = source_column(iota((D, 128), 0), axes)
    lanes = iota((D, 128), 1)
    pieces = [
        jnp.where(source == lanes + 128 * k, 1.0, 0.0).astype(BF16) for k in range(D // 128)
    ]
    return jnp.concatenate(pieces, axis=1)


def norm_stats(values):
    centre = jnp.mean(values, axis=-1, keepdims=True)
    centred = values - centre
    spread = jnp.mean(centred * centred, axis=-1, keepdims=True)
    scale = lax.rsqrt(spread + 1e-05)
    return centred * scale, scale


def norm_back(unit, scale, gain, cotangent):
    d_unit = cotangent * gain
    first = jnp.mean(d_unit, axis=-1, keepdims=True)
    second = jnp.mean(d_unit * unit, axis=-1, keepdims=True)
    return scale * (d_unit - first - unit * second)


def load_padded(ref, pad):
    pad[...] = jnp.zeros(pad.shape, pad.dtype)
    pad[:, 0:14, :] = ref[0, 0]
    return pad[...].reshape(ROWS, D)


def store_grid(ref, values):
    ref[0, 0] = values.reshape(14, 16, D)[:, 0:14, :]


def spread_kernel(flat):
    row, lane = iota((64, 48), 0), iota((64, 48), 1)
    cell = (row >> 4) * 4 + (((row & 15) + 1) & 3)
    cells = jnp.where(((row & 15) < 14) & ((lane & 15) == cell), 1.0, 0.0).astype(BF16)
    high = flat.astype(BF16)
    rest = flat - high.astype(F32)
    middle = rest.astype(BF16)
    low = (rest - middle.astype(F32)).astype(BF16)
    table = dot(cells, jnp.concatenate([high, middle, low], axis=0))
    return [table[16 * i : 16 * i + 16] for i in range(4)]


def spread_blocks(frame):
    row, lane = iota((64, 16), 0), iota((64, 16), 1)
    block = (row >> 4) * 4 + (((row & 15) + 1) >> 2)
    blocks = jnp.where(((row & 15) < 14) & (lane == block), 1.0, 0.0).astype(BF16)
    table = dot(blocks, frame)
    return [table[16 * a : 16 * a + 16] for a in range(4)]


def sum_columns(tables, group):
    row, lane = iota((48, 192), 0), iota((48, 192), 1)
    across = lane & 15
    same = (row >> 2 == lane >> 4) & (across < 14) & (group(across + 1) == (row & 3))
    pick = jnp.where(same, 1.0, 0.0).astype(BF16)
    stacked = jnp.concatenate([table.astype(BF16) for table in tables], axis=0)
    return dot(pick, stacked)


def add_to(tables, at, value):
    tables[at] = value if tables[at] is None else tables[at] + value


class Links:
    def __init__(self, send, recv):
        self.send, self.recv, self.used, self.started = send, recv, 0, []

    def start(self, source, target, device, shift=0, slots=1):
        copy = pltpu.make_async_remote_copy(
            src_ref=source, dst_ref=target,
            send_sem=self.send.at[self.used], recv_sem=self.recv.at[self.used + shift],
            device_id=device, device_id_type=MESH,
        )
        self.used += slots
        copy.start()
        self.started.append(copy)
        return copy

    def arrival(self, target, number):
        pltpu.make_async_remote_copy(
            src_ref=target, dst_ref=target,
            send_sem=self.send.at[number], recv_sem=self.recv.at[number],
            device_id=(lax.axis_index("clip"), lax.axis_index("tm")), device_id_type=MESH,
        ).wait_recv()

    def sent(self, copy):
        copy.wait_send()
        self.started = [other for other in self.started if other is not copy]


class Place:
    def __init__(self):
        clip, tm = lax.axis_index("clip"), lax.axis_index("tm")
        self.tm, self.clip = tm, clip
        self.core, high = clip % 2, clip // 2
        self.low = tm % 2
        self.at = (tm // 8, high * 2 + self.low, (tm // 2) % 4)

    def device(self, core, at):
        x, y, z = at
        return ((y // 2) * 2 + core, x * 8 + z * 2 + y % 2)

    def other_core(self):
        return self.device(1 - self.core, self.at)

    def along(self, axis, hop):
        at = list(self.at)
        at[axis] = (at[axis] + hop) % 4
        return self.device(self.core, at), at[axis]

    def pair(self, hop, low):
        return (self.clip, (self.tm - self.low + 2 * hop + 32) % 32 + low)


class Reduction:
    def __init__(self, links, place, parts, orders, held, base, offset, landed, store):
        self.links, self.place, self.parts = links, place, parts
        self.axes = [ORDERS[order] for order in orders]
        self.held, self.base, self.offset = held, base, offset
        self.in0, self.in1, self.sum1, self.in2, self.sum2, self.in3 = landed
        self.store = store
        self.copies = {}

    def columns(self, part, offset=0):
        return pl.ds(self.parts[part][0] + offset, self.parts[part][1])

    def blocks(self, part, width=512):
        first, count = self.parts[part]
        if count % width:
            width = count
        return [(first + k * width, width) for k in range(count // width)]

    def send0(self, part):
        cols = self.columns(part)
        rows = pl.ds(pl.multiple_of((1 - self.place.core) * HALF, HALF), HALF)
        self.copies[0, part] = [
            self.links.start(
                self.held.at[rows, self.columns(part, self.offset)], self.in0.at[:, cols],
                self.place.other_core(),
            )
        ]

    def arrive(self, stage, part):
        for copy in self.copies[stage, part]:
            copy.wait_recv()

    def spread(self, stage, part, source, base, offset, rows, target):
        axis = self.axes[part][stage - 1]
        cols = self.columns(part)
        source_cols = self.columns(part, offset)
        self.copies[stage, part] = []
        for hop in (2, 1, 3):
            device, at = self.place.along(axis, hop)
            window = pl.ds(pl.multiple_of(base + at * rows, rows), rows)
            self.copies[stage, part].append(
                self.links.start(
                    source.at[window, source_cols], target.at[hop - 1, :, cols], device
                )
            )

    def send1(self, part):
        self.arrive(0, part)
        first, count = self.parts[part]

        def body(k, carry):
            rows = pl.ds(pl.multiple_of(k * 48, 48), 48)
            mine = pl.ds(pl.multiple_of(self.base + k * 48, 48), 48)
            cols, held_cols = pl.ds(first, count), pl.ds(first + self.offset, count)
            total = self.held[mine, held_cols].astype(F32) + self.in0[rows, cols].astype(F32)
            self.held[mine, held_cols] = total.astype(BF16)
            return carry

        lax.fori_loop(0, HALF // 48, body, 0)
        self.spread(1, part, self.held, self.base, self.offset, 96, self.in1)

    def send2(self, part):
        self.arrive(1, part)
        mine = self.place.at[self.axes[part][0]]
        rows = pl.ds(pl.multiple_of(self.base + mine * 96, 96), 96)
        place_row, place_col = iota((128, 96), 0), iota((128, 96), 1)
        owner = place_row >> 3
        inner = place_row & 7
        widen = jnp.where((inner < 6) & (place_col == owner * 6 + inner), 1.0, 0.0).astype(BF16)
        for first, count in self.blocks(part):
            cols = pl.ds(first, count)
            total = self.held[rows, pl.ds(first + self.offset, count)].astype(F32)
            for slot in range(3):
                total = total + self.in1[slot, :, cols].astype(F32)
            self.sum1[:, cols] = dot(widen, total.astype(BF16)).astype(BF16)
        self.spread(2, part, self.sum1, 0, 0, 32, self.in2)

    def send3(self, part):
        self.arrive(2, part)
        mine = self.place.at[self.axes[part][1]]
        rows = pl.ds(pl.multiple_of(mine * 32, 32), 32)
        for first, count in self.blocks(part):
            cols = pl.ds(first, count)
            total = self.sum1[rows, cols].astype(F32)
            for slot in range(3):
                total = total + self.in2[slot, :, cols].astype(F32)
            self.sum2[:, cols] = total
        self.spread(3, part, self.sum2, 0, 0, 8, self.in3)

    def finish(self, part):
        self.arrive(3, part)
        mine = self.place.at[self.axes[part][2]]
        rows = pl.ds(pl.multiple_of(mine * 8, 8), 8)
        for first, count in self.blocks(part):
            cols = pl.ds(first, count)
            total = self.sum2[rows, cols]
            for slot in range(3):
                total = total + self.in3[slot, :, cols]
            self.store(part, (first - self.parts[part][0]) // 512, total)


ORDERS = ((0, 1, 2), (1, 2, 0), (2, 0, 1), (1, 0, 2))
MLP_ORDERS = (1, 1, 3, 3, 0, 2)
MLP_PARTS = tuple((k * 1024, 1024) for k in range(STEPS))
FIRST_PARTS = tuple((p * 512, 512) for p in range(3))
LAST_PARTS = ((0, 512), (512, 512), (1024, 640))
MLP_COLS, FIRST_COLS, LAST_COLS = 6144, 1536, 1664
N_COPIES = 6 * 10 + 2 * 30 + 3 + 12 + 24 + 3


def landing(cols):
    return [
        pltpu.VMEM((HALF, cols), BF16),
        pltpu.VMEM((3, 96, cols), BF16),
        pltpu.VMEM((128, cols), BF16),
        pltpu.VMEM((3, 32, cols), BF16),
        pltpu.VMEM((32, cols), F32),
        pltpu.VMEM((3, 8, cols), F32),
    ]


def block_kernel(
    one_hbm, two_hbm, cot_one_hbm, cot_two_hbm, gain_ref, attn_hbm, mlp_hbm, pool_hbm,
    one_out, two_out, total_out, grad_two_out, mlp_out, attn_out, rest_out,
    *scratch,
):
    scratch = list(scratch)

    def take(count):
        taken = scratch[:count]
        del scratch[:count]
        return taken

    send_sem, recv_sem, local_sem, weight_sem = take(4)
    one_in, two_in, cot_one_in, cot_two_in, pool_in = take(5)
    up_buf, down_buf, stage = take(3)
    mlp_own, mlp_land = take(1)[0], take(6)
    first_land, last_land = take(6), take(6)
    attn, orders, pool, pad = take(4)
    normed, cot, branch = take(3)
    normed_two, query, keyval, d_att, total, lefts = take(6)
    parts, from_pair, from_edge = take(3)
    keys, values, d_keys, d_values = take(4)
    x_keys, z_keys, x_values, z_values = take(4)
    key_sum, value_sum, pair_sum, pair_land, edge_land = take(5)
    attended, d_query, extra, extra_gain, d_proj = take(5)
    mlp_sums, attn_sums, rest_sums, out_sem = take(4)

    place = Place()
    links = Links(send_sem, recv_sem)
    x, y, z = place.at
    low = place.low

    sources = (one_hbm, cot_two_hbm, two_hbm, cot_one_hbm, pool_hbm, attn_hbm)
    targets = (one_in, cot_two_in, two_in, cot_one_in, pool_in, attn)
    fetches = [
        pltpu.make_async_copy(source, target, local_sem.at[k])
        for k, (source, target) in enumerate(zip(sources, targets))
    ]
    one_copy, cot_two_copy, two_copy, cot_one_copy, pool_copy, attn_copy = fetches

    def weight_copies(k):
        rows = pl.ds(k % STEPS * CHUNK, CHUNK)
        return [
            pltpu.make_async_copy(mlp_hbm.at[0, rows], up_buf.at[k % 3], weight_sem.at[0, k % 3]),
            pltpu.make_async_copy(mlp_hbm.at[1, rows], down_buf.at[k % 3], weight_sem.at[1, k % 3]),
        ]

    one_copy.start()
    for k in range(3):
        for copy in weight_copies(k):
            copy.start()

    barrier = pltpu.get_barrier_semaphore()
    partners = [place.other_core()]
    partners += [place.pair(hop, side) for hop in (-1, 1) for side in range(2)]
    partners += [place.along(axis, hop)[0] for axis in range(3) for hop in (1, 2, 3)]
    for device in partners:
        pl.semaphore_signal(barrier, inc=1, device_id=device, device_id_type=MESH)

    writes = []

    def write(source, target):
        copy = pltpu.make_async_copy(source, target, out_sem.at[len(writes)])
        copy.start()
        writes.append(copy)

    def store_mlp(part, block, values):
        mlp_sums[:, block, pl.ds(part * CHUNK, CHUNK)] = values[0:6]

    def store_first(part, block, values):
        at = pl.ds(part * 256, 256)
        attn_sums[:, 0, at] = values[0:6, 0:256]
        attn_sums[:, 3, at] = values[0:6, 256:512]

    def store_last(part, block, values):
        at = pl.ds(part * 256, 256)
        attn_sums[:, 1, at] = values[0:6, 0:256]
        attn_sums[:, 2, at] = values[0:6, 256:512]
        if part == 2:
            rest_sums[...] = values[:, 512:640]

    own_base = pl.multiple_of(place.core * HALF, HALF)
    other_base = pl.multiple_of((1 - place.core) * HALF, HALF)
    mlp = Reduction(links, place, MLP_PARTS, MLP_ORDERS, mlp_own, 0, 0, mlp_land, store_mlp)
    first = Reduction(links, place, FIRST_PARTS, (0, 1, 2), stage, own_base, 0, first_land, store_first)
    last = Reduction(links, place, LAST_PARTS, (0, 1, 2), stage, own_base, FIRST_COLS, last_land, store_last)

    def kept(chunk):
        at = chunk * 2 * CHUNK
        rows = pl.ds(0, ROWS)
        return mlp_own.at[rows, pl.ds(at, CHUNK)], mlp_own.at[rows, pl.ds(at + CHUNK, CHUNK)]

    def next_weights(k):
        if k + 3 < 2 * STEPS:
            for copy in weight_copies(k + 3):
                copy.start()

    orders[1] = permutation(ORDERS[1])
    one_copy.wait()
    unit, scale = norm_stats(load_padded(one_in, pad).astype(F32))
    normed[...] = (unit * gain_ref[0:1, :]).astype(BF16)
    for k in range(STEPS):
        for copy in weight_copies(k):
            copy.wait()
        hidden = dot_nt(normed[...], up_buf[k % 3])
        inner = 0.7978845608028654 * (hidden + 0.044715 * hidden * hidden * hidden)
        tanh = jnp.tanh(inner)
        half_sum = 0.5 * (1.0 + tanh)
        active = (hidden * half_sum).astype(BF16)
        slope = half_sum + 0.5 * hidden * (1.0 - tanh * tanh) * (
            0.7978845608028654 * (1.0 + 3.0 * 0.044715 * hidden * hidden)
        )
        active_at, slope_at = kept(k)
        active_at[...] = active
        slope_at[...] = slope.astype(BF16)
        if k == 0:
            branch[...] = dot(active, down_buf[k % 3])
        else:
            branch[...] += dot(active, down_buf[k % 3])
        next_weights(k)
        if k == 2:
            two_copy.start()
            pool_copy.start()
            attn_copy.start()
            cot_two_copy.start()
            cot_one_copy.start()

    def back(chunk):
        k = STEPS + chunk
        for copy in weight_copies(k):
            copy.wait()
        up, down = up_buf[k % 3], down_buf[k % 3]
        active_at, slope_at = kept(chunk)
        active = active_at[...]
        d_hidden = (slope_at[...].astype(F32) * dot_nt(cot[...], down)).astype(BF16)
        if chunk == 0:
            branch[...] = dot(d_hidden, up)
        else:
            branch[...] += dot(d_hidden, up)
        next_weights(k)
        order = MLP_ORDERS[chunk]
        if chunk == 0 or MLP_ORDERS[chunk - 1] != order:
            lefts[0] = dot_nt(orders[order], normed[...]).astype(BF16)
            lefts[1] = dot_nt(orders[order], cot[...]).astype(BF16)
        row = chunk % 2 * HALF
        col = chunk // 2 * 2 * CHUNK
        first_col = chunk * 2 * CHUNK
        for side, values_in in enumerate((d_hidden, active)):
            stage[pl.ds(row, HALF), pl.ds(col + side * CHUNK, CHUNK)] = dot(
                lefts[side, pl.ds(other_base, HALF)], values_in
            ).astype(BF16)
        mlp.copies[0, chunk] = [
            links.start(
                stage.at[pl.ds(row, HALF), pl.ds(col, 2 * CHUNK)],
                mlp.in0.at[:, pl.ds(first_col, 2 * CHUNK)],
                place.other_core(),
            )
        ]
        for side, values_in in enumerate((d_hidden, active)):
            mlp_own[:, pl.ds(first_col + side * CHUNK, CHUNK)] = dot(
                lefts[side, pl.ds(own_base, HALF)], values_in
            ).astype(BF16)

    two_copy.wait()
    restored = (load_padded(two_in, pad).astype(F32) - branch[...]).astype(BF16)
    store_grid(two_in, restored)
    write(two_in, two_out)
    unit_two, scale_two = norm_stats(restored.astype(F32))
    normed_two[...] = (unit_two * gain_ref[1:2, :]).astype(BF16)
    attn_copy.wait()
    keyval[:, 0:D] = dot(normed_two[...], attn[1]).astype(BF16)
    keyval[:, D:] = dot(normed_two[...], attn[2]).astype(BF16)
    pool_copy.wait()
    sums = [None] * 12
    for offset in range(3):
        for i in range(4):
            pool[offset, 4 * i : 4 * i + 4, :] = pool_in[offset, i]
        table = spread_kernel(pool[offset])
        for y_at in range(14):
            row = keyval[16 * y_at : 16 * y_at + 16, :].astype(F32)
            at = (2 - offset) * 4 + (y_at + 1) // 4
            add_to(sums, at, table[(y_at + 1) % 4] * row)
    pooled_parts = sum_columns(sums, lambda across: across >> 2).astype(BF16)
    for k in range(3):
        parts[k] = pooled_parts[16 * k : 16 * k + 16]

    mine = pl.ds(1 - low, 2)
    pl.semaphore_wait(barrier, len(partners))
    pair_copy = links.start(parts.at[mine], from_pair, place.pair(0, 1 - low))
    edge_base = links.used
    for side in range(2):
        links.start(
            parts.at[2 * low], from_edge.at[1 - low],
            (place.clip, (place.tm - low + 4 * low - 2 + 32) % 32 + side),
            shift=1 - low if side == 0 else -low, slots=1,
        )
    query[...] = dot(normed_two[...], attn[0]).astype(BF16)
    cot_two_copy.wait()
    cot[...] = load_padded(cot_two_in, pad)
    back(0)
    orders[3] = permutation(ORDERS[3])
    orders[0] = permutation(ORDERS[0])
    pair_copy.wait_recv()
    for slot in range(2):
        links.arrival(from_edge.at[slot], edge_base + slot)
    ends = (place.tm // 2 > 0, place.tm // 2 < 15)
    for slot in range(2):
        edge = jnp.where(ends[slot], from_edge[slot].astype(F32), 0.0)
        frame = parts[1 - low + slot].astype(F32) + from_pair[slot].astype(F32) + edge
        frame = frame.astype(BF16)
        keys[x, z, 16 * slot : 16 * slot + 16, :] = frame[:, 0:D]
        values[x, z, 16 * slot : 16 * slot + 16, :] = frame[:, D:]

    copies = []
    for hop in (2, 1, 3):
        copies.append(links.start(keys.at[x, z], keys.at[x, z], place.along(2, hop)[0]))
        copies.append(links.start(values.at[x, z], values.at[x, z], place.along(0, hop)[0]))
    back(1)
    orders[2] = permutation(ORDERS[2])
    for copy in copies:
        copy.wait_recv()
    copies = []
    for hop in (2, 1, 3):
        copies.append(links.start(keys.at[x], keys.at[x], place.along(0, hop)[0]))
        copies.append(links.start(values.at[:, z], values.at[:, z], place.along(2, hop)[0]))
    for chunk in range(2, STEPS):
        mlp.send1(chunk - 2)
        back(chunk)
    unit, scale = norm_stats(load_padded(one_in, pad).astype(F32))
    d_gain_one = jnp.sum(branch[...] * unit, axis=0, keepdims=True)
    d_first = norm_back(unit, scale, gain_ref[0:1, :], branch[...])
    cot_one_copy.wait()
    total[...] = (load_padded(cot_one_in, pad).astype(F32) + d_first).astype(BF16)
    store_grid(cot_one_in, total[...])
    write(cot_one_in, total_out)
    d_att[...] = dot_nt(total[...], attn[3]).astype(BF16)
    for part in range(3):
        lefts[part] = dot_nt(orders[part], total[...]).astype(BF16)
    for copy in copies:
        copy.wait_recv()
    mlp.send1(4)
    mlp.send1(5)

    def heads(pair):
        lanes = pl.ds(pair * 128, 128)
        query_pair = query[:, lanes] * jnp.asarray(0.125, BF16)
        d_att_pair = d_att[:, lanes]
        key = keys[:, :, :, lanes].reshape(512, 128)
        value = values[:, :, :, lanes].reshape(512, 128)
        queries, d_atts, keys_h, values_h, probs_h, d_scores_h = [], [], [], [], [], []
        for side in range(2):

            def only(array):
                lane = iota(array.shape, 1)
                keep = lane < 64 if side == 0 else lane >= 64
                return jnp.where(keep, array, jnp.zeros_like(array))

            queries.append(only(query_pair))
            d_atts.append(only(d_att_pair))
            keys_h.append(only(key))
            values_h.append(only(value))
            weights = jnp.exp(dot_nt(queries[side], key))
            probs = weights * (1.0 / jnp.sum(weights, axis=-1, keepdims=True))
            product = probs * dot_nt(d_atts[side], value)
            d_scores = product - probs * jnp.sum(product, axis=-1, keepdims=True)
            probs_h.append(probs.astype(BF16))
            d_scores_h.append(d_scores.astype(BF16))

        def joined(pieces, axis):
            return jnp.concatenate(pieces, axis=axis)

        att = dot(joined(probs_h, 1), joined(values_h, 0))
        d_q = dot(joined(d_scores_h, 1), joined(keys_h, 0)) * 0.125
        d_k = dot_tn(joined(d_scores_h, 0), joined(queries, 0))
        d_v = dot_tn(joined(probs_h, 0), joined(d_atts, 0))
        attended[:, lanes] = att.astype(BF16)
        d_query[:, lanes] = d_q.astype(BF16)
        d_keys[:, :, :, lanes] = d_k.astype(BF16).reshape(4, 4, 32, 128)
        d_values[:, :, :, lanes] = d_v.astype(BF16).reshape(4, 4, 32, 128)

    copies = []
    for group in range(3):
        for pair in range(2 * group, 2 * group + 2):
            heads(pair)
        lanes = pl.ds(group * 256, 256)
        for hop in (2, 1, 3):
            device, at = place.along(0, hop)
            copies.append(
                links.start(d_keys.at[at, :, :, lanes], x_keys.at[hop - 1, :, :, lanes], device)
            )
            device, at = place.along(2, hop)
            copies.append(
                links.start(d_values.at[:, at, :, lanes], z_values.at[hop - 1, :, :, lanes], device)
            )

    for part in range(STEPS):
        for copy in mlp.copies[0, part]:
            links.sent(copy)
    branch_f = dot(attended[...], attn[3])
    store_grid(one_in, (load_padded(one_in, pad).astype(F32) - branch_f).astype(BF16))
    write(one_in, one_out)
    for part in range(3):
        inside = pl.ds(part * 256, 256)
        lhs = dot_nt(orders[part], d_query[...]).astype(BF16)
        stage[:, pl.ds(part * 512, 256)] = dot(lhs, normed_two[:, inside]).astype(BF16)
        stage[:, pl.ds(part * 512 + 256, 256)] = dot(
            lefts[part], attended[:, inside]
        ).astype(BF16)
        first.send0(part)
    branch[...] = dot_nt(d_query[...], attn[0])

    for copy in copies:
        copy.wait_recv()
    sum_k = d_keys[x].astype(F32)
    sum_v = d_values[:, z].astype(F32)
    for slot in range(3):
        sum_k = sum_k + x_keys[slot].astype(F32)
        sum_v = sum_v + z_values[slot].astype(F32)
    key_sum[...] = sum_k.astype(BF16)
    value_sum[...] = sum_v.astype(BF16)
    copies = []
    for hop in (2, 1, 3):
        device, at = place.along(2, hop)
        copies.append(links.start(key_sum.at[at], z_keys.at[hop - 1], device))
        device, at = place.along(0, hop)
        copies.append(links.start(value_sum.at[at], x_values.at[hop - 1], device))
    for part in (0, 1, 4, 5):
        mlp.send2(part)
    for copy in copies:
        copy.wait_recv()
    sum_k = key_sum[z].astype(F32)
    sum_v = value_sum[x].astype(F32)
    for slot in range(3):
        sum_k = sum_k + z_keys[slot].astype(F32)
        sum_v = sum_v + x_values[slot].astype(F32)
    pair_sum[:, 0:D] = sum_k.astype(BF16)
    pair_sum[:, D:] = sum_v.astype(BF16)

    pair_copy = links.start(pair_sum, pair_land, place.pair(0, 1 - low))
    edge_base = links.used
    for hop, rows in ((-1, pl.ds(0, 16)), (1, pl.ds(16, 16))):
        side = 1 if hop == -1 else 0
        links.start(
            pair_sum.at[rows, :], edge_land.at[low], place.pair(hop, side),
            shift=low if hop == -1 else low - 1, slots=1,
        )
    for part in range(3):
        first.send1(part)
    mlp.send2(2)
    mlp.send2(3)
    pair_copy.wait_recv()
    for slot in range(2):
        links.arrival(edge_land.at[slot], edge_base + slot)
    edge = edge_land[0].astype(F32) + edge_land[1].astype(F32)
    inside = (low == 0) & (place.tm > 0) | (low == 1) & (place.tm < 31)
    edge = jnp.where(inside, edge, 0.0).astype(BF16)
    pair_frames = (pair_sum[...].astype(F32) + pair_land[...].astype(F32)).astype(BF16)
    frame_0, frame_1 = pair_frames[0:16, :], pair_frames[16:32, :]
    before = jnp.where(low == 0, edge, frame_0)
    here = jnp.where(low == 0, frame_0, frame_1)
    after = jnp.where(low == 0, frame_1, edge)

    sums = [None] * 12
    d_rows = [None] * 14
    for offset, source in enumerate((after, here, before)):
        table = spread_kernel(pool[offset])
        expanded = spread_blocks(source)
        for y_at in range(14):
            i, block = (y_at + 1) % 4, (y_at + 1) // 4
            row = keyval[16 * y_at : 16 * y_at + 16, :].astype(F32)
            add_to(d_rows, y_at, table[i] * expanded[block])
            add_to(sums, offset * 4 + i, row * expanded[block])
    extra[...] = sum_columns(sums, lambda across: across & 3).astype(BF16)
    for y_at in range(14):
        d_proj[16 * y_at : 16 * y_at + 16, :] = d_rows[y_at].astype(BF16)
    d_keyval = d_proj[...]
    d_key_proj, d_value_proj = d_keyval[:, 0:D], d_keyval[:, D:]

    def last_part(part):
        inside = pl.ds(part * 256, 256)
        start = FIRST_COLS + part * 512
        lhs = dot_nt(orders[part], d_key_proj).astype(BF16)
        stage[:, pl.ds(start, 256)] = dot(lhs, normed_two[:, inside]).astype(BF16)
        lhs = dot_nt(orders[part], d_value_proj).astype(BF16)
        stage[:, pl.ds(start + 256, 256)] = dot(lhs, normed_two[:, inside]).astype(BF16)

    for part in range(2):
        last_part(part)
        last.send0(part)
    last_part(2)
    last.send1(0)
    d_normed_two = branch[...] + dot_nt(d_key_proj, attn[1]) + dot_nt(d_value_proj, attn[2])
    row, lane = iota((256, 256), 0), iota((256, 256), 1)
    parted = jnp.where(row == 2 * (lane & 127) + (lane >> 7), 1.0, 0.0).astype(BF16)
    extra_gain[...] = jnp.zeros(extra_gain.shape, F32)
    for k in range(6):
        lanes = pl.ds(k * 128, 128)
        sides = dot(extra[:, pl.ds(k * 256, 256)], parted)
        extra_gain[0:48, lanes] = sides[:, 0:128]
        extra_gain[48:96, lanes] = sides[:, 128:256]
    extra_gain[96:97, :] = d_gain_one
    extra_gain[97:98, :] = jnp.sum(d_normed_two * unit_two, axis=0, keepdims=True)
    block = dot_nt(orders[2], extra_gain[...].astype(BF16))
    stage[:, pl.ds(FIRST_COLS + 1536, 128)] = block.astype(BF16)
    last.send0(2)
    last.send1(1)
    d_second = norm_back(unit_two, scale_two, gain_ref[1:2, :], d_normed_two)
    result = load_padded(cot_two_in, pad).astype(F32) + d_second
    store_grid(cot_two_in, result.astype(BF16))
    write(cot_two_in, grad_two_out)
    last.send1(2)

    for part in range(3):
        first.send2(part)
    for part in (0, 1, 4, 5):
        mlp.send3(part)
    for part in range(3):
        last.send2(part)
    for part in range(3):
        first.send3(part)
    mlp.send3(2)
    mlp.send3(3)
    for part in (0, 1, 4, 5):
        mlp.finish(part)
    for part in range(3):
        last.send3(part)
    for part in range(3):
        first.finish(part)
    mlp.finish(2)
    mlp.finish(3)
    write(mlp_sums, mlp_out)
    for part in range(3):
        last.finish(part)
    write(attn_sums, attn_out)
    write(rest_sums, rest_out)
    for copy in links.started:
        copy.wait_send()
    for copy in writes:
        copy.wait()


def run_block(half_one, half_two, grad_one, grad_two, norm_gain, attn_weight, mlp_weight, pool_kernel):
    vmem = pl.BlockSpec(memory_space=pltpu.VMEM)
    hbm = pl.BlockSpec(memory_space=pl.ANY)
    shape = jax.ShapeDtypeStruct
    scratch = [
        pltpu.SemaphoreType.DMA((N_COPIES,)),
        pltpu.SemaphoreType.DMA((N_COPIES,)),
        pltpu.SemaphoreType.DMA((6,)),
        pltpu.SemaphoreType.DMA((2, 3)),
        *[pltpu.VMEM((1, 1, 14, 14, D), BF16) for _ in range(4)],
        pltpu.VMEM((3, 4, 4, KV), F32),
        pltpu.VMEM((3, CHUNK, D), BF16),
        pltpu.VMEM((3, CHUNK, D), BF16),
        pltpu.VMEM((D, FIRST_COLS + LAST_COLS), BF16),
        pltpu.VMEM((HALF, MLP_COLS), BF16), *landing(MLP_COLS),
        *landing(FIRST_COLS),
        *landing(LAST_COLS),
        pltpu.VMEM((4, D, D), BF16),
        pltpu.VMEM((4, D, D), BF16),
        pltpu.VMEM((3, 16, KV), F32),
        pltpu.VMEM((14, 16, D), BF16),
        pltpu.VMEM((ROWS, D), BF16),
        pltpu.VMEM((ROWS, D), BF16),
        pltpu.VMEM((ROWS, D), F32),
        pltpu.VMEM((ROWS, D), BF16),
        pltpu.VMEM((ROWS, D), BF16),
        pltpu.VMEM((ROWS, KV), BF16),
        pltpu.VMEM((ROWS, D), BF16),
        pltpu.VMEM((ROWS, D), BF16),
        pltpu.VMEM((3, D, ROWS), BF16),
        pltpu.VMEM((3, 16, KV), BF16),
        pltpu.VMEM((2, 16, KV), BF16),
        pltpu.VMEM((2, 16, KV), BF16),
        *[pltpu.VMEM((4, 4, 32, D), BF16) for _ in range(4)],
        pltpu.VMEM((3, 4, 32, D), BF16),
        pltpu.VMEM((3, 32, D), BF16),
        pltpu.VMEM((3, 32, D), BF16),
        pltpu.VMEM((3, 4, 32, D), BF16),
        pltpu.VMEM((4, 32, D), BF16),
        pltpu.VMEM((4, 32, D), BF16),
        pltpu.VMEM((32, KV), BF16),
        pltpu.VMEM((32, KV), BF16),
        pltpu.VMEM((2, 16, KV), BF16),
        pltpu.VMEM((ROWS, D), BF16),
        pltpu.VMEM((ROWS, D), BF16),
        pltpu.VMEM((48, KV), BF16),
        pltpu.VMEM((128, D), F32),
        pltpu.VMEM((ROWS, KV), BF16),
        pltpu.VMEM((6, 2, FF), F32),
        pltpu.VMEM((6, 4, D), F32),
        pltpu.VMEM((8, 128), F32),
        pltpu.SemaphoreType.DMA((7,)),
    ]
    return pl.pallas_call(
        block_kernel,
        in_specs=[hbm, hbm, hbm, hbm, vmem, hbm, hbm, hbm],
        out_specs=[hbm] * 7,
        out_shape=[
            *[shape(half_one.shape, BF16) for _ in range(4)],
            shape((6, 2, FF), F32), shape((6, 4, D), F32), shape((8, 128), F32),
        ],
        scratch_shapes=scratch,
        compiler_params=pltpu.CompilerParams(
            collective_id=0, has_side_effects=True, vmem_limit_bytes=63 * MIB
        ),
        name="reversible_block",
    )(half_one, half_two, grad_one, grad_two, norm_gain, attn_weight, mlp_weight, pool_kernel)


def hand_out_kernel(*refs):
    taken, rest_ref, given, kernel_out, gain_out = refs[0:6], refs[6], refs[7:13], *refs[13:15]
    held, in_sem, out_sem = refs[15:21], *refs[21:]
    loads = [
        pltpu.make_async_copy(source, target, in_sem.at[k])
        for k, (source, target) in enumerate(zip(taken, held))
    ]
    copies = [
        pltpu.make_async_copy(source, target, out_sem.at[k])
        for k, (source, target) in enumerate(zip(held, given))
    ]
    for load in loads:
        load.start()
    for load, copy in zip(loads, copies):
        load.wait()
        copy.start()
    rest = rest_ref[...]

    def columns(width, step, side):
        row, lane = iota((8, width), 0), iota((8, width), 1)
        pick = jnp.where((row < 6) & (lane == step * row + side), 1.0, 0.0)
        return lax.dot_general(
            rest, pick, (((0,), (0,)), ((), ())),
            precision=lax.Precision.HIGHEST, preferred_element_type=F32,
        )

    kernel_grad = columns(12, 2, 0)[0:48] + columns(12, 2, 1)[48:96]
    for offset in range(3):
        for i in range(4):
            at = 16 * offset + 4 * i
            kernel_out[offset, i] = kernel_grad[at : at + 4]
    gain_out[...] = columns(6, 1, 0)[96:98]
    for copy in copies:
        copy.wait()


def hand_out(results, rest):
    vmem = pl.BlockSpec(memory_space=pltpu.VMEM)
    hbm = pl.BlockSpec(memory_space=pl.ANY)
    shape = jax.ShapeDtypeStruct
    return pl.pallas_call(
        hand_out_kernel,
        in_specs=[hbm] * 6 + [vmem],
        out_specs=[hbm] * 6 + [vmem] * 2,
        out_shape=[shape(array.shape, array.dtype) for array in results]
        + [shape((3, 4, 4, 12), F32), shape((2, 6), F32)],
        scratch_shapes=[pltpu.VMEM(array.shape, array.dtype) for array in results]
        + [pltpu.SemaphoreType.DMA((6,)), pltpu.SemaphoreType.DMA((6,))],
        compiler_params=pltpu.CompilerParams(vmem_limit_bytes=62 * MIB),
        name="hand_out",
    )(*results, rest)


def shards(half_one, half_two, grad_one, grad_two, norm_gain, attn_weight, mlp_weight, pool_kernel):
    *results, rest = run_block(
        half_one, half_two, grad_one, grad_two, norm_gain, attn_weight, mlp_weight, pool_kernel
    )
    (input_one, input_two, total, input_grad_two, mlp_sums, attn_sums, kernel_grad, gain_grad) = (
        hand_out(results, rest)
    )
    mlp_grad = mlp_sums.transpose(1, 2, 0)
    attn_grad = attn_sums.transpose(1, 2, 0)
    return (input_one, input_two, total, input_grad_two, attn_grad, mlp_grad, kernel_grad, gain_grad)


def solution(mesh):
    placed = (
        P("clip", "tm", None, None, None),
        P("clip", "tm", None, None, None),
        P("clip", "tm", None, None, None),
        P("clip", "tm", None, None, None),
        P(),
        P(),
        P(),
        P(),
    )
    return jax.shard_map(
        shards,
        mesh=mesh,
        in_specs=placed,
        out_specs=(
            P("clip", "tm", None, None, None),
            P("clip", "tm", None, None, None),
            P("clip", "tm", None, None, None),
            P("clip", "tm", None, None, None),
            P(None, None, ("clip", "tm")),
            P(None, None, ("clip", "tm")),
            P(None, None, None, ("clip", "tm")),
            P(None, ("clip", "tm")),
        ),
        check_vma=False,
    )
```
